32 devices in a mesh: dp: 8 (over y, x, core), fsdp: 4 (over z).
Axes of the slice: x: 2, y: 2, z: 4, core: 2. Of those that a mesh axis runs over, the one named last changes fastest.
Arguments:
- latents: bfloat16 [32, 768, 1024], P(('dp', 'fsdp')), may hold values from -6 to 6
- lengths: int32 [32, 4], P(('dp', 'fsdp')), may hold values from 1 to 512, 768 in all within a row
- cotangent: bfloat16 [32, 768, 1024], P(('dp', 'fsdp')), may hold values from -6 to 6
- matrices: float32 [6, 1024, 1024], P(None, ('dp', 'fsdp')), may hold values from -2 to 2
- norm_params: float32 [4, 1024], P(None, ('dp', 'fsdp')), may hold values from -2 to 2
- moment1_mat: float32 [6, 1024, 1024], P(None, ('dp', 'fsdp')), may hold values from -256 to 256
- moment2_mat: float32 [6, 1024, 1024], P(None, ('dp', 'fsdp')), may hold values from 24.576 to 1228.8
- moment1_norm: float32 [4, 1024], P(None, ('dp', 'fsdp')), may hold values from -256 to 256
- moment2_norm: float32 [4, 1024], P(None, ('dp', 'fsdp')), may hold values from 24.576 to 1228.8
Outputs:
- out_latents: bfloat16 [32, 768, 1024], P(('dp', 'fsdp'))
- grad_latents: bfloat16 [32, 768, 1024], P(('dp', 'fsdp'))
- grad_matrices: float32 [6, 1024, 1024], P(None, ('dp', 'fsdp'))
- grad_norms: float32 [4, 1024], P(None, ('dp', 'fsdp'))
- update_matrices: float32 [6, 1024, 1024], P(None, ('dp', 'fsdp'))
- update_norms: float32 [4, 1024], P(None, ('dp', 'fsdp'))
- new_moment1_mat: float32 [6, 1024, 1024], P(None, ('dp', 'fsdp'))
- new_moment2_mat: float32 [6, 1024, 1024], P(None, ('dp', 'fsdp'))
- new_moment1_norm: float32 [4, 1024], P(None, ('dp', 'fsdp'))
- new_moment2_norm: float32 [4, 1024], P(None, ('dp', 'fsdp'))
- trust_ratios: float32 [10], replicated
The draws below stay inside these ranges and needn't reach their ends.
Inputs may be any that keep to these rules, and one draw needn't show every extreme that they name: The first 3 entries of a row are the lengths of its image latent sets in order; the last is the padding at the row's end. Every row sums to 768 and its largest entry is 512.
All inputs are finite; a program needn't handle non-finite values.
Results may differ from the reference program's by a relative error of at most 0.012.
The reference program's roundings to bfloat16 on the way count: a program that leaves them out, or rounds other values in their place, can miss the bound.
Values may be sent and summed in bfloat16 or wider, within the bound.
No kernel may reach another device: no remote copies, remote signals or barrier semaphores. Data moves between devices by JAX's collectives and lax.ppermute only.
A program may use at most 192 MiB of HBM per device.

```python
import math
import jax
import jax.numpy as jnp
import numpy as np
from jax import lax

D = 1024
HEADS = 8
HEAD_DIM = 128
ROW_LEN = 768
SET_MAX = 512
SETS = 3
BLOCK = 768
ROWS = 32
TOKENS = 24576


def draw_matrices(key, part):
    key = jax.random.fold_in(key, 11)
    key_normal, key_rows = jax.random.split(key)
    entries = jnp.clip(jax.random.normal(key_normal, (6, D, D), jnp.float32), -4.0, 4.0)
    rough_rows = jax.random.uniform(key_rows, (6, D, 1), jnp.float32, 0.7, 1.3)
    rising = 0.5 + jnp.arange(D, dtype=jnp.float32)[None, :, None] / D
    factor = jnp.array([1.0, 1.0, 1.0, 8.0, 1.0, 1.0], jnp.float32)[:, None, None]
    return entries * rough_rows * rising * factor / math.sqrt(D)


def draw_norm_params(key, part):
    key = jax.random.fold_in(key, 23)
    entries = jnp.clip(jax.random.normal(key, (4, D), jnp.float32), -4.0, 4.0)
    is_gain = (jnp.arange(4) % 2 == 0)[:, None]
    return jnp.where(is_gain, 1.0 + 0.12 * entries, 0.3 * entries)


def shard_levels(stream_key, shape, cuts, least, largest):
    factor_of, own = 1.0, jax.random.fold_in(stream_key, 6)
    for dim, parts in cuts:
        steps = jnp.exp(jax.random.uniform(jax.random.fold_in(own, dim), (parts,), jnp.float32, least / len(cuts), largest / len(cuts)))
        factor_of = factor_of * jnp.repeat(steps, shape[dim] // parts).reshape([-1 if axis == dim else 1 for axis in range(len(shape))])
    return factor_of


def length_profile(number_of, total, reach, skew):
    loads = [(1 << 20) // math.isqrt(grade ** skew) + 1 for grade in range(2, number_of + 1)]
    rest, holding = total - reach - (number_of - 1), [1] * (number_of - 1)
    while rest > 0:
        free = [i for i in range(number_of - 1) if holding[i] < reach]
        whole, left = sum([loads[i] for i in free]), rest
        for i in free:
            more = min(reach - holding[i], max(1, left * loads[i] // whole), rest)
            holding[i] = holding[i] + more
            rest = rest - more
    return np.array([reach] + holding)


def uneven_parts(stream_key, number_of, total, bound, lean):
    if number_of == 2:
        one = jax.random.randint(stream_key, (), max(1, total - bound), min(bound, total - 1) + 1)
        return jnp.stack([one, total - one])
    sizes = jnp.asarray(length_profile(number_of, total, bound, lean), jnp.int32)
    couples = (number_of - 1) // 2
    giver, taker = sizes[1:1 + 2 * couples:2], sizes[2:2 + 2 * couples:2]
    slack = jnp.minimum(giver - 1, bound - taker)
    moved = jax.random.randint(jax.random.fold_in(stream_key, 1), (couples,), 0, 1 << 20) % (slack + 1)
    sizes = sizes.at[1:1 + 2 * couples:2].set(giver - moved).at[2:2 + 2 * couples:2].set(taker + moved)
    return sizes[jax.random.permutation(jax.random.fold_in(stream_key, 2), number_of)]


def gaussian(rng, extent, deviation, most, pieces=(), held_as=jnp.bfloat16):
    values = deviation * jax.random.normal(rng, extent, jnp.float32)
    if pieces:
        values = values * shard_levels(rng, extent, pieces, -0.22, 0.18)
    return jnp.clip(values, -most, most).astype(held_as)


def setup_inputs(seed: int = 0) -> dict:
    seeds = jax.random.split(jax.random.key(seed), 10)
    return {
        "latents": gaussian(seeds[0], (ROWS, ROW_LEN, D), 1.0, 6.0, ((0, 32),)),
        "lengths": jax.vmap(lambda own: uneven_parts(own, SETS + 1, ROW_LEN, SET_MAX, 1))(jax.random.split(seeds[1], ROWS)).reshape((ROWS, SETS + 1)).astype(jnp.int32),
        "cotangent": gaussian(seeds[2], (ROWS, ROW_LEN, D), 1.0, 6.0, ((0, 32),)),
        "matrices": draw_matrices(jax.random.fold_in(seeds[9], 71), 0),
        "norm_params": draw_norm_params(jax.random.fold_in(seeds[9], 71), 0),
        "moment1_mat": gaussian(seeds[5], (6, D, D), (0.3 * TOKENS ** 0.5), 256.0, ((1, 32),), jnp.float32),
        "moment2_mat": jnp.clip(jnp.exp(math.log(1228.8) - 3.912023 * jax.random.uniform(seeds[6], (6, D, D), jnp.float32) ** shard_levels(seeds[6], (6, D, D), ((1, 32),), -0.2, 0.2)), 24.576, 1228.8),
        "moment1_norm": gaussian(seeds[7], (4, D), (0.3 * TOKENS ** 0.5), 256.0, ((1, 32),), jnp.float32),
        "moment2_norm": jnp.clip(jnp.exp(math.log(1228.8) - 3.912023 * jax.random.uniform(seeds[8], (4, D), jnp.float32) ** shard_levels(seeds[8], (4, D), ((1, 32),), -0.2, 0.2)), 24.576, 1228.8),
    }


@jax.custom_vjp
def low(v):
    return lax.optimization_barrier(v.astype(jnp.bfloat16)).astype(jnp.float32)

@jax.custom_vjp
def low_back(v):
    return v

def low_keep(v):
    return (low(v), None)

def low_pass(kept, grad):
    return (grad,)

def back_keep(v):
    return (v, None)

def back_low(kept, grad):
    return (low(grad),)
low.defvjp(low_keep, low_pass)
low_back.defvjp(back_keep, back_low)
HIGH = lax.Precision.HIGHEST
ln_eps = 1e-05
beta_one = 0.9
beta_two = 0.999
adam_eps = 1e-06
decay_rate = 0.01
adam_step = 100.0
masked_score = -1000000000.0
gelu_coef = 0.7978845608

def round_both(value):
    return low(low_back(value))

def segment_ids(lengths_row):
    set_ends = jnp.cumsum(lengths_row[:-1]).astype(jnp.int32)
    positions = jnp.arange(ROW_LEN, dtype=jnp.int32)
    return lax.optimization_barrier(jnp.sum((positions[:, None] >= set_ends[None, :]).astype(jnp.int32), axis=1))

def layer_norm(value, gain, shift):
    centered = value - lax.optimization_barrier(jnp.mean(value, -1, keepdims=True))
    normed = centered * lax.rsqrt(lax.optimization_barrier(jnp.mean(centered * centered, -1, keepdims=True)) + ln_eps)
    return normed * gain + shift

def gelu_curve(upward):
    return 0.5 * upward * (1.0 + jnp.tanh(gelu_coef * (upward + 0.044715 * upward * upward * upward)))

def attend(queries, key_heads, values, segment):
    block_count = ROW_LEN // BLOCK
    q_blocks = queries.reshape(block_count, BLOCK, HEADS, HEAD_DIM)
    s_blocks = segment.reshape(block_count, BLOCK)
    score_scale = 1.0 / math.sqrt(HEAD_DIM)

    def one_block(pair):
        q_block, seg_block = pair
        scores = low_back(jnp.einsum('qhd,khd->hqk', q_block, key_heads, precision=HIGH) * score_scale)
        match = seg_block[:, None] == segment[None, :]
        scores = jnp.where(match[None], scores, masked_score)
        row_max = lax.optimization_barrier(jnp.max(scores, -1, keepdims=True))
        exp_scores = jnp.exp(scores - row_max)
        probs = low(exp_scores / lax.optimization_barrier(jnp.sum(exp_scores, -1, keepdims=True)))
        return jnp.einsum('hqk,khd->qhd', probs, values, precision=HIGH)
    blocks = lax.map(jax.checkpoint(one_block), (q_blocks, s_blocks))
    return blocks.reshape(ROW_LEN, HEADS, HEAD_DIM)

def row_forward(inputs, mats, norms, segment):
    live_rows = (segment < SETS).astype(jnp.float32)[:, None]
    h_one = low(layer_norm(inputs, norms[0], norms[1]))
    qkv = round_both(jnp.einsum('td,ide->ite', h_one, mats[:3], precision=HIGH))
    heads_all = qkv.reshape(3, ROW_LEN, HEADS, HEAD_DIM)
    attended = attend(heads_all[0], heads_all[1], heads_all[2], segment)
    attended = round_both(attended.reshape(ROW_LEN, D))
    branch = low_back(jnp.dot(attended, mats[3], precision=HIGH))
    middle = inputs + live_rows * branch
    h_two = low(layer_norm(middle, norms[2], norms[3]))
    upward = low_back(jnp.dot(h_two, mats[4], precision=HIGH))
    activ = low(gelu_curve(upward))
    mlp_out = low_back(jnp.dot(activ, mats[5], precision=HIGH))
    return middle + live_rows * mlp_out

def lamb_parts(weight, grad, first, second, sum_axes):
    m_one = beta_one * first + (1.0 - beta_one) * grad
    m_two = beta_two * second + (1.0 - beta_two) * grad * grad
    step_dir = m_one / (1.0 - beta_one ** adam_step) / (jnp.sqrt(m_two / (1.0 - beta_two ** adam_step)) + adam_eps) + decay_rate * weight
    return (m_one, m_two, step_dir, lax.optimization_barrier(jnp.sum(weight * weight, axis=sum_axes)), lax.optimization_barrier(jnp.sum(step_dir * step_dir, axis=sum_axes)))

def reference(latents, lengths, cotangent, matrices, norm_params, moment1_mat, moment2_mat, moment1_norm, moment2_norm):
    low_mats = low(matrices)
    low_norms = low(norm_params)
    segments = jax.vmap(segment_ids)(lengths)
    group_rows = math.gcd(ROWS, 4)
    group_count = ROWS // group_rows
    x_groups = latents.astype(jnp.float32).reshape(group_count, group_rows, ROW_LEN, D)
    c_groups = cotangent.astype(jnp.float32).reshape(group_count, group_rows, ROW_LEN, D)
    s_groups = segments.reshape(group_count, group_rows, ROW_LEN)

    def one_group(totals, group_item):
        x_rows, c_rows, s_rows = group_item

        def forward(x_in, mats_in, norms_in):
            return jax.vmap(row_forward, in_axes=(0, None, None, 0))(x_in, mats_in, norms_in, s_rows)
        result, pull = jax.vjp(forward, x_rows, low_mats, low_norms)
        grad_x, grad_m, grad_n = pull(c_rows)
        return ((totals[0] + grad_m, totals[1] + grad_n), (result.astype(jnp.bfloat16), grad_x.astype(jnp.bfloat16)))
    start_totals = (jnp.zeros((6, D, D), jnp.float32), jnp.zeros((4, D), jnp.float32))
    (grad_mats, grad_norms), (results, grads_in) = lax.scan(one_group, start_totals, (x_groups, c_groups, s_groups))
    out_latents = results.reshape(ROWS, ROW_LEN, D)
    grad_latents = grads_in.reshape(ROWS, ROW_LEN, D)
    m1_mat, m2_mat, dir_mat, wsq_mat, usq_mat = lamb_parts(matrices, grad_mats, moment1_mat, moment2_mat, (1, 2))
    m1_norm, m2_norm, dir_norm, wsq_norm, usq_norm = lamb_parts(norm_params, grad_norms, moment1_norm, moment2_norm, (1,))
    weight_sq = jnp.concatenate([wsq_mat, wsq_norm])
    update_sq = jnp.concatenate([usq_mat, usq_norm])
    ratios = jnp.sqrt(weight_sq) / jnp.sqrt(update_sq)
    scaled_mats = ratios[:6][:, None, None] * dir_mat
    scaled_norms = ratios[6:][:, None] * dir_norm
    return (out_latents, grad_latents, grad_mats, grad_norms, scaled_mats, scaled_norms, m1_mat, m2_mat, m1_norm, m2_norm, ratios)
```

```python
import math

import jax
import jax.numpy as jnp
from jax import lax
from jax.experimental import pallas as pl
from jax.experimental.pallas import tpu as pltpu
from jax.sharding import PartitionSpec as P

HEADS = 8


ln_eps = 1e-05
beta_one = 0.9
beta_two = 0.999
adam_eps = 1e-06
decay_rate = 0.01
adam_step = 100.0
masked_score = -1000000000.0
gelu_coef = 0.7978845608


def segment_ids(lengths_row, row_len):
    set_ends = jnp.cumsum(lengths_row[:-1])
    positions = jnp.arange(row_len, dtype=jnp.int32)
    return jnp.sum((positions[:, None] >= set_ends[None, :]).astype(jnp.int32), axis=1)


def gelu_curve(upward):
    return (
        0.5 * upward * (1.0 + jnp.tanh(gelu_coef * (upward + 0.044715 * upward * upward * upward)))
    )


def norm_parts(value):
    centered = value - jnp.mean(value, -1, keepdims=True)
    inv_std = lax.rsqrt(jnp.mean(centered * centered, -1, keepdims=True) + ln_eps)
    return (centered * inv_std, inv_std)


def norm_back(grad_out, normed, inv_std, gain):
    grad_normed = grad_out * gain
    return inv_std * (
        grad_normed
        - jnp.mean(grad_normed, -1, keepdims=True)
        - normed * jnp.mean(grad_normed * normed, -1, keepdims=True)
    )


def block_scores(q_block, key_heads, seg_block, segment, score_scale):
    scores = (
        jnp.einsum("qhd,khd->hqk", q_block, key_heads, preferred_element_type=jnp.float32)
        * score_scale
    )
    match = seg_block[:, None] == segment[None, :]
    return jnp.where(match[None], scores, masked_score)


def lamb_parts(weight, grad, first, second, sum_axes):
    m_one = beta_one * first + (1.0 - beta_one) * grad
    m_two = beta_two * second + (1.0 - beta_two) * grad * grad
    step_dir = (
        m_one
        / (1.0 - beta_one**adam_step)
        / (jnp.sqrt(m_two / (1.0 - beta_two**adam_step)) + adam_eps)
        + decay_rate * weight
    )
    return (
        m_one,
        m_two,
        step_dir,
        jnp.sum(weight * weight, axis=sum_axes),
        jnp.sum(step_dir * step_dir, axis=sum_axes),
    )


AXES = ("dp", "fsdp")


def swap(value, mask, count):
    return lax.ppermute(value, AXES, [(i, i ^ mask) for i in range(count)])


def device_index():
    return lax.axis_index("dp") * lax.axis_size("fsdp") + lax.axis_index("fsdp")


def hyper_sum(value, count):
    mask = 1
    while mask < count:
        value = value + swap(value, mask, count)
        mask *= 2
    return value


def gather_part(shard, order, inner, pair, count):
    parts = [shard] + [swap(shard, k, count) for k in range(1, inner)]
    masks = list(range(inner))
    held = jnp.stack(parts)
    for bit in order:
        held = jnp.concatenate([held, swap(held, bit, count)])
        masks = masks + [m ^ bit for m in masks]
    return masks + [m ^ pair for m in masks], (held, swap(held, pair, count))


def place_kernel(rows, layout, me_ref, *refs):
    out_ref, sem = refs[-2], refs[-1]
    me = me_ref[0]
    copies = []
    for number, (masks, first, column) in enumerate(layout):
        half = len(masks) // 2
        for side in range(2):
            src = refs[2 * number + side]
            mats, width = src.shape[1], src.shape[3]
            for j in range(half):
                row = pl.multiple_of((me ^ masks[side * half + j]) * rows, rows)
                copies.append(
                    pltpu.make_async_copy(
                        src.at[j],
                        out_ref.at[first : first + mats, pl.ds(row, rows), column : column + width],
                        sem,
                    )
                )
    for copy in copies:
        copy.start()
    for copy in copies:
        copy.wait()


def place(me, parts, mats, rows, count, width):
    layout = [(masks, first, column) for (masks, _), first, column in parts]
    arrays = [a for (_, pair), _, _ in parts for a in pair]
    return pl.pallas_call(
        lambda *refs: place_kernel(rows, layout, *refs),
        out_shape=jax.ShapeDtypeStruct((mats, rows * count, width), jnp.bfloat16),
        in_specs=[pl.BlockSpec(memory_space=pltpu.SMEM)]
        + [pl.BlockSpec(memory_space=pl.ANY)] * len(arrays),
        out_specs=pl.BlockSpec(memory_space=pl.ANY),
        scratch_shapes=[pltpu.SemaphoreType.DMA],
    )(me, *arrays)


def split_kernel(rows, masks, column, width, me_ref, src_ref, send_ref, keep_ref, sem):
    me = me_ref[0]
    half = len(masks) // 2
    copies = []
    for number, mask in enumerate(masks):
        row = pl.multiple_of((me ^ mask) * rows, rows)
        dst = keep_ref.at[number] if number < half else send_ref.at[number - half]
        copies.append(
            pltpu.make_async_copy(
                src_ref.at[:, pl.ds(row, rows), column : column + width], dst, sem
            )
        )
    for copy in copies:
        copy.start()
    for copy in copies:
        copy.wait()


def scatter_part(me, grads, column, width, order, inner, pair, count):
    rows = grads.shape[1] // count
    masks = list(range(inner))
    for bit in order[::-1]:
        masks = masks + [m ^ bit for m in masks]
    masks = masks + [m ^ pair for m in masks]
    half = len(masks) // 2
    shape = jax.ShapeDtypeStruct((half, grads.shape[0], rows, width), jnp.bfloat16)
    send, keep = pl.pallas_call(
        lambda *refs: split_kernel(rows, masks, column, width, *refs),
        out_shape=(shape, shape),
        in_specs=[
            pl.BlockSpec(memory_space=pltpu.SMEM),
            pl.BlockSpec(memory_space=pl.ANY),
        ],
        out_specs=[pl.BlockSpec(memory_space=pl.ANY)] * 2,
        scratch_shapes=[pltpu.SemaphoreType.DMA],
    )(me, grads)
    taken = swap(send, pair, count)
    held = keep.astype(jnp.float32) + taken.astype(jnp.float32)
    for bit in order:
        size = held.shape[0] // 2
        taken = swap(held[size:].astype(jnp.bfloat16), bit, count)
        held = held[:size] + taken.astype(jnp.float32)
    total = held[0]
    for k in range(1, inner):
        total = total + swap(held[k].astype(jnp.bfloat16), k, count).astype(jnp.float32)
    return total


def on_device(
    latents,
    lengths,
    cotangent,
    matrices,
    norm_params,
    moment1_mat,
    moment2_mat,
    moment1_norm,
    moment2_norm,
):
    row_len = latents.shape[1]
    width = latents.shape[2]
    head_dim = width // HEADS
    block_rows = row_len // max(1, row_len // 768)
    set_count = lengths.shape[1] - 1
    score_scale = 1.0 / math.sqrt(head_dim)
    low_mats = matrices.astype(jnp.bfloat16)
    low_norms = norm_params.astype(jnp.bfloat16)
    dp, fsdp = lax.axis_size("dp"), lax.axis_size("fsdp")
    count = dp * fsdp
    rows = matrices.shape[1]
    index = device_index()
    me = index.astype(jnp.int32)[None]
    ring = dp == 8 and fsdp == 4 and rows % 16 == 0
    half_w = width // 2
    if ring:
        inner, pair, first_bit, second_bit = fsdp, fsdp, 2 * fsdp, 4 * fsdp
        parts = []
        for first in (0, 3):
            for column, order in ((0, (first_bit, second_bit)), (half_w, (second_bit, first_bit))):
                shard = low_mats[first : first + 3, :, column : column + half_w]
                parts.append((gather_part(shard, order, inner, pair, count), first, column))
        weights = place(me, parts, 6, rows, count, width)
        spread = jnp.zeros((4, width), jnp.bfloat16)
        spread = lax.dynamic_update_slice(spread, low_norms, (0, index * rows))
        norms_low = hyper_sum(spread, count)
    else:
        weights = lax.all_gather(low_mats, AXES, axis=1, tiled=True)
        norms_low = lax.all_gather(low_norms, AXES, axis=1, tiled=True)
    weights_back = weights
    norm_vals = norms_low.astype(jnp.float32)
    segment = segment_ids(lengths[0], row_len)
    live_rows = (segment < set_count).astype(jnp.float32)[:, None]
    inputs = latents[0].astype(jnp.float32)
    normed_one, inv_one = norm_parts(inputs)
    h_one = (normed_one * norm_vals[0] + norm_vals[1]).astype(jnp.bfloat16)
    qkv = jnp.einsum("td,ide->tie", h_one, weights[:3], preferred_element_type=jnp.float32).astype(
        jnp.bfloat16
    )
    heads_all = qkv.reshape(row_len, 3, HEADS, head_dim)
    queries = heads_all[:, 0]
    key_heads = heads_all[:, 1]
    values = heads_all[:, 2]
    scores = block_scores(queries, key_heads, segment, segment, score_scale)
    row_max = jnp.max(scores, -1, keepdims=True)
    exp_scores = jnp.exp(scores - row_max)
    denom_sum = jnp.sum(exp_scores, -1, keepdims=True)
    probs_low = (exp_scores / denom_sum).astype(jnp.bfloat16)
    block_outs = jnp.einsum("hqk,khd->qhd", probs_low, values, preferred_element_type=jnp.float32)
    block_lse = [row_max + jnp.log(denom_sum)]
    attended = block_outs.reshape(row_len, width).astype(jnp.bfloat16)
    branch = jnp.dot(attended, weights[3], preferred_element_type=jnp.float32)
    middle = inputs + live_rows * branch
    normed_two, inv_two = norm_parts(middle)
    h_two = (normed_two * norm_vals[2] + norm_vals[3]).astype(jnp.bfloat16)
    upward = jnp.dot(h_two, weights[4], preferred_element_type=jnp.float32)
    activ, gelu_pull = jax.vjp(gelu_curve, upward)
    activ_low = activ.astype(jnp.bfloat16)
    result = middle + live_rows * jnp.dot(activ_low, weights[5], preferred_element_type=jnp.float32)
    gains_back = norm_vals
    grad_out = cotangent[0].astype(jnp.float32)
    grad_mlp = (live_rows * grad_out).astype(jnp.bfloat16)
    grad_five = jnp.einsum("tf,td->fd", activ_low, grad_mlp, preferred_element_type=jnp.float32)
    grad_activ = jnp.einsum(
        "td,fd->tf", grad_mlp, weights_back[5], preferred_element_type=jnp.float32
    )
    grad_up = gelu_pull(grad_activ)[0].astype(jnp.bfloat16)
    grad_four = jnp.einsum("te,tf->ef", h_two, grad_up, preferred_element_type=jnp.float32)
    grad_htwo = jnp.einsum(
        "tf,ef->te", grad_up, weights_back[4], preferred_element_type=jnp.float32
    )
    gain_two = jnp.sum(grad_htwo * normed_two, 0)
    shift_two = jnp.sum(grad_htwo, 0)
    grad_middle = grad_out + norm_back(grad_htwo, normed_two, inv_two, gains_back[2])
    mlp_mats_local = jnp.stack([grad_four, grad_five])
    mlp_norms_local = jnp.stack([gain_two, shift_two])
    grad_branch = (live_rows * grad_middle).astype(jnp.bfloat16)
    grad_three = jnp.einsum("te,td->ed", attended, grad_branch, preferred_element_type=jnp.float32)
    grad_attn = jnp.einsum(
        "td,ed->te", grad_branch, weights_back[3], preferred_element_type=jnp.float32
    )
    grad_attn = grad_attn.astype(jnp.bfloat16).reshape(row_len, HEADS, head_dim)
    grad_q_parts = []
    grad_keys = jnp.zeros((row_len, HEADS, head_dim), jnp.float32)
    grad_values = jnp.zeros((row_len, HEADS, head_dim), jnp.float32)
    for number, offset in enumerate(range(0, row_len, block_rows)):
        scores = block_scores(queries, key_heads, segment, segment, score_scale)
        probs = jnp.exp(scores - block_lse[number])
        probs_low = probs.astype(jnp.bfloat16)
        grad_values = jnp.einsum(
            "hqk,qhd->khd", probs_low, grad_attn, preferred_element_type=jnp.float32
        )
        grad_probs = jnp.einsum(
            "qhd,khd->hqk", grad_attn, values, preferred_element_type=jnp.float32
        )
        row_dot = jnp.sum(grad_probs * probs, -1, keepdims=True)
        grad_scores = (probs * (grad_probs - row_dot)).astype(jnp.bfloat16)
        grad_q_parts.append(
            jnp.einsum("hqk,khd->qhd", grad_scores, key_heads, preferred_element_type=jnp.float32)
            * score_scale
        )
        grad_keys = (
            jnp.einsum("hqk,qhd->khd", grad_scores, queries, preferred_element_type=jnp.float32)
            * score_scale
        )
    grad_queries = grad_q_parts[0]
    grad_qkv = (
        jnp.stack([grad_queries, grad_keys, grad_values], 1)
        .reshape(row_len, 3, width)
        .astype(jnp.bfloat16)
    )
    grad_proj = jnp.einsum("td,tie->ide", h_one, grad_qkv, preferred_element_type=jnp.float32)
    grad_hone = jnp.einsum(
        "tie,ide->td", grad_qkv, weights_back[:3], preferred_element_type=jnp.float32
    )
    gain_one = jnp.sum(grad_hone * normed_one, 0)
    shift_one = jnp.sum(grad_hone, 0)
    grad_input = grad_middle + norm_back(grad_hone, normed_one, inv_one, gains_back[0])
    attn_mats_local = jnp.concatenate([grad_proj, grad_three[None]], 0)
    attn_norms_local = jnp.stack([gain_one, shift_one])
    norms_local = jnp.concatenate([attn_norms_local, mlp_norms_local], 0)
    if ring:
        pieces = []
        for local in (attn_mats_local[:3], jnp.concatenate([grad_three[None], mlp_mats_local], 0)):
            low_grads = local.astype(jnp.bfloat16)
            pieces.append(
                jnp.concatenate(
                    [
                        scatter_part(me, low_grads, column, half_w, order, inner, pair, count)
                        for column, order in (
                            (0, (second_bit, first_bit)),
                            (half_w, (first_bit, second_bit)),
                        )
                    ],
                    -1,
                )
            )
        grad_mats = jnp.concatenate(pieces, 0)
        grad_norms = lax.dynamic_slice(
            hyper_sum(norms_local, count), (0, index * rows), (4, rows)
        )
    else:
        mats_local = jnp.concatenate([attn_mats_local, mlp_mats_local], 0)
        grad_mats = lax.psum_scatter(mats_local, AXES, scatter_dimension=1, tiled=True)
        grad_norms = lax.psum_scatter(norms_local, AXES, scatter_dimension=1, tiled=True)
    m1_mat, m2_mat, dir_mat, wsq_mat, usq_mat = lamb_parts(
        matrices, grad_mats, moment1_mat, moment2_mat, (1, 2)
    )
    m1_norm, m2_norm, dir_norm, wsq_norm, usq_norm = lamb_parts(
        norm_params, grad_norms, moment1_norm, moment2_norm, (1,)
    )
    squares = jnp.stack(
        [jnp.concatenate([wsq_mat, wsq_norm]), jnp.concatenate([usq_mat, usq_norm])]
    )
    squares = hyper_sum(squares, count) if ring else lax.psum(squares, AXES)
    weight_sq, update_sq = squares[0], squares[1]
    ratios = jnp.sqrt(weight_sq) / jnp.sqrt(update_sq)
    scaled_mats = ratios[:6][:, None, None] * dir_mat
    scaled_norms = ratios[6:][:, None] * dir_norm
    return (
        result.astype(jnp.bfloat16)[None],
        grad_input.astype(jnp.bfloat16)[None],
        grad_mats,
        grad_norms,
        scaled_mats,
        scaled_norms,
        m1_mat,
        m2_mat,
        m1_norm,
        m2_norm,
        ratios,
    )


def solution(mesh):
    return jax.shard_map(
        on_device,
        mesh=mesh,
        in_specs=(
            P(("dp", "fsdp"), None, None),
            P(("dp", "fsdp"), None),
            P(("dp", "fsdp"), None, None),
            P(None, ("dp", "fsdp"), None),
            P(None, ("dp", "fsdp")),
            P(None, ("dp", "fsdp"), None),
            P(None, ("dp", "fsdp"), None),
            P(None, ("dp", "fsdp")),
            P(None, ("dp", "fsdp")),
        ),
        out_specs=(
            P(("dp", "fsdp"), None, None),
            P(("dp", "fsdp"), None, None),
            P(None, ("dp", "fsdp"), None),
            P(None, ("dp", "fsdp")),
            P(None, ("dp", "fsdp"), None),
            P(None, ("dp", "fsdp")),
            P(None, ("dp", "fsdp"), None),
            P(None, ("dp", "fsdp"), None),
            P(None, ("dp", "fsdp")),
            P(None, ("dp", "fsdp")),
            P(),
        ),
        check_vma=False,
    )
```

```python
import functools
import math

import jax
import jax.numpy as jnp
from jax import lax
from jax.experimental import pallas as pl
from jax.experimental.pallas import tpu as pltpu
from jax.sharding import PartitionSpec as P

HEADS = 8
AXES = ("dp", "fsdp")

ln_eps = 1e-05
beta_one = 0.9
beta_two = 0.999
adam_eps = 1e-06
decay_rate = 0.01
adam_step = 100.0
gelu_coef = 0.7978845608
cubic_coef = 0.044715
mask_depth = -1e30

F32 = jnp.float32
LOW = jnp.bfloat16
NT = (((1,), (1,)), ((), ()))
TN = (((0,), (0,)), ((), ()))
SMEM = pl.BlockSpec(memory_space=pltpu.SMEM)
VMEM = pl.BlockSpec(memory_space=pltpu.VMEM)


def params(mib):
    return pltpu.CompilerParams(vmem_limit_bytes=mib * 2**20)


def shape(dims, kind):
    return jax.ShapeDtypeStruct(dims, kind)


def product(left, right, dims=(((1,), (0,)), ((), ()))):
    return lax.dot_general(left, right, dims, preferred_element_type=F32)


def cost(flops, moved):
    return pl.CostEstimate(flops=int(flops), bytes_accessed=int(moved), transcendentals=0)


def swap(value, mask, count):
    return lax.ppermute(value, AXES, [(i, i ^ mask) for i in range(count)])


def hyper_sum(value, count):
    mask = 1
    while mask < count:
        value = value + swap(value, mask, count)
        mask *= 2
    return value


def mask_order(order, inner, pair):
    masks = list(range(inner))
    for bit in order:
        masks = masks + [m ^ bit for m in masks]
    return masks + [m ^ pair for m in masks]


def gather_near(shard, inner, count):
    return jnp.stack([shard] + [swap(shard, k, count) for k in range(1, inner)])


def gather_far(held, order, pair, count):
    for bit in order:
        held = jnp.concatenate([held, swap(held, bit, count)])
    return held, swap(held, pair, count)


def scatter_sum(keep, send, order, inner, pair, count):
    taken = swap(send, pair, count)
    held = keep.astype(F32) + taken.astype(F32)
    for bit in order[::-1]:
        size = held.shape[0] // 2
        taken = swap(held[size:].astype(LOW), bit, count)
        held = held[:size] + taken.astype(F32)
    total = held[0]
    for k in range(1, inner):
        total = total + swap(held[k].astype(LOW), k, count).astype(F32)
    return total


def normalize(value):
    centered = value - jnp.mean(value, -1, keepdims=True)
    inv_std = lax.rsqrt(jnp.mean(centered * centered, -1, keepdims=True) + ln_eps)
    return centered * inv_std, inv_std


def norm_back(grad_out, normed, inv_std, gain):
    grad_normed = grad_out * gain
    return inv_std * (
        grad_normed
        - jnp.mean(grad_normed, -1, keepdims=True)
        - normed * jnp.mean(grad_normed * normed, -1, keepdims=True)
    )


def place_rows(table_ref, line, chunk_refs, out_ref, column):
    start = 0
    for ref in chunk_refs:
        number, _, rows, wide = ref.shape

        @pl.loop(0, number)
        def _(j, ref=ref, rows=rows, wide=wide, start=start):
            row = pl.multiple_of(table_ref[line, start + j] * rows, rows)
            out_ref[:, pl.ds(row, rows), column : column + wide] = ref[j]

        start += number


def place_all(table_ref, layout, refs, out_ref):
    first = 0
    for line, (number, column) in enumerate(layout):
        place_rows(table_ref, line, refs[first : first + number], out_ref, column)
        first += number


def project_kernel(layout, block, table_ref, x_ref, norm_ref, *refs):
    parts, (hidden_ref, out_ref, weight_ref) = refs[:-3], refs[-3:]
    place_all(table_ref, layout, parts, weight_ref)
    mats, width, _ = weight_ref.shape

    @pl.loop(0, x_ref.shape[0] // block)
    def _(i):
        rows = pl.ds(pl.multiple_of(i * block, block), block)
        normed, _ = normalize(x_ref[rows, :].astype(F32))
        hidden = (normed * norm_ref[0:1, :] + norm_ref[1:2, :]).astype(LOW)
        hidden_ref[rows, :] = hidden
        for j in range(mats):
            out_ref[rows, j * width : (j + 1) * width] = product(hidden, weight_ref[j]).astype(LOW)


def attend_kernel(group, dim, power, q_ref, k_ref, v_ref, in_ref, out_ref, o_ref, lse_ref):
    for g in range(group):
        span = slice(g * dim, (g + 1) * dim)
        keys = jnp.concatenate([k_ref[:, span], out_ref[...]], 1)
        queries = jnp.concatenate([q_ref[:, span], in_ref[...]], 1)
        scores = product(keys, queries, NT)
        top = jnp.max(scores, 0, keepdims=True)
        weight = jnp.exp2((scores - top) * power)
        total = jnp.sum(weight, 0, keepdims=True)
        probs = (weight * (1.0 / total)).astype(LOW)
        o_ref[:, span] = product(v_ref[:, span].T, probs).T.astype(LOW)
        lse_ref[g] = top * power + jnp.log2(total)


def attend_back_kernel(
    group, dim, power, scale, block,
    q_ref, k_ref, v_ref, do_ref, o_ref, in_ref, out_ref, lse_ref,
    dq_ref, dk_ref, dv_ref, sum_ref,
):
    length = q_ref.shape[0]
    for g in range(group):
        span = slice(g * dim, (g + 1) * dim)
        queries, grad = q_ref[:, span], do_ref[:, span]
        marked = jnp.concatenate([queries, in_ref[...]], 1)
        both = grad.astype(F32) * o_ref[:, span].astype(F32)
        row_dot = lax.dot_general(
            jnp.ones((8, dim), F32), both, NT,
            preferred_element_type=F32, precision=lax.Precision.HIGHEST,
        )[0:1]
        log_sum = lse_ref[g]
        for r in range(length // block):
            rows = slice(r * block, (r + 1) * block)
            keys = k_ref[rows, span]
            scores = product(jnp.concatenate([keys, out_ref[rows, :]], 1), marked, NT)
            probs = jnp.exp2(scores * power - log_sum)
            grad_probs = product(v_ref[rows, span], grad, NT)
            grad_scores = (probs * (grad_probs - row_dot)).astype(LOW)
            dv_ref[rows, span] = product(probs.astype(LOW), grad).astype(LOW)
            dk_ref[rows, span] = (product(grad_scores, queries) * scale).astype(LOW)
            part = product(keys.T, grad_scores)
            if r == 0:
                sum_ref[g] = part
            else:
                sum_ref[g] += part
        dq_ref[:, span] = (sum_ref[g].T * scale).astype(LOW)


def middle_kernel(layout, block, table_ref, x_ref, dz_ref, att_ref, live_ref, norm_ref, *refs):
    parts = refs[:-9]
    (result_ref, dmid_ref, dmlp_ref, hidden_ref, dup_ref, act_ref, dbranch_ref, dnorm_ref, weight_ref) = refs[-9:]
    place_all(table_ref, layout, parts, weight_ref)
    gain, shift = norm_ref[2:3, :], norm_ref[3:4, :]
    dnorm_ref[...] = jnp.zeros_like(dnorm_ref)

    @pl.loop(0, x_ref.shape[0] // block)
    def _(i):
        rows = pl.ds(pl.multiple_of(i * block, block), block)
        live = live_ref[rows, :]
        middle = x_ref[rows, :].astype(F32) + live * product(att_ref[rows, :], weight_ref[0])
        normed, inv_std = normalize(middle)
        hidden = (normed * gain + shift).astype(LOW)
        hidden_ref[rows, :] = hidden
        upward = product(hidden, weight_ref[1])
        square = upward * upward
        bend = jnp.tanh(gelu_coef * (upward + cubic_coef * square * upward))
        half = 0.5 * (1.0 + bend)
        active = (upward * half).astype(LOW)
        act_ref[rows, :] = active
        slope = half + (0.5 * gelu_coef) * upward * (1.0 - bend * bend) * (
            1.0 + (3.0 * cubic_coef) * square
        )
        result_ref[rows, :] = (middle + live * product(active, weight_ref[2])).astype(LOW)
        grad = dz_ref[rows, :].astype(F32)
        dmlp = (live * grad).astype(LOW)
        dmlp_ref[rows, :] = dmlp
        dup = (product(dmlp, weight_ref[2], NT) * slope).astype(LOW)
        dup_ref[rows, :] = dup
        dhidden = product(dup, weight_ref[1], NT)
        dnorm_ref[0:1, :] += jnp.sum(dhidden * normed, 0, keepdims=True)
        dnorm_ref[1:2, :] += jnp.sum(dhidden, 0, keepdims=True)
        dmid = grad + norm_back(dhidden, normed, inv_std, gain)
        dmid_ref[rows, :] = dmid
        dbranch_ref[rows, :] = (live * dmid).astype(LOW)


def branch_back_kernel(dbranch_ref, weight_ref, out_ref):
    out_ref[...] = product(dbranch_ref[...], weight_ref[0], NT).astype(LOW)


def last_kernel(block, x_ref, dmid_ref, norm_ref, weight_ref, *refs):
    grads, (out_ref, dnorm_ref) = refs[:-2], refs[-2:]
    mats = weight_ref.shape[0]
    gain = norm_ref[0:1, :]
    dnorm_ref[...] = jnp.zeros_like(dnorm_ref)

    @pl.loop(0, x_ref.shape[0] // block)
    def _(i):
        rows = pl.ds(pl.multiple_of(i * block, block), block)
        total, column = None, 0
        for first in range(0, len(grads), mats):
            wide = grads[first].shape[1]
            for j in range(mats):
                part = product(
                    grads[first + j][rows, :], weight_ref[j, :, column : column + wide], NT
                )
                total = part if total is None else total + part
            column += wide
        normed, inv_std = normalize(x_ref[rows, :].astype(F32))
        dnorm_ref[0:1, :] += jnp.sum(total * normed, 0, keepdims=True)
        dnorm_ref[1:2, :] += jnp.sum(total, 0, keepdims=True)
        out_ref[rows, :] = (
            dmid_ref[rows, :] + norm_back(total, normed, inv_std, gain)
        ).astype(LOW)


def weight_grad_kernel(mats, halves, table_ref, *refs):
    lefts, rights = refs[:mats], refs[mats : 2 * mats]
    outs, held_ref = refs[2 * mats : -1], refs[-1]
    width = held_ref.shape[0]
    step = min(256, width)
    per = len(outs) // halves
    for j in range(mats):
        for c in range(0, width, step):
            left = lefts[j][:, c : c + step]
            held_ref[c : c + step, :] = product(left, rights[j][...], TN).astype(LOW)
        for h in range(halves):
            start = 0
            for ref in outs[h * per : (h + 1) * per]:
                number, _, rows, wide = ref.shape

                @pl.loop(0, number)
                def _(n, ref=ref, rows=rows, wide=wide, start=start, j=j, h=h):
                    row = pl.multiple_of(table_ref[h, start + n] * rows, rows)
                    ref[n, j] = held_ref[pl.ds(row, rows), h * wide : (h + 1) * wide]

                start += number


def weight_grads(table, lefts, rights, outs, halves):
    mats = len(rights)
    length, width = lefts[0].shape
    wide = rights[0].shape[1]
    return pl.pallas_call(
        functools.partial(weight_grad_kernel, mats, halves),
        out_shape=[shape((n, mats, rows, w), LOW) for n, rows, w in outs],
        in_specs=[SMEM] + [VMEM] * (2 * mats),
        out_specs=[VMEM] * len(outs),
        scratch_shapes=[pltpu.VMEM((width, wide), LOW)],
        compiler_params=params(48),
        cost_estimate=cost(2 * mats * length * width * wide, 4 * mats * width * wide),
    )(table, *lefts, *rights)


def lamb_parts(weight, grad, first, second, sum_axes):
    m_one = beta_one * first + (1.0 - beta_one) * grad
    m_two = beta_two * second + (1.0 - beta_two) * grad * grad
    step_dir = (
        m_one
        / (1.0 - beta_one**adam_step)
        / (jnp.sqrt(m_two / (1.0 - beta_two**adam_step)) + adam_eps)
        + decay_rate * weight
    )
    return (
        m_one,
        m_two,
        step_dir,
        jnp.sum(weight * weight, axis=sum_axes),
        jnp.sum(step_dir * step_dir, axis=sum_axes),
    )


def on_device(
    latents,
    lengths,
    cotangent,
    matrices,
    norm_params,
    moment1_mat,
    moment2_mat,
    moment1_norm,
    moment2_norm,
):
    _, length, width = latents.shape
    dim = width // HEADS
    scale = 1.0 / math.sqrt(dim)
    power = scale * math.log2(math.e)
    dp, fsdp = lax.axis_size("dp"), lax.axis_size("fsdp")
    count = dp * fsdp
    rows = matrices.shape[1]
    index = lax.axis_index("dp") * fsdp + lax.axis_index("fsdp")
    ring = dp == 8 and fsdp == 4 and rows % 16 == 0
    inner, pair = fsdp, fsdp
    orders = ((2 * fsdp, 4 * fsdp), (4 * fsdp, 2 * fsdp))
    half_w = width // 2
    block = 256 if length % 256 == 0 else length
    low_mats = matrices.astype(LOW)
    low_norms = norm_params.astype(LOW)

    if ring:
        masks = jnp.array([mask_order(o, inner, pair) for o in orders], jnp.int32)
        table = jnp.bitwise_xor(masks, index.astype(jnp.int32))
        columns = (0, half_w)
        near, groups = [], []
        for first in (0, 3):
            shards = [low_mats[first : first + 3, :, c : c + half_w] for c in columns]
            if near:
                shards, near = lax.optimization_barrier((shards, near))
            fresh = [gather_near(s, inner, count) for s in shards]
            near = near + fresh
        for first in (0, 2):
            groups.append(
                [gather_far(n, o, pair, count) for n, o in zip(near[first : first + 2], orders)]
            )
        layout = tuple((2, c) for c in columns)
        spread = lax.dynamic_update_slice(
            jnp.zeros((4, width), LOW), low_norms, (0, index * rows)
        )
        norms_low = hyper_sum(spread, count)
        grad_outs = [(count // 2, rows, half_w)] * 4
    else:
        weights = lax.all_gather(low_mats, AXES, axis=1, tiled=True)
        norms_low = lax.all_gather(low_norms, AXES, axis=1, tiled=True)
        table = jnp.zeros((1, 1), jnp.int32)
        groups = [[(weights[None, :3],)], [(weights[None, 3:],)]]
        layout = ((1, 0),)
        grad_outs = [(1, width, width)]
    norm_vals = norms_low.astype(F32)

    ends = jnp.cumsum(lengths[0, :-1])
    sets = ends.shape[0]
    segment = jnp.sum(
        (jnp.arange(length, dtype=jnp.int32)[:, None] >= ends[None, :]).astype(jnp.int32), axis=1
    )
    live = (segment < sets).astype(F32)[:, None]
    lanes = jnp.arange(128, dtype=jnp.int32)[None, :]
    same = segment[:, None] == lanes
    mark_in = same.astype(LOW)
    mark_out = jnp.where(same | (lanes > sets), 0.0, mask_depth).astype(LOW)

    x, dz = latents[0], cotangent[0]
    parts = [a for arrays in groups[0] for a in arrays]
    hidden_one, qkv, weights_in = pl.pallas_call(
        functools.partial(project_kernel, layout, block),
        out_shape=[
            shape((length, width), LOW),
            shape((length, 3 * width), LOW),
            shape((3, width, width), LOW),
        ],
        in_specs=[SMEM] + [VMEM] * (2 + len(parts)),
        out_specs=[VMEM] * 3,
        compiler_params=params(48),
        cost_estimate=cost(6 * length * width * width, 12 * width * width),
    )(table, x, norm_vals, *parts)

    group = 2

    def heads_at(offset):
        return pl.BlockSpec((length, dim * group), lambda h, o=offset // group: (0, o + h))

    whole = pl.BlockSpec((length, 128), lambda h: (0, 0))
    attended, log_sums = pl.pallas_call(
        functools.partial(attend_kernel, group, dim, power),
        grid=(HEADS // group,),
        in_specs=[heads_at(0), heads_at(HEADS), heads_at(2 * HEADS), whole, whole],
        out_specs=[heads_at(0), pl.BlockSpec((group, 1, length), lambda h: (h, 0, 0))],
        out_shape=[shape((length, width), LOW), shape((HEADS, 1, length), F32)],
        compiler_params=params(48),
        cost_estimate=cost(8 * length * length * width, 8 * length * width),
    )(qkv, qkv, qkv, mark_in, mark_out)

    parts = [a for arrays in groups[1] for a in arrays]
    (result, dmid, dmlp, hidden_two, dup, active, dbranch, dnorm_two, weights_out) = pl.pallas_call(
        functools.partial(middle_kernel, layout, block),
        out_shape=[
            shape((length, width), LOW),
            shape((length, width), F32),
            *[shape((length, width), LOW)] * 5,
            shape((2, width), F32),
            shape((3, width, width), LOW),
        ],
        in_specs=[SMEM] + [VMEM] * (5 + len(parts)),
        out_specs=[VMEM] * 9,
        compiler_params=params(56),
        cost_estimate=cost(10 * length * width * width, 12 * width * width),
    )(table, x, dz, attended, live, norm_vals, *parts)
    out_grads = weight_grads(
        table, [attended, hidden_two, active], [dbranch, dup, dmlp], grad_outs, len(layout)
    )
    dattended = pl.pallas_call(
        branch_back_kernel,
        out_shape=shape((length, width), LOW),
        in_specs=[VMEM] * 2,
        out_specs=VMEM,
        compiler_params=params(48),
        cost_estimate=cost(2 * length * width * width, 2 * width * width),
    )(dbranch, weights_out)

    def attend_back(first, number):
        def at(offset):
            return pl.BlockSpec(
                (length, dim * group), lambda h, o=(offset + first) // group: (0, o + h)
            )

        return pl.pallas_call(
            functools.partial(attend_back_kernel, group, dim, power, scale, length),
            grid=(number // group,),
            in_specs=[at(0), at(HEADS), at(2 * HEADS), at(0), at(0), whole, whole]
            + [pl.BlockSpec((group, 1, length), lambda h: (first // group + h, 0, 0))],
            out_specs=[heads_at(0)] * 3,
            out_shape=[shape((length, dim * number), LOW)] * 3,
            scratch_shapes=[pltpu.VMEM((group, dim, length), F32)],
            compiler_params=params(48),
            cost_estimate=cost(20 * length * length * dim * number, 16 * length * dim * number),
        )(qkv, qkv, qkv, dattended, attended, mark_in, mark_out, log_sums)

    grads_in, in_grads = [], []
    half_heads = HEADS // len(layout)
    for number in range(len(layout)):
        found = attend_back(number * half_heads, half_heads)
        grads_in += found
        lines = table[number : number + 1]
        per = len(grad_outs) // len(layout)
        in_grads += weight_grads(
            lines, [hidden_one] * 3, found, grad_outs[number * per : (number + 1) * per], 1
        )
    grad_latents, dnorm_one = pl.pallas_call(
        functools.partial(last_kernel, block),
        out_shape=[shape((length, width), LOW), shape((2, width), F32)],
        in_specs=[VMEM] * (4 + len(grads_in)),
        out_specs=[VMEM] * 2,
        compiler_params=params(48),
        cost_estimate=cost(6 * length * width * width, 6 * width * width),
    )(x, dmid, norm_vals, weights_in, *grads_in)

    norms_local = jnp.concatenate([dnorm_one, dnorm_two], 0)
    if ring:
        sums = []
        for grads in (in_grads, out_grads):
            sums.append(
                jnp.concatenate(
                    [
                        scatter_sum(grads[2 * n], grads[2 * n + 1], o, inner, pair, count)
                        for n, o in enumerate(orders)
                    ],
                    -1,
                )
            )
        grad_mats = jnp.concatenate(sums, 0)
        grad_norms = lax.dynamic_slice(
            hyper_sum(norms_local, count), (0, index * rows), (4, rows)
        )
    else:
        mats_local = jnp.concatenate([in_grads[0][0], out_grads[0][0]], 0).astype(F32)
        grad_mats = lax.psum_scatter(mats_local, AXES, scatter_dimension=1, tiled=True)
        grad_norms = lax.psum_scatter(norms_local, AXES, scatter_dimension=1, tiled=True)

    m1_mat, m2_mat, dir_mat, wsq_mat, usq_mat = lamb_parts(
        matrices, grad_mats, moment1_mat, moment2_mat, (1, 2)
    )
    m1_norm, m2_norm, dir_norm, wsq_norm, usq_norm = lamb_parts(
        norm_params, grad_norms, moment1_norm, moment2_norm, (1,)
    )
    squares = jnp.stack(
        [jnp.concatenate([wsq_mat, wsq_norm]), jnp.concatenate([usq_mat, usq_norm])]
    )
    squares = hyper_sum(squares, count) if ring else lax.psum(squares, AXES)
    ratios = jnp.sqrt(squares[0]) / jnp.sqrt(squares[1])
    scaled_mats = ratios[:6][:, None, None] * dir_mat
    scaled_norms = ratios[6:][:, None] * dir_norm
    return (
        result[None],
        grad_latents[None],
        grad_mats,
        grad_norms,
        scaled_mats,
        scaled_norms,
        m1_mat,
        m2_mat,
        m1_norm,
        m2_norm,
        ratios,
    )


def solution(mesh):
    return jax.shard_map(
        on_device,
        mesh=mesh,
        in_specs=(
            P(("dp", "fsdp"), None, None),
            P(("dp", "fsdp"), None),
            P(("dp", "fsdp"), None, None),
            P(None, ("dp", "fsdp"), None),
            P(None, ("dp", "fsdp")),
            P(None, ("dp", "fsdp"), None),
            P(None, ("dp", "fsdp"), None),
            P(None, ("dp", "fsdp")),
            P(None, ("dp", "fsdp")),
        ),
        out_specs=(
            P(("dp", "fsdp"), None, None),
            P(("dp", "fsdp"), None, None),
            P(None, ("dp", "fsdp"), None),
            P(None, ("dp", "fsdp")),
            P(None, ("dp", "fsdp"), None),
            P(None, ("dp", "fsdp")),
            P(None, ("dp", "fsdp"), None),
            P(None, ("dp", "fsdp"), None),
            P(None, ("dp", "fsdp")),
            P(None, ("dp", "fsdp")),
            P(),
        ),
        check_vma=False,
    )
```

```python
import functools
import math

import jax
import jax.numpy as jnp
from jax import lax
from jax.experimental import pallas as pl
from jax.experimental.pallas import tpu as pltpu
from jax.sharding import PartitionSpec as P

HEADS = 8
AXES = ("dp", "fsdp")

ln_eps = 1e-05
beta_one = 0.9
beta_two = 0.999
adam_eps = 1e-06
decay_rate = 0.01
adam_step = 100.0
gelu_coef = 0.7978845608
cubic_coef = 0.044715
mask_depth = -1e30

F32 = jnp.float32
LOW = jnp.bfloat16
NT = (((1,), (1,)), ((), ()))
TN = (((0,), (0,)), ((), ()))
SMEM = pl.BlockSpec(memory_space=pltpu.SMEM)
VMEM = pl.BlockSpec(memory_space=pltpu.VMEM)


def params(mib):
    return pltpu.CompilerParams(vmem_limit_bytes=mib * 2**20)


def shape(dims, kind):
    return jax.ShapeDtypeStruct(dims, kind)


def product(left, right, dims=(((1,), (0,)), ((), ()))):
    return lax.dot_general(left, right, dims, preferred_element_type=F32)


def cost(flops, moved):
    return pl.CostEstimate(flops=int(flops), bytes_accessed=int(moved), transcendentals=0)


def swap(value, mask, count):
    return lax.ppermute(value, AXES, [(i, i ^ mask) for i in range(count)])


def hyper_sum(value, count):
    mask = 1
    while mask < count:
        value = value + swap(value, mask, count)
        mask *= 2
    return value


def mask_order(order, inner, pair):
    masks = list(range(inner))
    for bit in order:
        masks = masks + [m ^ bit for m in masks]
    return masks + [m ^ pair for m in masks]


def after(value, *others):
    return lax.optimization_barrier((value, others))[0]


def gather_near(shard, inner, count):
    return jnp.stack([shard] + [swap(shard, k, count) for k in range(1, inner)])


def grow(held, taken):
    return [jnp.concatenate(both) for both in zip(held, taken)]


def swap_all(values, bits, count):
    return [swap(v, b, count) for v, b in zip(values, bits)]


def fold(held, taken):
    total = [h + t.astype(F32) for h, t in zip(held, taken)]
    size = total[0].shape[0] // 2
    return [t[:size] for t in total], [t[size:].astype(LOW) for t in total]


def near_sum(held, inner, count):
    taken = [swap(held[k].astype(LOW), k, count) for k in range(1, inner)]
    return held[0], taken


def add_all(value, others):
    for other in others:
        value = value + other.astype(F32)
    return value


def normalize(value):
    centered = value - jnp.mean(value, -1, keepdims=True)
    inv_std = lax.rsqrt(jnp.mean(centered * centered, -1, keepdims=True) + ln_eps)
    return centered * inv_std, inv_std


def norm_back(grad_out, normed, inv_std, gain):
    grad_normed = grad_out * gain
    return inv_std * (
        grad_normed
        - jnp.mean(grad_normed, -1, keepdims=True)
        - normed * jnp.mean(grad_normed * normed, -1, keepdims=True)
    )


def place_rows(table_ref, line, chunk_refs, out_ref, column):
    start = 0
    for ref in chunk_refs:
        number, _, rows, wide = ref.shape

        @pl.loop(0, number)
        def _(j, ref=ref, rows=rows, wide=wide, start=start):
            row = pl.multiple_of(table_ref[line, start + j] * rows, rows)
            out_ref[:, pl.ds(row, rows), column : column + wide] = ref[j]

        start += number


def place_all(table_ref, layout, refs, out_ref):
    first = 0
    for line, (number, column) in enumerate(layout):
        place_rows(table_ref, line, refs[first : first + number], out_ref, column)
        first += number


def project_kernel(layout, block, table_ref, x_ref, norm_ref, *refs):
    parts, (hidden_ref, out_ref, weight_ref) = refs[:-3], refs[-3:]
    place_all(table_ref, layout, parts, weight_ref)
    mats, width, _ = weight_ref.shape

    @pl.loop(0, x_ref.shape[0] // block)
    def _(i):
        rows = pl.ds(pl.multiple_of(i * block, block), block)
        normed, _ = normalize(x_ref[rows, :].astype(F32))
        hidden = (normed * norm_ref[0:1, :] + norm_ref[1:2, :]).astype(LOW)
        hidden_ref[rows, :] = hidden
        for j in range(mats):
            out_ref[rows, j * width : (j + 1) * width] = product(hidden, weight_ref[j]).astype(LOW)


def attend_kernel(group, dim, power, q_ref, k_ref, v_ref, in_ref, out_ref, o_ref, lse_ref):
    for g in range(group):
        span = slice(g * dim, (g + 1) * dim)
        keys = jnp.concatenate([k_ref[:, span], out_ref[...]], 1)
        queries = jnp.concatenate([q_ref[:, span], in_ref[...]], 1)
        scores = product(keys, queries, NT)
        top = jnp.max(scores, 0, keepdims=True)
        weight = jnp.exp2((scores - top) * power)
        total = jnp.sum(weight, 0, keepdims=True)
        probs = (weight * (1.0 / total)).astype(LOW)
        o_ref[:, span] = product(v_ref[:, span].T, probs).T.astype(LOW)
        lse_ref[g] = top * power + jnp.log2(total)


def attend_back_kernel(
    group, dim, power, scale, block,
    q_ref, k_ref, v_ref, do_ref, o_ref, in_ref, out_ref, lse_ref,
    dq_ref, dk_ref, dv_ref, sum_ref,
):
    length = q_ref.shape[0]
    for g in range(group):
        span = slice(g * dim, (g + 1) * dim)
        queries, grad = q_ref[:, span], do_ref[:, span]
        marked = jnp.concatenate([queries, in_ref[...]], 1)
        both = grad.astype(F32) * o_ref[:, span].astype(F32)
        row_dot = lax.dot_general(
            jnp.ones((8, dim), F32), both, NT,
            preferred_element_type=F32, precision=lax.Precision.HIGHEST,
        )[0:1]
        log_sum = lse_ref[g]
        for r in range(length // block):
            rows = slice(r * block, (r + 1) * block)
            keys = k_ref[rows, span]
            scores = product(jnp.concatenate([keys, out_ref[rows, :]], 1), marked, NT)
            probs = jnp.exp2(scores * power - log_sum)
            grad_probs = product(v_ref[rows, span], grad, NT)
            grad_scores = (probs * (grad_probs - row_dot)).astype(LOW)
            dv_ref[rows, span] = product(probs.astype(LOW), grad).astype(LOW)
            dk_ref[rows, span] = (product(grad_scores, queries) * scale).astype(LOW)
            part = product(keys.T, grad_scores)
            if r == 0:
                sum_ref[g] = part
            else:
                sum_ref[g] += part
        dq_ref[:, span] = (sum_ref[g].T * scale).astype(LOW)


def middle_kernel(layout, block, table_ref, x_ref, dz_ref, live_ref, norm_ref, *refs):
    atts, parts = refs[: len(layout)], refs[len(layout) : -9]
    (result_ref, dmid_ref, dmlp_ref, hidden_ref, dup_ref, act_ref, dbranch_ref, dnorm_ref, weight_ref) = refs[-9:]
    place_all(table_ref, layout, parts, weight_ref)
    gain, shift = norm_ref[2:3, :], norm_ref[3:4, :]
    dnorm_ref[...] = jnp.zeros_like(dnorm_ref)

    @pl.loop(0, x_ref.shape[0] // block)
    def _(i):
        rows = pl.ds(pl.multiple_of(i * block, block), block)
        live = live_ref[rows, :]
        branch, first = None, 0
        for ref in atts:
            part = product(ref[rows, :], weight_ref[0, first : first + ref.shape[1], :])
            branch = part if branch is None else branch + part
            first += ref.shape[1]
        middle = x_ref[rows, :].astype(F32) + live * branch
        normed, inv_std = normalize(middle)
        hidden = (normed * gain + shift).astype(LOW)
        hidden_ref[rows, :] = hidden
        upward = product(hidden, weight_ref[1])
        square = upward * upward
        bend = jnp.tanh(gelu_coef * (upward + cubic_coef * square * upward))
        half = 0.5 * (1.0 + bend)
        active = (upward * half).astype(LOW)
        act_ref[rows, :] = active
        slope = half + (0.5 * gelu_coef) * upward * (1.0 - bend * bend) * (
            1.0 + (3.0 * cubic_coef) * square
        )
        result_ref[rows, :] = (middle + live * product(active, weight_ref[2])).astype(LOW)
        grad = dz_ref[rows, :].astype(F32)
        dmlp = (live * grad).astype(LOW)
        dmlp_ref[rows, :] = dmlp
        dup = (product(dmlp, weight_ref[2], NT) * slope).astype(LOW)
        dup_ref[rows, :] = dup
        dhidden = product(dup, weight_ref[1], NT)
        dnorm_ref[0:1, :] += jnp.sum(dhidden * normed, 0, keepdims=True)
        dnorm_ref[1:2, :] += jnp.sum(dhidden, 0, keepdims=True)
        dmid = grad + norm_back(dhidden, normed, inv_std, gain)
        dmid_ref[rows, :] = dmid
        dbranch_ref[rows, :] = (live * dmid).astype(LOW)


def branch_back_kernel(dbranch_ref, weight_ref, out_ref):
    out_ref[...] = product(dbranch_ref[...], weight_ref[0], NT).astype(LOW)


def last_kernel(block, x_ref, dmid_ref, norm_ref, weight_ref, *refs):
    grads, (out_ref, dnorm_ref) = refs[:-2], refs[-2:]
    mats = weight_ref.shape[0]
    gain = norm_ref[0:1, :]
    dnorm_ref[...] = jnp.zeros_like(dnorm_ref)

    @pl.loop(0, x_ref.shape[0] // block)
    def _(i):
        rows = pl.ds(pl.multiple_of(i * block, block), block)
        total, column = None, 0
        for first in range(0, len(grads), mats):
            wide = grads[first].shape[1]
            for j in range(mats):
                part = product(
                    grads[first + j][rows, :], weight_ref[j, :, column : column + wide], NT
                )
                total = part if total is None else total + part
            column += wide
        normed, inv_std = normalize(x_ref[rows, :].astype(F32))
        dnorm_ref[0:1, :] += jnp.sum(total * normed, 0, keepdims=True)
        dnorm_ref[1:2, :] += jnp.sum(total, 0, keepdims=True)
        out_ref[rows, :] = (
            dmid_ref[rows, :] + norm_back(total, normed, inv_std, gain)
        ).astype(LOW)


def weight_grad_kernel(pieces, per, table_ref, *refs):
    mats, lefts = len(pieces), sum(pieces)
    rights, outs, held_ref = refs[lefts : lefts + mats], refs[lefts + mats : -1], refs[-1]
    first = 0
    for j in range(mats):
        start = 0
        for left in refs[first : first + pieces[j]]:
            step = min(256, left.shape[1])
            for c in range(0, left.shape[1], step):
                held_ref[start : start + step, :] = product(
                    left[:, c : c + step], rights[j][...], TN
                ).astype(LOW)
                start += step
        first += pieces[j]
        column = 0
        for h in range(len(outs) // per):
            start = 0
            for ref in outs[h * per : (h + 1) * per]:
                number, _, rows, wide = ref.shape

                @pl.loop(0, number)
                def _(n, ref=ref, rows=rows, wide=wide, start=start, j=j, h=h, column=column):
                    row = pl.multiple_of(table_ref[h, start + n] * rows, rows)
                    ref[n, j] = held_ref[pl.ds(row, rows), column : column + wide]

                start += number
            column += wide


def weight_grads(table, lefts, rights, outs, per):
    mats = len(rights)
    pieces = [len(p) for p in lefts]
    length, wide = rights[0].shape
    width = sum(p.shape[1] for p in lefts[0])
    return pl.pallas_call(
        functools.partial(weight_grad_kernel, pieces, per),
        out_shape=[shape((n, mats, rows, w), LOW) for n, rows, w in outs],
        in_specs=[SMEM] + [VMEM] * (sum(pieces) + mats),
        out_specs=[VMEM] * len(outs),
        scratch_shapes=[pltpu.VMEM((width, wide), LOW)],
        compiler_params=params(48),
        cost_estimate=cost(2 * mats * length * width * wide, 4 * mats * width * wide),
    )(table, *[a for p in lefts for a in p], *rights)


def lamb_parts(weight, grad, first, second, sum_axes):
    m_one = beta_one * first + (1.0 - beta_one) * grad
    m_two = beta_two * second + (1.0 - beta_two) * grad * grad
    step_dir = (
        m_one
        / (1.0 - beta_one**adam_step)
        / (jnp.sqrt(m_two / (1.0 - beta_two**adam_step)) + adam_eps)
        + decay_rate * weight
    )
    return (
        m_one,
        m_two,
        step_dir,
        jnp.sum(weight * weight, axis=sum_axes),
        jnp.sum(step_dir * step_dir, axis=sum_axes),
    )


def on_device(
    latents,
    lengths,
    cotangent,
    matrices,
    norm_params,
    moment1_mat,
    moment2_mat,
    moment1_norm,
    moment2_norm,
):
    _, length, width = latents.shape
    dim = width // HEADS
    scale = 1.0 / math.sqrt(dim)
    power = scale * math.log2(math.e)
    dp, fsdp = lax.axis_size("dp"), lax.axis_size("fsdp")
    count = dp * fsdp
    rows = matrices.shape[1]
    index = lax.axis_index("dp") * fsdp + lax.axis_index("fsdp")
    ring = dp == 8 and fsdp == 4 and rows % 16 == 0
    inner, pair = fsdp, fsdp
    half_w = width // 2
    block = 256 if length % 256 == 0 else length
    low_mats = matrices.astype(LOW)
    low_norms = norm_params.astype(LOW)

    if ring:
        halves = [(0, half_w), (half_w, half_w)]
        quarter = half_w // 2
        firsts, seconds = (2 * fsdp, 4 * fsdp), (4 * fsdp, 2 * fsdp)
        in_parts = [[(0, half_w, 0)], [(half_w, quarter, 0), (half_w + quarter, quarter, 1)]]
        masks = jnp.array(
            [mask_order(o, inner, pair) for o in zip(firsts, seconds)], jnp.int32
        )
        table = jnp.bitwise_xor(masks, index.astype(jnp.int32))
        shards = [[low_mats[i : i + 3, :, c : c + w] for c, w in halves] for i in (0, 3)]
        start = [gather_near(s, inner, count) for s in shards[0]]
        taken = swap_all(start, firsts, count)
        shards[1] = after(shards[1], *start)
        later = [gather_near(s, inner, count) for s in shards[1]]
        start = grow(start, taken)
        taken = swap_all(start, seconds, count)
        start = grow(start, taken)
        later = after(later, *start)
        others = swap_all(start, [pair, pair], count)
        parts_in = [a for both in zip(start, others) for a in both]
        layout = tuple((2, c) for c, _ in halves)
        spread = lax.dynamic_update_slice(
            jnp.zeros((4, width), LOW), low_norms, (0, index * rows)
        )
        norms_low = hyper_sum(spread, count)
        grad_outs = [(count // 2, rows, half_w)] * 2
    else:
        weights = lax.all_gather(low_mats, AXES, axis=1, tiled=True)
        norms_low = lax.all_gather(low_norms, AXES, axis=1, tiled=True)
        table = jnp.zeros((1, 1), jnp.int32)
        parts_in, later = [weights[None, :3]], [weights[None, 3:]]
        layout = ((1, 0),)
    norm_vals = norms_low.astype(F32)

    ends = jnp.cumsum(lengths[0, :-1])
    sets = ends.shape[0]
    segment = jnp.sum(
        (jnp.arange(length, dtype=jnp.int32)[:, None] >= ends[None, :]).astype(jnp.int32), axis=1
    )
    live = (segment < sets).astype(F32)[:, None]
    lanes = jnp.arange(128, dtype=jnp.int32)[None, :]
    same = segment[:, None] == lanes
    mark_in = same.astype(LOW)
    mark_out = jnp.where(same | (lanes > sets), 0.0, mask_depth).astype(LOW)

    x, dz = latents[0], cotangent[0]
    if ring:
        taken = swap_all(later, firsts, count)
        x = after(x, *later)
    hidden_one, qkv, weights_in = pl.pallas_call(
        functools.partial(project_kernel, layout, block),
        out_shape=[
            shape((length, width), LOW),
            shape((length, 3 * width), LOW),
            shape((3, width, width), LOW),
        ],
        in_specs=[SMEM] + [VMEM] * (2 + len(parts_in)),
        out_specs=[VMEM] * 3,
        compiler_params=params(48),
        cost_estimate=cost(6 * length * width * width, 12 * width * width),
    )(table, x, norm_vals, *parts_in)
    x = latents[0]

    group = 2
    split = len(layout)
    part_heads = HEADS // split
    part_w = part_heads * dim
    whole = pl.BlockSpec((length, 128), lambda h: (0, 0))

    def heads_at(first):
        return pl.BlockSpec((length, dim * group), lambda h: (0, first // group + h))

    def sums_at(first):
        return pl.BlockSpec((group, 1, length), lambda h: (first // group + h, 0, 0))

    def attend(number, qkv):
        first = number * part_heads
        return pl.pallas_call(
            functools.partial(attend_kernel, group, dim, power),
            grid=(part_heads // group,),
            in_specs=[heads_at(first + i * HEADS) for i in range(3)] + [whole, whole],
            out_specs=[heads_at(0), sums_at(0)],
            out_shape=[shape((length, part_w), LOW), shape((part_heads, 1, length), F32)],
            compiler_params=params(48),
            cost_estimate=cost(8 * length * length * part_w, 8 * length * part_w),
        )(qkv, qkv, qkv, mark_in, mark_out)

    if ring:
        later = grow(later, after(taken, hidden_one))
        taken = swap_all(later, seconds, count)
        attended, log_sums = zip(*[attend(n, after(qkv, *later)) for n in range(split)])
        later = grow(later, after(taken, *attended))
        others = swap_all(later, [pair, pair], count)
        later = [a for both in zip(later, others) for a in both]
    else:
        attended, log_sums = zip(*[attend(n, qkv) for n in range(split)])

    (result, dmid, dmlp, hidden_two, dup, active, dbranch, dnorm_two, weights_out) = pl.pallas_call(
        functools.partial(middle_kernel, layout, block),
        out_shape=[
            shape((length, width), LOW),
            shape((length, width), F32),
            *[shape((length, width), LOW)] * 5,
            shape((2, width), F32),
            shape((3, width, width), LOW),
        ],
        in_specs=[SMEM] + [VMEM] * (4 + split + len(later)),
        out_specs=[VMEM] * 9,
        compiler_params=params(56),
        cost_estimate=cost(10 * length * width * width, 12 * width * width),
    )(table, x, dz, live, norm_vals, *attended, *later)

    def branch_back(dbranch):
        return pl.pallas_call(
            branch_back_kernel,
            out_shape=shape((length, width), LOW),
            in_specs=[VMEM] * 2,
            out_specs=VMEM,
            compiler_params=params(48),
            cost_estimate=cost(2 * length * width * width, 2 * width * width),
        )(dbranch, weights_out)

    def attend_back(number, dattended):
        first = number * part_heads
        return pl.pallas_call(
            functools.partial(attend_back_kernel, group, dim, power, scale, length),
            grid=(part_heads // group,),
            in_specs=[heads_at(first + i * HEADS) for i in range(3)]
            + [heads_at(first), heads_at(0), whole, whole, sums_at(0)],
            out_specs=[heads_at(0)] * 3,
            out_shape=[shape((length, part_w), LOW)] * 3,
            scratch_shapes=[pltpu.VMEM((group, dim, length), F32)],
            compiler_params=params(48),
            cost_estimate=cost(20 * length * length * part_w, 16 * length * part_w),
        )(qkv, qkv, qkv, dattended, attended[number], mark_in, mark_out, log_sums[number])

    def last(x, grads):
        return pl.pallas_call(
            functools.partial(last_kernel, block),
            out_shape=[shape((length, width), LOW), shape((2, width), F32)],
            in_specs=[VMEM] * (4 + len(grads)),
            out_specs=[VMEM] * 2,
            compiler_params=params(48),
            cost_estimate=cost(6 * length * width * width, 6 * width * width),
        )(x, dmid, norm_vals, weights_in, *grads)

    out_lefts, out_rights = [attended, [hidden_two], [active]], [dbranch, dup, dmlp]
    in_lefts = [[hidden_one]] * 3
    if ring:
        out_chunks = [(count // 2, rows, half_w)] * 4
        grads = weight_grads(table, out_lefts, out_rights, out_chunks, 2)
        taken = swap_all(grads[1::2], [pair] * 2, count)
        dattended = branch_back(after(dbranch, *grads))
        held = [k.astype(F32) for k in grads[::2]]
        held, sent = fold(held, after(taken, dattended))
        taken = swap_all(sent, seconds, count)

        found = attend_back(0, after(dattended, *sent))
        grads_in = list(found)
        grads = weight_grads(table[:1], in_lefts, found, [(count // 2, rows, half_w)] * 2, 2)
        taken_a = swap(grads[1], pair, count)
        held, sent = fold(held, after(taken, *grads))
        taken = swap_all(sent, firsts, count)

        found = attend_back(1, after(dattended, *sent, *grads))
        grads_in += found
        held = [h + t.astype(F32) for h, t in zip(held, after(taken, *found))]
        near = [near_sum(h, inner, count) for h in held]
        held_a, sent_a = fold([grads[0].astype(F32)], [after(taken_a, *found)])
        taken_a = swap_all(sent_a, seconds[:1], count)

        sizes = [(count // 2, rows, quarter)] * 4
        right = [after(f, *sent_a) for f in found]
        grads = weight_grads(table, in_lefts, right, sizes, 2)
        taken_b = swap_all(grads[1::2], [pair] * 2, count)
        held_a, sent_a = fold(held_a, after(taken_a, *grads))
        taken_a = swap_all(sent_a, firsts[:1], count)
        held_b, sent_b = fold([k.astype(F32) for k in grads[::2]], taken_b)
        taken_b = swap_all(sent_b, seconds, count)

        grad_latents, dnorm_one = last(after(x, *sent_b, *sent_a), grads_in)
        norms_local = jnp.concatenate([dnorm_one, dnorm_two], 0)
        grad_norms = hyper_sum(norms_local, count)
        held_a = [h + t.astype(F32) for h, t in zip(held_a, after(taken_a, grad_latents))]
        near_a = near_sum(held_a[0], inner, count)
        held_b, sent_b = fold(held_b, after(taken_b, grad_latents))
        taken_b = swap_all(sent_b, firsts, count)
        held_b = [h + t.astype(F32) for h, t in zip(held_b, taken_b)]
        near_b = [near_sum(h, inner, count) for h in held_b]
        grad_mats = jnp.concatenate(
            [
                jnp.concatenate([add_all(*p) for p in group_], -1)
                for group_ in ([near_a, *near_b], near)
            ],
            0,
        )
        grad_norms = lax.dynamic_slice(grad_norms, (0, index * rows), (4, rows))
    else:
        (out_grads,) = weight_grads(table, out_lefts, out_rights, [(1, width, width)], 1)
        grads_in = attend_back(0, branch_back(dbranch))
        (in_grads,) = weight_grads(table, in_lefts, grads_in, [(1, width, width)], 1)
        grad_latents, dnorm_one = last(x, grads_in)
        norms_local = jnp.concatenate([dnorm_one, dnorm_two], 0)
        mats_local = jnp.concatenate([in_grads[0], out_grads[0]], 0).astype(F32)
        grad_mats = lax.psum_scatter(mats_local, AXES, scatter_dimension=1, tiled=True)
        grad_norms = lax.psum_scatter(norms_local, AXES, scatter_dimension=1, tiled=True)

    m1_mat, m2_mat, dir_mat, wsq_mat, usq_mat = lamb_parts(
        matrices, grad_mats, moment1_mat, moment2_mat, (1, 2)
    )
    m1_norm, m2_norm, dir_norm, wsq_norm, usq_norm = lamb_parts(
        norm_params, grad_norms, moment1_norm, moment2_norm, (1,)
    )
    squares = jnp.stack(
        [jnp.concatenate([wsq_mat, wsq_norm]), jnp.concatenate([usq_mat, usq_norm])]
    )
    squares = hyper_sum(squares, count) if ring else lax.psum(squares, AXES)
    ratios = jnp.sqrt(squares[0]) / jnp.sqrt(squares[1])
    scaled_mats = ratios[:6][:, None, None] * dir_mat
    scaled_norms = ratios[6:][:, None] * dir_norm
    return (
        result[None],
        grad_latents[None],
        grad_mats,
        grad_norms,
        scaled_mats,
        scaled_norms,
        m1_mat,
        m2_mat,
        m1_norm,
        m2_norm,
        ratios,
    )


def solution(mesh):
    return jax.shard_map(
        on_device,
        mesh=mesh,
        in_specs=(
            P(("dp", "fsdp"), None, None),
            P(("dp", "fsdp"), None),
            P(("dp", "fsdp"), None, None),
            P(None, ("dp", "fsdp"), None),
            P(None, ("dp", "fsdp")),
            P(None, ("dp", "fsdp"), None),
            P(None, ("dp", "fsdp"), None),
            P(None, ("dp", "fsdp")),
            P(None, ("dp", "fsdp")),
        ),
        out_specs=(
            P(("dp", "fsdp"), None, None),
            P(("dp", "fsdp"), None, None),
            P(None, ("dp", "fsdp"), None),
            P(None, ("dp", "fsdp")),
            P(None, ("dp", "fsdp"), None),
            P(None, ("dp", "fsdp")),
            P(None, ("dp", "fsdp"), None),
            P(None, ("dp", "fsdp"), None),
            P(None, ("dp", "fsdp")),
            P(None, ("dp", "fsdp")),
            P(),
        ),
        check_vma=False,
    )
```

```python
import functools
import math

import jax
import jax.numpy as jnp
from jax import lax
from jax.experimental import pallas as pl
from jax.experimental.pallas import tpu as pltpu
from jax.sharding import PartitionSpec as P

HEADS = 8
AXES = ("dp", "fsdp")
LANES = 128

ln_eps = 1e-05
beta_one = 0.9
beta_two = 0.999
adam_eps = 1e-06
decay_rate = 0.01
adam_step = 100.0
gelu_coef = 0.7978845608
cubic_coef = 0.044715
mask_depth = -1e30

F32 = jnp.float32
LOW = jnp.bfloat16
NT = (((1,), (1,)), ((), ()))
TN = (((0,), (0,)), ((), ()))
SMEM = pl.BlockSpec(memory_space=pltpu.SMEM)
VMEM = pl.BlockSpec(memory_space=pltpu.VMEM)


def params(mib):
    return pltpu.CompilerParams(vmem_limit_bytes=mib * 2**20)


def shape(dims, kind):
    return jax.ShapeDtypeStruct(dims, kind)


def product(left, right, dims=(((1,), (0,)), ((), ()))):
    return lax.dot_general(left, right, dims, preferred_element_type=F32)


def cost(flops, moved):
    return pl.CostEstimate(flops=int(flops), bytes_accessed=int(moved), transcendentals=0)


def whole(array):
    return pl.BlockSpec(
        array.shape, lambda i: (0,) * len(array.shape), pipeline_mode=pl.Buffered(1)
    )


def rows_of(array, block):
    lead = array.shape[:-2]
    return pl.BlockSpec((*lead, block, array.shape[-1]), lambda i: (*(0,) * len(lead), i, 0))


def swap(value, mask, count):
    return lax.ppermute(value, AXES, [(i, i ^ mask) for i in range(count)])


def swap_all(values, bits, count):
    return [swap(v, b, count) for v, b in zip(values, bits)]


def hyper_sum(value, count):
    mask = 1
    while mask < count:
        value = value + swap(value, mask, count)
        mask *= 2
    return value


def after(value, *others):
    return lax.optimization_barrier((value, others))[0]


def mask_order(order, inner):
    masks = list(range(inner))
    for bit in order:
        masks = masks + [m ^ bit for m in masks]
    return masks


def by_columns(shards, parts):
    mats, rows, columns = shards.shape
    blocks = columns // parts // LANES
    split = shards.reshape(mats, rows, parts, blocks, LANES)
    return split.transpose(2, 0, 3, 1, 4).reshape(parts, mats * blocks * rows, LANES)


def normalize(value):
    centered = value - jnp.mean(value, -1, keepdims=True)
    inv_std = lax.rsqrt(jnp.mean(centered * centered, -1, keepdims=True) + ln_eps)
    return centered * inv_std, inv_std


def norm_back(grad_out, normed, inv_std, gain):
    grad_normed = grad_out * gain
    return inv_std * (
        grad_normed
        - jnp.mean(grad_normed, -1, keepdims=True)
        - normed * jnp.mean(grad_normed * normed, -1, keepdims=True)
    )


def place_all(table_ref, layout, rows, refs, out_ref):
    mats = out_ref.shape[0]
    for (line, start, column, blocks), ref in zip(layout, refs):

        @pl.loop(0, ref.shape[0])
        def _(n, line=line, start=start, column=column, blocks=blocks, ref=ref):
            row = pl.multiple_of(table_ref[line, start + n] * rows, rows)
            for j in range(mats):
                for b in range(blocks):
                    first = (j * blocks + b) * rows
                    lane = column + b * LANES
                    out_ref[j, pl.ds(row, rows), lane : lane + LANES] = ref[
                        n, first : first + rows, :
                    ]


def lane_rows(low, first, number):
    lane = lax.broadcasted_iota(jnp.int32, low, 1)
    return (lane >= first) & (lane < first + number)


def spread_norms(table_ref, layout, first_row, refs, held_ref, norm_ref):
    for (line, start, _, _), ref in zip(layout, refs):
        if line == 0:

            @pl.loop(0, ref.shape[0])
            def _(n, line=line, start=start, ref=ref):
                held_ref[pl.ds(table_ref[line, start + n], 1), :] = ref[
                    n, first_row : first_row + 16, :
                ].astype(F32)[0:1]

    near = LANES // 32
    blocks = held_ref.shape[0] // near
    for i in range(4):
        total = jnp.zeros((blocks, LANES), F32)
        for z in range(near):
            value = held_ref[pl.ds(z, blocks, stride=near), :]
            value = pltpu.roll(value, (32 * (z - i)) % LANES, 1)
            total = total + jnp.where(lane_rows(total.shape, 32 * z, 32), value, 0.0)
        for b in range(blocks):
            norm_ref[i : i + 1, b * LANES : (b + 1) * LANES] = total[b : b + 1]


def pack_norms(norms, held_ref):
    near = LANES // 32
    blocks = held_ref.shape[0] // near
    held = [jnp.zeros((blocks, LANES), F32) for _ in range(near)]
    for i, norm in enumerate(norms):
        stacked = jnp.concatenate(
            [norm[:, b * LANES : (b + 1) * LANES] for b in range(blocks)], 0
        )
        for z in range(near):
            value = pltpu.roll(stacked, (32 * (i - z)) % LANES, 1)
            held[z] = held[z] + jnp.where(lane_rows(value.shape, 32 * i, 32), value, 0.0)
    for z in range(near):
        held_ref[pl.ds(z, blocks, stride=near), :] = held[z]


def project_kernel(layout, rows, norm_row, parts, table_ref, x_ref, *refs):
    chunks = refs[:parts]
    hidden_ref, out_ref, norm_ref, weight_ref, held_ref = refs[-5:]
    mats, width, _ = weight_ref.shape

    @pl.when(pl.program_id(0) == 0)
    def _():
        place_all(table_ref, layout, rows, chunks, weight_ref)
        if norm_row is None:
            norm_ref[...] = refs[parts][...]
        else:
            spread_norms(table_ref, layout, norm_row, chunks, held_ref, norm_ref)

    normed, _ = normalize(x_ref[...].astype(F32))
    hidden = (normed * norm_ref[0:1, :] + norm_ref[1:2, :]).astype(LOW)
    hidden_ref[...] = hidden
    for j in range(mats):
        out_ref[:, j * width : (j + 1) * width] = product(hidden, weight_ref[j]).astype(LOW)


def attend_kernel(group, dim, power, q_ref, k_ref, v_ref, in_ref, out_ref, o_ref, lse_ref):
    for g in range(group):
        span = slice(g * dim, (g + 1) * dim)
        keys = jnp.concatenate([k_ref[:, span], out_ref[...]], 1)
        queries = jnp.concatenate([q_ref[:, span], in_ref[...]], 1)
        scores = product(keys, queries, NT)
        top = jnp.max(scores, 0, keepdims=True)
        weight = jnp.exp2((scores - top) * power)
        total = jnp.sum(weight, 0, keepdims=True)
        probs = (weight * (1.0 / total)).astype(LOW)
        o_ref[:, span] = product(v_ref[:, span].T, probs).T.astype(LOW)
        lse_ref[g] = top * power + jnp.log2(total)


def attend_back_kernel(
    group, dim, power, scale,
    q_ref, k_ref, v_ref, do_ref, o_ref, in_ref, out_ref, lse_ref,
    grad_ref,
):
    for g in range(group):
        span = slice(g * dim, (g + 1) * dim)
        queries, keys, grad = q_ref[:, span], k_ref[:, span], do_ref[:, span]
        both = grad.astype(F32) * o_ref[:, span].astype(F32)
        row_dot = lax.dot_general(
            jnp.ones((8, dim), F32), both, NT,
            preferred_element_type=F32, precision=lax.Precision.HIGHEST,
        )[0:1]
        scores = product(
            jnp.concatenate([keys, out_ref[...]], 1),
            jnp.concatenate([queries, in_ref[...]], 1),
            NT,
        )
        probs = jnp.exp2(scores * power - lse_ref[g])
        grad_probs = product(v_ref[:, span], grad, NT)
        grad_scores = (probs * (grad_probs - row_dot)).astype(LOW)
        grad_ref[2, :, span] = product(probs.astype(LOW), grad).astype(LOW)
        grad_ref[1, :, span] = (product(grad_scores, queries) * scale).astype(LOW)
        grad_ref[0, :, span] = (product(keys.T, grad_scores).T * scale).astype(LOW)


def middle_kernel(layout, rows, atts, table_ref, x_ref, dz_ref, live_ref, norm_ref, *refs):
    att_refs, chunks = refs[:atts], refs[atts:-10]
    dnorm_ref, result_ref, dmid_ref, dmlp_ref, hidden_ref = refs[-10:-5]
    dup_ref, act_ref, dbranch_ref, datt_ref, weight_ref = refs[-5:]

    @pl.when(pl.program_id(0) == 0)
    def _():
        place_all(table_ref, layout, rows, chunks, weight_ref)
        dnorm_ref[...] = jnp.zeros_like(dnorm_ref)

    gain, shift = norm_ref[2:3, :], norm_ref[3:4, :]
    live = live_ref[...]
    branch, first = None, 0
    for ref in att_refs:
        part = product(ref[...], weight_ref[0, first : first + ref.shape[1], :])
        branch = part if branch is None else branch + part
        first += ref.shape[1]
    middle = x_ref[...].astype(F32) + live * branch
    normed, inv_std = normalize(middle)
    hidden = (normed * gain + shift).astype(LOW)
    hidden_ref[...] = hidden
    upward = product(hidden, weight_ref[1])
    square = upward * upward
    bend = jnp.tanh(gelu_coef * (upward + cubic_coef * square * upward))
    half = 0.5 * (1.0 + bend)
    active = (upward * half).astype(LOW)
    act_ref[...] = active
    slope = half + (0.5 * gelu_coef) * upward * (1.0 - bend * bend) * (
        1.0 + (3.0 * cubic_coef) * square
    )
    result_ref[...] = (middle + live * product(active, weight_ref[2])).astype(LOW)
    grad = dz_ref[...].astype(F32)
    dmlp = (live * grad).astype(LOW)
    dmlp_ref[...] = dmlp
    dup = (product(dmlp, weight_ref[2], NT) * slope).astype(LOW)
    dup_ref[...] = dup
    dhidden = product(dup, weight_ref[1], NT)
    dnorm_ref[0:1, :] += jnp.sum(dhidden * normed, 0, keepdims=True)
    dnorm_ref[1:2, :] += jnp.sum(dhidden, 0, keepdims=True)
    dmid = grad + norm_back(dhidden, normed, inv_std, gain)
    dmid_ref[...] = dmid
    dbranch = (live * dmid).astype(LOW)
    dbranch_ref[...] = dbranch
    datt_ref[...] = product(dbranch, weight_ref[0], NT).astype(LOW)


def last_kernel(layout, rows, parts, table_ref, x_ref, dmid_ref, norm_ref, *refs):
    chunks, grads = refs[:parts], refs[parts:-3]
    out_ref, dnorm_ref, weight_ref = refs[-3:]
    mats = weight_ref.shape[0]

    @pl.when(pl.program_id(0) == 0)
    def _():
        place_all(table_ref, layout, rows, chunks, weight_ref)
        dnorm_ref[...] = jnp.zeros_like(dnorm_ref)

    total, column = None, 0
    for ref in grads:
        wide = ref.shape[2]
        for j in range(mats):
            part = product(ref[j], weight_ref[j, :, column : column + wide], NT)
            total = part if total is None else total + part
        column += wide
    normed, inv_std = normalize(x_ref[...].astype(F32))
    dnorm_ref[0:1, :] += jnp.sum(total * normed, 0, keepdims=True)
    dnorm_ref[1:2, :] += jnp.sum(total, 0, keepdims=True)
    out_ref[...] = (
        dmid_ref[...] + norm_back(total, normed, inv_std, norm_ref[0:1, :])
    ).astype(LOW)


def weight_grad_kernel(pieces, rights, norms, rows, table_ref, *refs):
    lefts = refs[: sum(pieces)]
    right_refs = refs[len(lefts) : len(lefts) + len(rights)]
    norm_refs = refs[len(lefts) + len(rights) : len(lefts) + len(rights) + norms]
    outs, (held_ref, pack_ref) = refs[len(lefts) + len(rights) + norms : -2], refs[-2:]
    mats = len(pieces)
    parts = outs[0].shape[0]
    blocks = held_ref.shape[1] // LANES // parts
    first = 0
    for j in range(mats):
        start = 0
        for left in lefts[first : first + pieces[j]]:
            step = min(256, left.shape[1])
            for c in range(0, left.shape[1], step):
                column = 0
                for (mat, entry), ref in zip(rights, right_refs):
                    if mat == j or mat is None:
                        right = ref[...] if entry is None else ref[j]
                        wide = right.shape[1]
                        held_ref[start : start + step, column : column + wide] = product(
                            left[:, c : c + step], right, TN
                        ).astype(LOW)
                        column += wide
                start += step
        first += pieces[j]
        for h in range(parts):
            for side, ref in enumerate(outs):
                number = ref.shape[1]

                @pl.loop(0, number)
                def _(n, ref=ref, side=side, number=number, j=j, h=h):
                    row = pl.multiple_of(table_ref[h, side * number + n] * rows, rows)
                    for b in range(blocks):
                        lane = (h * blocks + b) * LANES
                        at = (j * blocks + b) * rows
                        ref[h, n, at : at + rows, :] = held_ref[
                            pl.ds(row, rows), lane : lane + LANES
                        ]

    if norms:
        pack_norms(
            [ref[i : i + 1, :] for ref in norm_refs for i in range(ref.shape[0])], pack_ref
        )
        at = mats * blocks * rows
        for h in range(parts):
            for side, ref in enumerate(outs):
                number = ref.shape[1]

                @pl.loop(0, number)
                def _(n, ref=ref, side=side, number=number, h=h):
                    row = pack_ref[pl.ds(table_ref[h, side * number + n], 1), :]
                    ref[h, n, at : at + 16, :] = jnp.broadcast_to(row, (16, LANES)).astype(LOW)


def weight_grads(table, lefts, rights, norms, rows, chunks, parts, sides):
    mats = len(lefts)
    pieces = [len(p) for p in lefts]
    flat = [a for p in lefts for a in p]
    length = flat[0].shape[0]
    width = sum(p.shape[1] for p in lefts[0])
    wide = sum(a.shape[-1] for m, _, a in rights if m in (0, None))
    size = mats * wide // parts // LANES * rows + (16 if norms else 0)
    return pl.pallas_call(
        functools.partial(
            weight_grad_kernel, pieces, [r[:2] for r in rights], len(norms), rows
        ),
        out_shape=[shape((parts, chunks // sides, size, LANES), LOW)] * sides,
        in_specs=[SMEM] + [VMEM] * (len(flat) + len(rights) + len(norms)),
        out_specs=[VMEM] * sides,
        scratch_shapes=[pltpu.VMEM((width, wide), LOW), pltpu.VMEM((32, LANES), F32)],
        compiler_params=params(28),
        cost_estimate=cost(2 * mats * length * width * wide, 4 * mats * width * wide),
    )(table, *flat, *[a for _, _, a in rights], *norms)


def sum_kernel(plans, *refs):
    ins, outs = refs[: -len(plans)], refs[-len(plans) :]
    for plan, out in zip(plans, outs):
        for at, terms in plan:
            total = None
            for number, entry in terms:
                value = ins[number][entry].astype(F32)
                total = value if total is None else total + value
            out[at] = total.astype(out.dtype)


def stage_sums(inputs, plans, outs):
    return pl.pallas_call(
        functools.partial(sum_kernel, plans),
        out_shape=outs,
        in_specs=[VMEM] * len(inputs),
        out_specs=[VMEM] * len(outs),
        compiler_params=params(24),
        cost_estimate=cost(0, 2**22),
    )(*inputs)


def far_sums(keep, taken, earlier):
    parts, chunks, size, _ = keep.shape
    half = chunks // 2 ** (len(earlier) + 1)
    plans = [
        [
            (n, [(0, (h, half + n)), (1, (h, half + n))]
             + [(2 + parts * e + h, half + n) for e in range(len(earlier))])
            for n in range(half)
        ]
        for h in range(parts)
    ]
    outs = [shape((half, size, LANES), LOW)] * parts
    return stage_sums([keep, taken, *[t for e in earlier for t in e]], plans, outs)


def near_sums(keep, taken, earlier, inner):
    parts, _, size, _ = keep.shape
    plans = [
        [
            (h, [(0, (h, k)), (1, (h, k))] + [(2 + parts * e + h, k) for e in range(len(earlier))])
            for h in range(parts)
        ]
        for k in range(inner)
    ]
    outs = [shape((parts, size, LANES), F32 if k == 0 else LOW) for k in range(inner)]
    return stage_sums([keep, taken, *[t for e in earlier for t in e]], plans, outs)


def lamb_values(weight, grad, first, second):
    m_one = beta_one * first + (1.0 - beta_one) * grad
    m_two = beta_two * second + (1.0 - beta_two) * grad * grad
    step_dir = (
        m_one
        / (1.0 - beta_one**adam_step)
        / (jnp.sqrt(m_two / (1.0 - beta_two**adam_step)) + adam_eps)
        + decay_rate * weight
    )
    return m_one, m_two, step_dir


def whole_sum(value):
    return jnp.sum(jnp.sum(value, 0, keepdims=True), 1, keepdims=True)


def lamb_kernel(first, parts, terms, norm_ends, prior, *refs):
    weight_ref, one_ref, two_ref = refs[:3]
    norm_refs = refs[3:6] if norm_ends else ()
    base = 3 + len(norm_refs)
    term_refs = refs[base : base + terms]
    prior_refs = refs[base + terms : base + terms + prior]
    outs = refs[base + terms + prior :]
    mats, rows = 3, weight_ref.shape[1]
    lane = lax.broadcasted_iota(jnp.int32, (8, LANES), 1)
    line = lax.broadcasted_iota(jnp.int32, (8, LANES), 0)
    squares = jnp.zeros((8, LANES), F32)
    weight_sq = [jnp.zeros((1, LANES), F32)] * mats
    update_sq = [jnp.zeros((1, LANES), F32)] * mats
    for column, blocks, used, entry in parts:
        for j in range(mats):
            for b in range(blocks):
                at = (j * blocks + b) * rows
                grad = None
                for t in used:
                    value = term_refs[t][entry, at : at + rows, :].astype(F32)
                    grad = value if grad is None else grad + value
                span = slice(column + b * LANES, column + (b + 1) * LANES)
                weight = weight_ref[first + j, :, span]
                m_one, m_two, step = lamb_values(
                    weight, grad, one_ref[first + j, :, span], two_ref[first + j, :, span]
                )
                for ref, value in zip(outs, (grad, m_one, m_two, step)):
                    ref[j, :, span] = value
                weight_sq[j] += jnp.sum(weight * weight, 0, keepdims=True)
                update_sq[j] += jnp.sum(step * step, 0, keepdims=True)
    for j in range(mats):
        spot = lane == first + j
        squares += jnp.where(spot & (line == 0), jnp.sum(weight_sq[j], 1, keepdims=True), 0.0)
        squares += jnp.where(spot & (line == 1), jnp.sum(update_sq[j], 1, keepdims=True), 0.0)
    if prior:
        for ref, old in zip(outs[:4], prior_refs[:4]):
            ref[mats:] = old[...]
        squares += prior_refs[4][...]
    if norm_ends:
        used, entry, at = norm_ends
        row = None
        for t in used:
            value = term_refs[t][entry, at : at + 16, :].astype(F32)[0:1]
            row = value if row is None else row + value
        for i in range(4):
            span = slice(i * rows, (i + 1) * rows)
            weight = norm_refs[0][i : i + 1, :]
            grad = row[:, span]
            m_one, m_two, step = lamb_values(
                weight, grad, norm_refs[1][i : i + 1, :], norm_refs[2][i : i + 1, :]
            )
            for ref, value in zip(outs[5:], (grad, m_one, m_two, step)):
                ref[i : i + 1, :] = value
            spot = lane == 6 + i
            squares += jnp.where(spot & (line == 0), whole_sum(weight * weight), 0.0)
            squares += jnp.where(spot & (line == 1), whole_sum(step * step), 0.0)
    outs[4][...] = squares


def lamb_call(first, parts, terms, state, norm_state, norm_ends, prior):
    mats, rows, width = state[0].shape
    outs = [shape((mats if prior else 3, rows, width), F32)] * 4 + [shape((8, LANES), F32)]
    if norm_ends:
        outs += [shape(norm_state[0].shape, F32)] * 4
    inputs = [*state, *norm_state, *terms, *prior]
    return pl.pallas_call(
        functools.partial(lamb_kernel, first, parts, len(terms), norm_ends, len(prior)),
        out_shape=outs,
        in_specs=[VMEM] * len(inputs),
        out_specs=[VMEM] * len(outs),
        compiler_params=params(24),
        cost_estimate=cost(0, 2**22),
    )(*inputs)


def on_device(
    latents,
    lengths,
    cotangent,
    matrices,
    norm_params,
    moment1_mat,
    moment2_mat,
    moment1_norm,
    moment2_norm,
):
    _, length, width = latents.shape
    dim = width // HEADS
    scale = 1.0 / math.sqrt(dim)
    power = scale * math.log2(math.e)
    dp, fsdp = lax.axis_size("dp"), lax.axis_size("fsdp")
    count = dp * fsdp
    rows = matrices.shape[1]
    index = lax.axis_index("dp") * fsdp + lax.axis_index("fsdp")
    ring = dp == 8 and fsdp == 4 and rows == 32
    inner, pair = fsdp, fsdp
    block = 256 if length % 256 == 0 else length
    low_mats = matrices.astype(LOW)
    low_norms = norm_params.astype(LOW)

    if ring:
        firsts, seconds = (2 * fsdp, 4 * fsdp), (4 * fsdp, 2 * fsdp)
        half_blocks = width // 2 // LANES
        norm_row = 3 * half_blocks * rows
        masks = jnp.array(
            [
                [m ^ side for side in (0, pair) for m in mask_order(o, inner)]
                for o in zip(firsts, seconds)
            ],
            jnp.int32,
        )
        table = jnp.bitwise_xor(masks, index.astype(jnp.int32))
        norm_rows = jnp.pad(low_norms.reshape(1, 1, 4 * rows), ((0, 1), (0, 15), (0, 0)))
        shards = [
            jnp.concatenate([by_columns(low_mats[:3], 2), norm_rows], 1),
            by_columns(low_mats[3:], 2),
        ]
        quarter = count // 4
        layout = tuple(
            (h, side * count // 2 + part * quarter, h * width // 2, half_blocks)
            for h in range(2)
            for side in range(2)
            for part in range(2)
        )

        def near_of(shard):
            return [shard] + [swap(shard, k, count) for k in range(1, inner)]

        def halves_of(near):
            return [jnp.stack([n[h] for n in near]) for h in range(2)]

        def grow(held, taken):
            return [jnp.concatenate(both) for both in zip(held, taken)]

        def with_pairs(held, taken, early):
            late = swap_all(taken, [pair, pair], count)
            return [a for h in range(2) for a in (held[h], taken[h], early[h], late[h])]

        near = near_of(shards[0])
        held = halves_of(near)
        taken = swap_all(held, firsts, count)
        later = near_of(after(shards[1], *held))
        held = grow(held, taken)
        taken = swap_all(held, seconds, count)
        early = swap_all(held, [pair, pair], count)
        later = halves_of(after(later, *held))
        parts_in = with_pairs(held, taken, early)
        norm_vals = []
    else:
        weights = lax.all_gather(low_mats, AXES, axis=1, tiled=True)
        norm_vals = [lax.all_gather(low_norms, AXES, axis=1, tiled=True).astype(F32)]
        table = jnp.zeros((1, 1), jnp.int32)
        rows = width
        parts_in, parts_out = by_columns(weights[:3], 1), by_columns(weights[3:], 1)
        parts_in, parts_out = [parts_in], [parts_out]
        layout = ((0, 0, 0, width // LANES),)
        norm_row = None

    ends = jnp.cumsum(lengths[0, :-1])
    sets = ends.shape[0]
    segment = jnp.sum(
        (jnp.arange(length, dtype=jnp.int32)[:, None] >= ends[None, :]).astype(jnp.int32), axis=1
    )
    live = (segment < sets).astype(F32)[:, None]
    lanes = jnp.arange(LANES, dtype=jnp.int32)[None, :]
    same = segment[:, None] == lanes
    mark_in = same.astype(LOW)
    mark_out = jnp.where(same | (lanes > sets), 0.0, mask_depth).astype(LOW)

    x, dz = latents[0], cotangent[0]
    steps = (length // block,)
    if ring:
        taken = swap_all(later, firsts, count)
        x = after(x, *later)
    held_rows = pl.BlockSpec((4, width), lambda i: (0, 0))
    two_rows = pl.BlockSpec((2, width), lambda i: (0, 0))
    weight_scratch = pltpu.VMEM((3, width, width), LOW)
    hidden_one, qkv, norm_vals = pl.pallas_call(
        functools.partial(project_kernel, layout, rows, norm_row, len(parts_in)),
        grid=steps,
        out_shape=[
            shape((length, width), LOW),
            shape((length, 3 * width), LOW),
            shape((4, width), F32),
        ],
        in_specs=[SMEM, rows_of(x, block)]
        + [whole(a) for a in parts_in]
        + [held_rows] * len(norm_vals),
        out_specs=[
            pl.BlockSpec((block, width), lambda i: (i, 0)),
            pl.BlockSpec((block, 3 * width), lambda i: (i, 0)),
            held_rows,
        ],
        scratch_shapes=[weight_scratch, pltpu.VMEM((32, LANES), F32)],
        compiler_params=params(28),
        cost_estimate=cost(6 * length * width * width, 12 * width * width),
    )(table, x, *parts_in, *norm_vals)
    x = latents[0]

    group = 2
    marks = [pl.BlockSpec((length, LANES), lambda h: (0, 0))] * 2

    def heads_at(first):
        return pl.BlockSpec((length, dim * group), lambda h: (0, first // group + h))

    def sums_at(first):
        return pl.BlockSpec((group, 1, length), lambda h: (first // group + h, 0, 0))

    def attend(first, number, qkv):
        return pl.pallas_call(
            functools.partial(attend_kernel, group, dim, power),
            grid=(number // group,),
            in_specs=[heads_at(first + i * HEADS) for i in range(3)] + marks,
            out_specs=[heads_at(0), sums_at(0)],
            out_shape=[shape((length, number * dim), LOW), shape((number, 1, length), F32)],
            compiler_params=params(28),
            cost_estimate=cost(8 * length * length * number * dim, 8 * length * number * dim),
        )(qkv, qkv, qkv, mark_in, mark_out)

    ahead = HEADS // 2
    if ring:
        later = grow(later, after(taken, hidden_one))
        taken = swap_all(later, seconds, count)
        early = swap_all(later, [pair, pair], count)
        attended, log_sums = zip(*[attend(f, ahead, after(qkv, *later)) for f in (0, ahead)])
        taken = after(taken, *attended)
        parts_out = with_pairs(later, taken, early)
    else:
        attended, log_sums = zip(*[attend(f, ahead, qkv) for f in (0, ahead)])

    row_block = pl.BlockSpec((block, width), lambda i: (i, 0))
    (dnorm_two, result, dmid, dmlp, hidden_two, dup, active, dbranch, dattended) = pl.pallas_call(
        functools.partial(middle_kernel, layout, rows, len(attended)),
        grid=steps,
        out_shape=[
            shape((2, width), F32),
            shape((length, width), LOW),
            shape((length, width), F32),
            *[shape((length, width), LOW)] * 6,
        ],
        in_specs=[SMEM, row_block, row_block, rows_of(live, block), held_rows]
        + [rows_of(a, block) for a in attended]
        + [whole(a) for a in parts_out],
        out_specs=[two_rows] + [row_block] * 8,
        scratch_shapes=[weight_scratch],
        compiler_params=params(36),
        cost_estimate=cost(12 * length * width * width, 12 * width * width),
    )(table, x, dz, live, norm_vals, *attended, *parts_out)

    def attend_back(first, number, dattended):
        side = first // ahead
        inside = first - side * ahead
        return pl.pallas_call(
            functools.partial(attend_back_kernel, group, dim, power, scale),
            grid=(number // group,),
            in_specs=[heads_at(first + i * HEADS) for i in range(3)]
            + [heads_at(first), heads_at(inside), *marks, sums_at(inside)],
            out_specs=pl.BlockSpec((3, length, dim * group), lambda h: (0, 0, h)),
            out_shape=shape((3, length, number * dim), LOW),
            compiler_params=params(28),
            cost_estimate=cost(20 * length * length * number * dim, 16 * length * number * dim),
        )(qkv, qkv, qkv, dattended, attended[side], mark_in, mark_out, log_sums[side])

    def last(dmid, grads):
        return pl.pallas_call(
            functools.partial(last_kernel, layout, rows, len(parts_in)),
            grid=steps,
            out_shape=[shape((length, width), LOW), shape((2, width), F32)],
            in_specs=[SMEM, row_block, row_block, held_rows]
            + [whole(a) for a in parts_in]
            + [rows_of(g, block) for g in grads],
            out_specs=[row_block, two_rows],
            scratch_shapes=[weight_scratch],
            compiler_params=params(36),
            cost_estimate=cost(6 * length * width * width, 6 * width * width),
        )(table, x, dmid, norm_vals, *parts_in, *grads)

    out_lefts = [list(attended), [hidden_two], [active]]
    out_rights = [(0, None, dbranch), (1, None, dup), (2, None, dmlp)]
    in_lefts = [[hidden_one]] * 3
    state, norm_state = (matrices, moment1_mat, moment2_mat), (norm_params, moment1_norm, moment2_norm)
    if ring:
        keep, send = weight_grads(table, out_lefts, out_rights, [], rows, count, 2, 2)
        taken = swap(send, pair, count)
        grads = [attend_back(0, 2, after(dattended, keep))]
        grads.append(attend_back(2, 2, after(dattended, grads[0])))
        sums = far_sums(keep, after(taken, grads[1]), [])
        far_one = swap_all(sums, seconds, count)
        grads.append(attend_back(4, 2, after(dattended, *sums)))
        keep_a, send_a = weight_grads(
            table, in_lefts, [(None, 0, g) for g in grads], [], rows, count, 2, 2
        )
        taken_a = swap(send_a, pair, count)
        grads.append(attend_back(6, 2, after(dattended, keep_a)))
        sums_a = far_sums(keep_a, after(taken_a, grads[3]), [])
        far_one_a = swap_all(sums_a, seconds, count)
        sums = far_sums(keep, taken, [after(far_one, *sums_a)])
        far_two = swap_all(sums, firsts, count)
        grad_latents, dnorm_one = last(after(dmid, *sums), grads)
        keep_b, send_b = weight_grads(
            table,
            in_lefts,
            [(None, 0, grads[3])],
            [dnorm_one, dnorm_two],
            rows,
            count,
            2,
            2,
        )
        taken_b = swap(send_b, pair, count)
        sums_a = far_sums(keep_a, taken_a, [after(far_one_a, keep_b)])
        far_two_a = swap_all(sums_a, firsts, count)
        near = near_sums(keep, taken, [far_one, after(far_two, *sums_a)], inner)
        sums_b = far_sums(keep_b, after(taken_b, *near), [])
        far_one_b = swap_all(sums_b, seconds, count)
        near = [near[0]] + swap_all(near[1:], range(1, inner), count)
        near_a = near_sums(keep_a, taken_a, [far_one_a, after(far_two_a, *sums_b)], inner)
        near_a = [near_a[0]] + swap_all(near_a[1:], range(1, inner), count)
        sums_b = far_sums(keep_b, taken_b, [after(far_one_b, near_a[0])])
        far_two_b = swap_all(sums_b, firsts, count)
        parts = [(h * width // 2, half_blocks, range(inner), h) for h in range(2)]
        prior = lamb_call(3, parts, after(near, *sums_b), state, (), None, ())
        near_b = near_sums(keep_b, taken_b, [far_one_b, after(far_two_b, prior[4])], inner)
        near_b = [near_b[0]] + swap_all(near_b[1:], range(1, inner), count)
        a_blocks, b_blocks = 3 * group * dim // 2 // LANES, group * dim // 2 // LANES
        parts = [(h * a_blocks * LANES, a_blocks, range(inner), h) for h in range(2)] + [
            ((2 * a_blocks + h * b_blocks) * LANES, b_blocks, range(inner, 2 * inner), h)
            for h in range(2)
        ]
        norm_ends = (range(inner, 2 * inner), 0, 3 * b_blocks * rows)
        found = lamb_call(0, parts, [*near_a, *near_b], state, norm_state, norm_ends, prior)
        grad_mats, m1_mat, m2_mat, dir_mat, squares, grad_norms, m1_norm, m2_norm, dir_norm = found
        squares = hyper_sum(squares, count)[:2, :10]
    else:
        (out_grads,) = weight_grads(table, out_lefts, out_rights, [], rows, 1, 1, 1)
        grads = [attend_back(f, ahead, dattended) for f in (0, ahead)]
        (in_grads,) = weight_grads(
            table, in_lefts, [(None, 0, g) for g in grads], [], rows, 1, 1, 1
        )
        grad_latents, dnorm_one = last(dmid, grads)
        norms_local = jnp.concatenate([dnorm_one, dnorm_two], 0)
        mats_local = jnp.concatenate([in_grads[0, 0], out_grads[0, 0]], 0).astype(F32)
        mats_local = mats_local.reshape(6, width // LANES, width, LANES)
        mats_local = mats_local.transpose(0, 2, 1, 3).reshape(6, width, width)
        grad_mats = lax.psum_scatter(mats_local, AXES, scatter_dimension=1, tiled=True)
        grad_norms = lax.psum_scatter(norms_local, AXES, scatter_dimension=1, tiled=True)
        m1_mat, m2_mat, dir_mat = lamb_values(matrices, grad_mats, moment1_mat, moment2_mat)
        m1_norm, m2_norm, dir_norm = lamb_values(norm_params, grad_norms, moment1_norm, moment2_norm)
        squares = jnp.stack(
            [
                jnp.concatenate([jnp.sum(m * m, (1, 2)), jnp.sum(n * n, 1)])
                for m, n in ((matrices, norm_params), (dir_mat, dir_norm))
            ]
        )
        squares = lax.psum(squares, AXES)
    ratios = jnp.sqrt(squares[0]) / jnp.sqrt(squares[1])
    scaled_mats = ratios[:6][:, None, None] * dir_mat
    scaled_norms = ratios[6:][:, None] * dir_norm
    return (
        result[None],
        grad_latents[None],
        grad_mats,
        grad_norms,
        scaled_mats,
        scaled_norms,
        m1_mat,
        m2_mat,
        m1_norm,
        m2_norm,
        ratios,
    )


def solution(mesh):
    return jax.shard_map(
        on_device,
        mesh=mesh,
        in_specs=(
            P(("dp", "fsdp"), None, None),
            P(("dp", "fsdp"), None),
            P(("dp", "fsdp"), None, None),
            P(None, ("dp", "fsdp"), None),
            P(None, ("dp", "fsdp")),
            P(None, ("dp", "fsdp"), None),
            P(None, ("dp", "fsdp"), None),
            P(None, ("dp", "fsdp")),
            P(None, ("dp", "fsdp")),
        ),
        out_specs=(
            P(("dp", "fsdp"), None, None),
            P(("dp", "fsdp"), None, None),
            P(None, ("dp", "fsdp"), None),
            P(None, ("dp", "fsdp")),
            P(None, ("dp", "fsdp"), None),
            P(None, ("dp", "fsdp")),
            P(None, ("dp", "fsdp"), None),
            P(None, ("dp", "fsdp"), None),
            P(None, ("dp", "fsdp")),
            P(None, ("dp", "fsdp")),
            P(),
        ),
        check_vma=False,
    )
```

```python
import functools
import math

import jax
import jax.numpy as jnp
from jax import lax
from jax.experimental import pallas as pl
from jax.experimental.pallas import tpu as pltpu
from jax.sharding import PartitionSpec as P

HEADS = 8
AXES = ("dp", "fsdp")
LANES = 128

ln_eps = 1e-05
beta_one = 0.9
beta_two = 0.999
adam_eps = 1e-06
decay_rate = 0.01
adam_step = 100.0
gelu_coef = 0.7978845608
cubic_coef = 0.044715
mask_depth = -1e30

F32 = jnp.float32
LOW = jnp.bfloat16
NT = (((1,), (1,)), ((), ()))
TN = (((0,), (0,)), ((), ()))
SMEM = pl.BlockSpec(memory_space=pltpu.SMEM)
VMEM = pl.BlockSpec(memory_space=pltpu.VMEM)


def params(mib):
    return pltpu.CompilerParams(vmem_limit_bytes=mib * 2**20)


def shape(dims, kind):
    return jax.ShapeDtypeStruct(dims, kind)


def product(left, right, dims=(((1,), (0,)), ((), ()))):
    return lax.dot_general(left, right, dims, preferred_element_type=F32)


def cost(flops, moved):
    return pl.CostEstimate(flops=int(flops), bytes_accessed=int(moved), transcendentals=0)


def whole(array):
    return pl.BlockSpec(
        array.shape, lambda i: (0,) * len(array.shape), pipeline_mode=pl.Buffered(1)
    )


def rows_of(array, block):
    lead = array.shape[:-2]
    return pl.BlockSpec((*lead, block, array.shape[-1]), lambda i: (*(0,) * len(lead), i, 0))


def swap(value, mask, count):
    return lax.ppermute(value, AXES, [(i, i ^ mask) for i in range(count)])


def swap_all(values, bits, count):
    return [swap(v, b, count) for v, b in zip(values, bits)]


def hyper_sum(value, count):
    mask = 1
    while mask < count:
        value = value + swap(value, mask, count)
        mask *= 2
    return value


def after(value, *others):
    return lax.optimization_barrier((value, others))[0]


def mask_order(order, inner):
    masks = list(range(inner))
    for bit in order:
        masks = masks + [m ^ bit for m in masks]
    return masks


def by_columns(shards, parts):
    mats, rows, columns = shards.shape
    blocks = columns // parts // LANES
    split = shards.reshape(mats, rows, parts, blocks, LANES)
    return split.transpose(2, 0, 3, 1, 4).reshape(parts, mats * blocks * rows, LANES)


def normalize(value):
    centered = value - jnp.mean(value, -1, keepdims=True)
    inv_std = lax.rsqrt(jnp.mean(centered * centered, -1, keepdims=True) + ln_eps)
    return centered * inv_std, inv_std


def norm_back(grad_out, normed, inv_std, gain):
    grad_normed = grad_out * gain
    return inv_std * (
        grad_normed
        - jnp.mean(grad_normed, -1, keepdims=True)
        - normed * jnp.mean(grad_normed * normed, -1, keepdims=True)
    )


def place_all(table_ref, layout, rows, refs, out_ref):
    mats = out_ref.shape[0]
    for (line, start, column, blocks), ref in zip(layout, refs):

        @pl.loop(0, ref.shape[0])
        def _(n, line=line, start=start, column=column, blocks=blocks, ref=ref):
            row = pl.multiple_of(table_ref[line, start + n] * rows, rows)
            for j in range(mats):
                for b in range(blocks):
                    first = (j * blocks + b) * rows
                    lane = column + b * LANES
                    out_ref[j, pl.ds(row, rows), lane : lane + LANES] = ref[
                        n, first : first + rows, :
                    ]


def lane_rows(low, first, number):
    lane = lax.broadcasted_iota(jnp.int32, low, 1)
    return (lane >= first) & (lane < first + number)


def spread_norms(table_ref, layout, first_row, refs, held_ref, norm_ref):
    for (line, start, _, _), ref in zip(layout, refs):
        if line == 0:

            @pl.loop(0, ref.shape[0])
            def _(n, line=line, start=start, ref=ref):
                held_ref[pl.ds(table_ref[line, start + n], 1), :] = ref[
                    n, first_row : first_row + 16, :
                ].astype(F32)[0:1]

    near = LANES // 32
    blocks = held_ref.shape[0] // near
    for i in range(4):
        total = jnp.zeros((blocks, LANES), F32)
        for z in range(near):
            value = held_ref[pl.ds(z, blocks, stride=near), :]
            value = pltpu.roll(value, (32 * (z - i)) % LANES, 1)
            total = total + jnp.where(lane_rows(total.shape, 32 * z, 32), value, 0.0)
        for b in range(blocks):
            norm_ref[i : i + 1, b * LANES : (b + 1) * LANES] = total[b : b + 1]


def pack_norms(norms, held_ref):
    near = LANES // 32
    blocks = held_ref.shape[0] // near
    held = [jnp.zeros((blocks, LANES), F32) for _ in range(near)]
    for i, norm in enumerate(norms):
        stacked = jnp.concatenate(
            [norm[:, b * LANES : (b + 1) * LANES] for b in range(blocks)], 0
        )
        for z in range(near):
            value = pltpu.roll(stacked, (32 * (i - z)) % LANES, 1)
            held[z] = held[z] + jnp.where(lane_rows(value.shape, 32 * i, 32), value, 0.0)
    for z in range(near):
        held_ref[pl.ds(z, blocks, stride=near), :] = held[z]


def project_kernel(layout, rows, norm_row, parts, table_ref, x_ref, *refs):
    chunks = refs[:parts]
    hidden_ref, out_ref, norm_ref, weight_ref, held_ref = refs[-5:]
    mats, width, _ = weight_ref.shape

    @pl.when(pl.program_id(0) == 0)
    def _():
        place_all(table_ref, layout, rows, chunks, weight_ref)
        if norm_row is None:
            norm_ref[...] = refs[parts][...]
        else:
            spread_norms(table_ref, layout, norm_row, chunks, held_ref, norm_ref)

    normed, _ = normalize(x_ref[...].astype(F32))
    hidden = (normed * norm_ref[0:1, :] + norm_ref[1:2, :]).astype(LOW)
    hidden_ref[...] = hidden
    for j in range(mats):
        out_ref[:, j * width : (j + 1) * width] = product(hidden, weight_ref[j]).astype(LOW)


def attend_kernel(group, dim, power, q_ref, k_ref, v_ref, in_ref, out_ref, o_ref, lse_ref):
    for g in range(group):
        span = slice(g * dim, (g + 1) * dim)
        keys = jnp.concatenate([k_ref[:, span], out_ref[...]], 1)
        queries = jnp.concatenate([q_ref[:, span], in_ref[...]], 1)
        scores = product(keys, queries, NT)
        top = jnp.max(scores, 0, keepdims=True)
        weight = jnp.exp2((scores - top) * power)
        total = jnp.sum(weight, 0, keepdims=True)
        probs = (weight * (1.0 / total)).astype(LOW)
        o_ref[:, span] = product(v_ref[:, span].T, probs).T.astype(LOW)
        lse_ref[g] = top * power + jnp.log2(total)


def attend_back_kernel(
    group, dim, power, scale,
    q_ref, k_ref, v_ref, do_ref, o_ref, in_ref, out_ref, lse_ref,
    grad_ref,
):
    for g in range(group):
        span = slice(g * dim, (g + 1) * dim)
        queries, keys, grad = q_ref[:, span], k_ref[:, span], do_ref[:, span]
        both = grad.astype(F32) * o_ref[:, span].astype(F32)
        row_dot = lax.dot_general(
            jnp.ones((8, dim), F32), both, NT,
            preferred_element_type=F32, precision=lax.Precision.HIGHEST,
        )[0:1]
        scores = product(
            jnp.concatenate([keys, out_ref[...]], 1),
            jnp.concatenate([queries, in_ref[...]], 1),
            NT,
        )
        probs = jnp.exp2(scores * power - lse_ref[g])
        grad_probs = product(v_ref[:, span], grad, NT)
        grad_scores = (probs * (grad_probs - row_dot)).astype(LOW)
        grad_ref[2, :, span] = product(probs.astype(LOW), grad).astype(LOW)
        grad_ref[1, :, span] = (product(grad_scores, queries) * scale).astype(LOW)
        grad_ref[0, :, span] = (product(keys.T, grad_scores).T * scale).astype(LOW)


def middle_kernel(atts, x_ref, dz_ref, live_ref, norm_ref, weight_ref, *refs):
    att_refs = refs[:atts]
    result_ref, middle_ref, dmlp_ref, hidden_ref, dup_ref, act_ref = refs[atts:]
    live = live_ref[...]
    branch, first = None, 0
    for ref in att_refs:
        part = product(ref[...], weight_ref[0, first : first + ref.shape[1], :])
        branch = part if branch is None else branch + part
        first += ref.shape[1]
    middle = x_ref[...].astype(F32) + live * branch
    middle_ref[...] = middle
    normed, _ = normalize(middle)
    hidden = (normed * norm_ref[2:3, :] + norm_ref[3:4, :]).astype(LOW)
    hidden_ref[...] = hidden
    upward = product(hidden, weight_ref[1])
    square = upward * upward
    bend = jnp.tanh(gelu_coef * (upward + cubic_coef * square * upward))
    half = 0.5 * (1.0 + bend)
    active = (upward * half).astype(LOW)
    act_ref[...] = active
    slope = half + (0.5 * gelu_coef) * upward * (1.0 - bend * bend) * (
        1.0 + (3.0 * cubic_coef) * square
    )
    result_ref[...] = (middle + live * product(active, weight_ref[2])).astype(LOW)
    dmlp = (live * dz_ref[...].astype(F32)).astype(LOW)
    dmlp_ref[...] = dmlp
    dup_ref[...] = (product(dmlp, weight_ref[2], NT) * slope).astype(LOW)


def middle_back_kernel(
    middle_ref, dup_ref, dz_ref, live_ref, norm_ref, weight_ref,
    dmid_ref, dbranch_ref, datt_ref, dnorm_ref,
):
    @pl.when(pl.program_id(0) == 0)
    def _():
        dnorm_ref[...] = jnp.zeros_like(dnorm_ref)

    normed, inv_std = normalize(middle_ref[...])
    dhidden = product(dup_ref[...], weight_ref[1], NT)
    dnorm_ref[0:1, :] += jnp.sum(dhidden * normed, 0, keepdims=True)
    dnorm_ref[1:2, :] += jnp.sum(dhidden, 0, keepdims=True)
    dmid = dz_ref[...].astype(F32) + norm_back(dhidden, normed, inv_std, norm_ref[2:3, :])
    dmid_ref[...] = dmid
    dbranch = (live_ref[...] * dmid).astype(LOW)
    dbranch_ref[...] = dbranch
    datt_ref[...] = product(dbranch, weight_ref[0], NT).astype(LOW)


def last_kernel(layout, rows, parts, sides, table_ref, x_ref, dmid_ref, norm_ref, other_ref, *refs):
    chunks, grads = refs[:parts], refs[parts : -4 - sides]
    out_ref, dnorm_ref = refs[-4 - sides : -2 - sides]
    packs, (weight_ref, held_ref) = refs[-2 - sides : -2], refs[-2:]
    mats = weight_ref.shape[0]

    @pl.when(pl.program_id(0) == 0)
    def _():
        place_all(table_ref, layout, rows, chunks, weight_ref)
        dnorm_ref[...] = jnp.zeros_like(dnorm_ref)

    total, column = None, 0
    for ref in grads:
        wide = ref.shape[2]
        for j in range(mats):
            part = product(ref[j], weight_ref[j, :, column : column + wide], NT)
            total = part if total is None else total + part
        column += wide
    normed, inv_std = normalize(x_ref[...].astype(F32))
    dnorm_ref[0:1, :] += jnp.sum(total * normed, 0, keepdims=True)
    dnorm_ref[1:2, :] += jnp.sum(total, 0, keepdims=True)
    out_ref[...] = (
        dmid_ref[...] + norm_back(total, normed, inv_std, norm_ref[0:1, :])
    ).astype(LOW)

    @pl.when((pl.program_id(0) == pl.num_programs(0) - 1) & (sides > 0))
    def _():
        norms = [ref[i : i + 1, :] for ref in (dnorm_ref, other_ref) for i in range(2)]
        if packs:
            pack_norms(norms, held_ref)
        for side, ref in enumerate(packs):

            @pl.loop(0, ref.shape[0])
            def _(n, ref=ref, side=side):
                row = held_ref[pl.ds(table_ref[0, side * ref.shape[0] + n], 1), :]
                ref[n] = jnp.broadcast_to(row, (16, LANES)).astype(LOW)


def weight_grad_kernel(jobs, rows, lefts, extra, table_ref, *refs):
    rights = 1 + max(right for _, right, _ in jobs)
    outs, held_ref = refs[lefts + rights : -1], refs[-1]
    parts = outs[0].shape[0]
    at = 0
    for pieces, right, entry in jobs:
        value = refs[lefts + right][...] if entry is None else refs[lefts + right][entry]
        wide = value.shape[1]
        blocks = wide // LANES // parts
        start = 0
        for piece in pieces:
            left = refs[piece]
            step = min(256, left.shape[1])
            for c in range(0, left.shape[1], step):
                held_ref[start : start + step, :wide] = product(
                    left[:, c : c + step], value, TN
                ).astype(LOW)
                start += step
        for h in range(parts):
            for side, ref in enumerate(outs):
                number = ref.shape[1]

                @pl.loop(0, number)
                def _(n, ref=ref, side=side, number=number, h=h, at=at, blocks=blocks):
                    row = pl.multiple_of(table_ref[h, side * number + n] * rows, rows)
                    for b in range(blocks):
                        lane = (h * blocks + b) * LANES
                        first = at + b * rows
                        ref[h, n, first : first + rows, :] = held_ref[
                            pl.ds(row, rows), lane : lane + LANES
                        ]

        at += blocks * rows
    if extra:
        for ref in outs:
            ref[:, :, at : at + extra, :] = jnp.zeros((*ref.shape[:2], extra, LANES), LOW)


def weight_grads(table, lefts, rights, jobs, rows, chunks, parts, sides, extra=0):
    length = lefts[0].shape[0]
    width = rows * chunks
    wides = [rights[right].shape[-1] for _, right, _ in jobs]
    size = sum(wides) // parts // LANES * rows + extra
    return pl.pallas_call(
        functools.partial(weight_grad_kernel, jobs, rows, len(lefts), extra),
        out_shape=[shape((parts, chunks // sides, size, LANES), LOW)] * sides,
        in_specs=[SMEM] + [VMEM] * (len(lefts) + len(rights)),
        out_specs=[VMEM] * sides,
        scratch_shapes=[pltpu.VMEM((width, max(wides)), LOW)],
        compiler_params=params(28),
        cost_estimate=cost(2 * length * width * sum(wides), 4 * width * sum(wides)),
    )(table, *lefts, *rights)


def slots_of(jobs, rows, parts):
    slots = [[] for _ in range(parts)]
    at = 0
    for matrix, column, wide in jobs:
        blocks = wide // LANES // parts
        for h in range(parts):
            for b in range(blocks):
                slots[h].append((matrix, column + (h * blocks + b) * LANES, at + b * rows))
        at += blocks * rows
    return slots


def sum_kernel(plans, *refs):
    ins, outs = refs[: -len(plans)], refs[-len(plans) :]
    for plan, out in zip(plans, outs):
        for at, terms, ends in plan:
            total = sum(ins[number][entry].astype(F32) for number, entry in terms)
            out[at] = total.astype(out.dtype)
            if ends:
                size = ins[ends[0][0]].shape[1]
                last = total[-size:] + sum(ins[n][entry].astype(F32) for n, entry in ends)
                out[at, -size:, :] = last.astype(out.dtype)


def stage_sums(inputs, plans, outs):
    return pl.pallas_call(
        functools.partial(sum_kernel, plans),
        out_shape=outs,
        in_specs=[VMEM] * len(inputs),
        out_specs=[VMEM] * len(outs),
        compiler_params=params(24),
        cost_estimate=cost(0, 2**22),
    )(*inputs)


def terms_of(parts, earlier, h, entry):
    return [(0, (h, entry)), (1, (h, entry))] + [
        (2 + parts * e + h, entry) for e in range(earlier)
    ]


def far_sums(keep, taken, earlier, ends=()):
    parts, chunks, size, _ = keep.shape
    half = chunks // 2 ** (len(earlier) + 1)
    base = 2 + parts * len(earlier)
    plans = [
        [
            (
                n,
                terms_of(parts, len(earlier), h, half + n),
                [(base + e, half + n) for e in range(len(ends))] if h == 0 else [],
            )
            for n in range(half)
        ]
        for h in range(parts)
    ]
    outs = [shape((half, size, LANES), LOW)] * parts
    return stage_sums([keep, taken, *[t for e in earlier for t in e], *ends], plans, outs)


def near_sums(keep, taken, earlier, inner, ends=()):
    parts, _, size, _ = keep.shape
    base = 2 + parts * len(earlier)
    plans = [
        [
            (
                h,
                terms_of(parts, len(earlier), h, k),
                [(base + e, k) for e in range(len(ends))] if h == 0 else [],
            )
            for h in range(parts)
        ]
        for k in range(inner)
    ]
    outs = [shape((parts, size, LANES), F32 if k == 0 else LOW) for k in range(inner)]
    return stage_sums([keep, taken, *[t for e in earlier for t in e], *ends], plans, outs)


def lamb_values(weight, grad, first, second):
    m_one = beta_one * first + (1.0 - beta_one) * grad
    m_two = beta_two * second + (1.0 - beta_two) * grad * grad
    step_dir = (
        m_one
        / (1.0 - beta_one**adam_step)
        / (jnp.sqrt(m_two / (1.0 - beta_two**adam_step)) + adam_eps)
        + decay_rate * weight
    )
    return m_one, m_two, step_dir


def whole_sum(value):
    return jnp.sum(jnp.sum(value, 0, keepdims=True), 1, keepdims=True)


def lamb_kernel(base, mats, groups, terms, norm_ends, prior, *refs):
    weight_ref, one_ref, two_ref = refs[:3]
    norm_refs = refs[3:6] if norm_ends else ()
    first = 3 + len(norm_refs)
    term_refs = refs[first : first + terms]
    prior_refs = refs[first + terms : first + terms + prior]
    outs = refs[first + terms + prior :]
    rows = weight_ref.shape[1]
    lane = lax.broadcasted_iota(jnp.int32, (8, LANES), 1)
    line = lax.broadcasted_iota(jnp.int32, (8, LANES), 0)
    squares = jnp.zeros((8, LANES), F32)
    weight_sq = [jnp.zeros((1, LANES), F32)] * mats
    update_sq = [jnp.zeros((1, LANES), F32)] * mats
    for used, entry, slots in groups:
        for matrix, column, at in slots:
            grad = sum(term_refs[t][entry, at : at + rows, :].astype(F32) for t in used)
            span = slice(column, column + LANES)
            weight = weight_ref[matrix, :, span]
            m_one, m_two, step = lamb_values(
                weight, grad, one_ref[matrix, :, span], two_ref[matrix, :, span]
            )
            j = matrix - base
            for ref, value in zip(outs, (grad, m_one, m_two, step)):
                ref[j, :, span] = value
            weight_sq[j] += jnp.sum(weight * weight, 0, keepdims=True)
            update_sq[j] += jnp.sum(step * step, 0, keepdims=True)
    for j in range(mats):
        spot = lane == base + j
        squares += jnp.where(spot & (line == 0), jnp.sum(weight_sq[j], 1, keepdims=True), 0.0)
        squares += jnp.where(spot & (line == 1), jnp.sum(update_sq[j], 1, keepdims=True), 0.0)
    if prior:
        for ref, old in zip(outs[:4], prior_refs[:4]):
            ref[mats:] = old[...]
        squares += prior_refs[4][...]
    if norm_ends:
        used, entry, at = norm_ends
        row = sum(term_refs[t][entry, at : at + 16, :].astype(F32)[0:1] for t in used)
        for i in range(4):
            weight = norm_refs[0][i : i + 1, :]
            grad = row[:, i * rows : (i + 1) * rows]
            m_one, m_two, step = lamb_values(
                weight, grad, norm_refs[1][i : i + 1, :], norm_refs[2][i : i + 1, :]
            )
            for ref, value in zip(outs[5:], (grad, m_one, m_two, step)):
                ref[i : i + 1, :] = value
            spot = lane == 6 + i
            squares += jnp.where(spot & (line == 0), whole_sum(weight * weight), 0.0)
            squares += jnp.where(spot & (line == 1), whole_sum(step * step), 0.0)
    outs[4][...] = squares


def lamb_call(base, mats, groups, terms, state, norm_state=(), norm_ends=None, prior=()):
    total, rows, width = state[0].shape
    outs = [shape((total if prior else mats, rows, width), F32)] * 4 + [shape((8, LANES), F32)]
    if norm_ends:
        outs += [shape(norm_state[0].shape, F32)] * 4
    inputs = [*state, *norm_state, *terms, *prior]
    return pl.pallas_call(
        functools.partial(lamb_kernel, base, mats, groups, len(terms), norm_ends, len(prior)),
        out_shape=outs,
        in_specs=[VMEM] * len(inputs),
        out_specs=[VMEM] * len(outs),
        compiler_params=params(24),
        cost_estimate=cost(0, 2**22),
    )(*inputs)


def on_device(
    latents,
    lengths,
    cotangent,
    matrices,
    norm_params,
    moment1_mat,
    moment2_mat,
    moment1_norm,
    moment2_norm,
):
    _, length, width = latents.shape
    dim = width // HEADS
    scale = 1.0 / math.sqrt(dim)
    power = scale * math.log2(math.e)
    dp, fsdp = lax.axis_size("dp"), lax.axis_size("fsdp")
    count = dp * fsdp
    rows = matrices.shape[1]
    index = lax.axis_index("dp") * fsdp + lax.axis_index("fsdp")
    ring = dp == 8 and fsdp == 4 and rows == 32
    inner, pair = fsdp, fsdp
    block = 256 if length % 256 == 0 else length
    low_mats = matrices.astype(LOW)
    low_norms = norm_params.astype(LOW)

    if ring:
        firsts, seconds = (2 * fsdp, 4 * fsdp), (4 * fsdp, 2 * fsdp)
        half_blocks = width // 2 // LANES
        norm_row = 3 * half_blocks * rows
        masks = jnp.array(
            [
                [m ^ side for side in (0, pair) for m in mask_order(o, inner)]
                for o in zip(firsts, seconds)
            ],
            jnp.int32,
        )
        table = jnp.bitwise_xor(masks, index.astype(jnp.int32))
        norm_rows = jnp.pad(low_norms.reshape(1, 1, 4 * rows), ((0, 1), (0, 15), (0, 0)))
        shard = jnp.concatenate([by_columns(low_mats[:3], 2), norm_rows], 1)
        quarter = count // 4
        layout = tuple(
            (h, side * count // 2 + part * quarter, h * width // 2, half_blocks)
            for h in range(2)
            for side in range(2)
            for part in range(2)
        )

        def grow(held, taken):
            return [jnp.concatenate(both) for both in zip(held, taken)]

        near = [shard] + [swap(shard, k, count) for k in range(1, inner)]
        held = [jnp.stack([n[h] for n in near]) for h in range(2)]
        held = grow(held, swap_all(held, firsts, count))
        taken = swap_all(held, seconds, count)
        early = swap_all(held, [pair, pair], count)
        late = swap_all(taken, [pair, pair], count)
        parts_in = [a for h in range(2) for a in (held[h], taken[h], early[h], late[h])]
        weights_out = lax.all_gather(low_mats[3:], AXES, axis=1, tiled=True)
        norm_vals = []
    else:
        weights_in = lax.all_gather(low_mats[:3], AXES, axis=1, tiled=True)
        weights_out = lax.all_gather(low_mats[3:], AXES, axis=1, tiled=True)
        norm_vals = [lax.all_gather(low_norms, AXES, axis=1, tiled=True).astype(F32)]
        table = jnp.zeros((1, 1), jnp.int32)
        rows = width
        parts_in = [by_columns(weights_in, 1)]
        layout = ((0, 0, 0, width // LANES),)
        norm_row = None

    ends = jnp.cumsum(lengths[0, :-1])
    sets = ends.shape[0]
    segment = jnp.sum(
        (jnp.arange(length, dtype=jnp.int32)[:, None] >= ends[None, :]).astype(jnp.int32), axis=1
    )
    live = (segment < sets).astype(F32)[:, None]
    lanes = jnp.arange(LANES, dtype=jnp.int32)[None, :]
    same = segment[:, None] == lanes
    mark_in = same.astype(LOW)
    mark_out = jnp.where(same | (lanes > sets), 0.0, mask_depth).astype(LOW)

    x, dz = latents[0], cotangent[0]
    steps = (length // block,)
    held_rows = pl.BlockSpec((4, width), lambda i: (0, 0))
    two_rows = pl.BlockSpec((2, width), lambda i: (0, 0))
    weight_scratch = pltpu.VMEM((3, width, width), LOW)
    hidden_one, qkv, norm_vals = pl.pallas_call(
        functools.partial(project_kernel, layout, rows, norm_row, len(parts_in)),
        grid=steps,
        out_shape=[
            shape((length, width), LOW),
            shape((length, 3 * width), LOW),
            shape((4, width), F32),
        ],
        in_specs=[SMEM, rows_of(x, block)]
        + [whole(a) for a in parts_in]
        + [held_rows] * len(norm_vals),
        out_specs=[
            pl.BlockSpec((block, width), lambda i: (i, 0)),
            pl.BlockSpec((block, 3 * width), lambda i: (i, 0)),
            held_rows,
        ],
        scratch_shapes=[weight_scratch, pltpu.VMEM((32, LANES), F32)],
        compiler_params=params(28),
        cost_estimate=cost(6 * length * width * width, 12 * width * width),
    )(table, x, *parts_in, *norm_vals)

    group = 2
    marks = [pl.BlockSpec((length, LANES), lambda h: (0, 0))] * 2

    def heads_at(first):
        return pl.BlockSpec((length, dim * group), lambda h: (0, first // group + h))

    def sums_at(first):
        return pl.BlockSpec((group, 1, length), lambda h: (first // group + h, 0, 0))

    def attend(first, number, qkv):
        return pl.pallas_call(
            functools.partial(attend_kernel, group, dim, power),
            grid=(number // group,),
            in_specs=[heads_at(first + i * HEADS) for i in range(3)] + marks,
            out_specs=[heads_at(0), sums_at(0)],
            out_shape=[shape((length, number * dim), LOW), shape((number, 1, length), F32)],
            compiler_params=params(28),
            cost_estimate=cost(8 * length * length * number * dim, 8 * length * number * dim),
        )(qkv, qkv, qkv, mark_in, mark_out)

    ahead = HEADS // 2
    attended, log_sums = zip(*[attend(f, ahead, qkv) for f in (0, ahead)])

    row_block = pl.BlockSpec((block, width), lambda i: (i, 0))
    low_rows = shape((length, width), LOW)
    result, middle, dmlp, hidden_two, dup, active = pl.pallas_call(
        functools.partial(middle_kernel, len(attended)),
        grid=steps,
        out_shape=[low_rows, shape((length, width), F32), *[low_rows] * 4],
        in_specs=[row_block, row_block, rows_of(live, block), held_rows, whole(weights_out)]
        + [rows_of(a, block) for a in attended],
        out_specs=[row_block] * 6,
        compiler_params=params(32),
        cost_estimate=cost(8 * length * width * width, 12 * width * width),
    )(x, dz, live, norm_vals, weights_out, *attended)

    def middle_back(dup):
        return pl.pallas_call(
            middle_back_kernel,
            grid=steps,
            out_shape=[shape((length, width), F32), low_rows, low_rows, shape((2, width), F32)],
            in_specs=[row_block, row_block, row_block, rows_of(live, block), held_rows]
            + [whole(weights_out)],
            out_specs=[row_block] * 3 + [two_rows],
            compiler_params=params(28),
            cost_estimate=cost(4 * length * width * width, 12 * width * width),
        )(middle, dup, dz, live, norm_vals, weights_out)

    def attend_back(first, number, dattended):
        side = first // ahead
        inside = first - side * ahead
        return pl.pallas_call(
            functools.partial(attend_back_kernel, group, dim, power, scale),
            grid=(number // group,),
            in_specs=[heads_at(first + i * HEADS) for i in range(3)]
            + [heads_at(first), heads_at(inside), *marks, sums_at(inside)],
            out_specs=pl.BlockSpec((3, length, dim * group), lambda h: (0, 0, h)),
            out_shape=shape((3, length, number * dim), LOW),
            compiler_params=params(28),
            cost_estimate=cost(20 * length * length * number * dim, 16 * length * number * dim),
        )(qkv, qkv, qkv, dattended, attended[side], mark_in, mark_out, log_sums[side])

    def last(dmid, grads, sides):
        packs = [shape((count // max(sides, 1), 16, LANES), LOW)] * sides
        return pl.pallas_call(
            functools.partial(last_kernel, layout, rows, len(parts_in), sides),
            grid=steps,
            out_shape=[low_rows, shape((2, width), F32), *packs],
            in_specs=[SMEM, row_block, row_block, held_rows, two_rows]
            + [whole(a) for a in parts_in]
            + [rows_of(g, block) for g in grads],
            out_specs=[row_block, two_rows]
            + [pl.BlockSpec(p.shape, lambda i: (0, 0, 0)) for p in packs],
            scratch_shapes=[weight_scratch, pltpu.VMEM((32, LANES), F32)],
            compiler_params=params(36),
            cost_estimate=cost(6 * length * width * width, 6 * width * width),
        )(table, x, dmid, norm_vals, dnorm_two, *parts_in, *grads)

    state, norm_state = (matrices, moment1_mat, moment2_mat), (norm_params, moment1_norm, moment2_norm)
    in_jobs = [((0,), n, j) for n in range(2) for j in range(3)]
    mlp = ([hidden_two, active], [dup, dmlp], [((0,), 0, None), ((1,), 1, None)])
    if ring:
        pairs = range(1, inner)

        def slots(jobs):
            return slots_of(jobs, rows, 2)

        slots_mlp = slots([(4, 0, width), (5, 0, width)])
        heads_w = group * dim
        slots_one = slots(
            [(3, 0, width)] + [(j, n * heads_w, heads_w) for n in range(2) for j in range(3)]
        )
        slots_two = slots([(j, n * heads_w, heads_w) for n in (2, 3) for j in range(3)])

        keep, send = weight_grads(table, *mlp, rows, count, 2, 2)
        taken = swap(send, pair, count)
        dmid, dbranch, dattended, dnorm_two = middle_back(after(dup, keep))

        sent = far_sums(keep, after(taken, dattended), [])
        far = [swap_all(sent, seconds, count)]
        grads = [attend_back(0, 2, after(dattended, *sent))]
        grads.append(attend_back(2, 2, after(dattended, grads[0])))
        keep_one, send_one = weight_grads(
            table,
            [*attended, hidden_one],
            [dbranch, *grads],
            [((0, 1), 0, None)] + [((2,), 1 + n, j) for _, n, j in in_jobs],
            rows,
            count,
            2,
            2,
        )

        sent = far_sums(keep, taken, after(far, keep_one))
        far.append(swap_all(sent, firsts, count))
        taken_one = swap(after(send_one, *sent), pair, count)
        grads.append(attend_back(4, 2, after(dattended, *sent, keep_one)))

        near = near_sums(keep, taken, [far[0], after(far[1], grads[2])], inner)
        sent_one = far_sums(keep_one, after(taken_one, grads[2]), [])
        far_one = [swap_all(sent_one, seconds, count)]
        near = [near[0]] + swap_all(near[1:], pairs, count)
        grads.append(attend_back(6, 2, after(dattended, *sent_one, near[0])))
        keep_two, send_two = weight_grads(
            table, [hidden_one], grads[2:], in_jobs, rows, count, 2, 2, 16
        )

        sent_one = far_sums(keep_one, taken_one, after(far_one, keep_two, *near))
        far_one.append(swap_all(sent_one, firsts, count))
        taken_two = swap(after(send_two, *sent_one), pair, count)
        grad_latents, dnorm_one, *packs = last(after(dmid, *sent_one), grads, 2)

        near_one = near_sums(
            keep_one, taken_one, [far_one[0], after(far_one[1], grad_latents)], inner
        )
        near_one = [near_one[0]] + swap_all(near_one[1:], pairs, count)
        ends = [packs[0], swap(after(packs[1], near_one[0]), pair, count)]
        groups = [(range(inner), h, slots_mlp[h]) for h in range(2)]
        prior = lamb_call(4, 2, groups, near, state)

        taken_two, ends[1] = after((taken_two, ends[1]), prior[4])
        sent_two = far_sums(keep_two, taken_two, [], ends)
        far_two = [swap_all(sent_two, seconds, count)]
        sent_two = far_sums(keep_two, taken_two, far_two, ends)
        far_two.append(swap_all(sent_two, firsts, count))
        near_one = [near_one[0], *after(near_one[1:], *sent_two)]
        near_two = near_sums(keep_two, taken_two, far_two, inner, ends)
        near_two = [near_two[0]] + swap_all(near_two[1:], pairs, count)
        groups = [(range(inner), h, slots_one[h]) for h in range(2)]
        groups += [(range(inner, 2 * inner), h, slots_two[h]) for h in range(2)]
        norm_ends = (range(inner, 2 * inner), 0, near_two[0].shape[1] - 16)
        found = lamb_call(
            0, 4, groups, [*near_one, *near_two], state, norm_state, norm_ends, prior
        )
        grad_mats, m1_mat, m2_mat, dir_mat, squares, grad_norms, m1_norm, m2_norm, dir_norm = found
        squares = hyper_sum(squares, count)[:2, :10]
    else:
        dmid, dbranch, dattended, dnorm_two = middle_back(dup)
        grads = [attend_back(f, ahead, dattended) for f in (0, ahead)]
        (mlp_grads,) = weight_grads(table, *mlp, rows, 1, 1, 1)
        (in_grads,) = weight_grads(
            table,
            [*attended, hidden_one],
            [dbranch, *grads],
            [((0, 1), 0, None)] + [((2,), 1 + n, j) for j in range(3) for n in range(2)],
            rows,
            1,
            1,
            1,
        )
        grad_latents, dnorm_one = last(dmid, grads, 0)
        norms_local = jnp.concatenate([dnorm_one, dnorm_two], 0)
        local = jnp.concatenate([in_grads[0, 0], mlp_grads[0, 0]], 0).astype(F32)
        local = local.reshape(6, width // LANES, width, LANES)
        local = local.transpose(0, 2, 1, 3).reshape(6, width, width)
        local = jnp.concatenate([local[1:4], local[:1], local[4:]], 0)
        grad_mats = lax.psum_scatter(local, AXES, scatter_dimension=1, tiled=True)
        grad_norms = lax.psum_scatter(norms_local, AXES, scatter_dimension=1, tiled=True)
        m1_mat, m2_mat, dir_mat = lamb_values(matrices, grad_mats, moment1_mat, moment2_mat)
        m1_norm, m2_norm, dir_norm = lamb_values(norm_params, grad_norms, moment1_norm, moment2_norm)
        squares = jnp.stack(
            [
                jnp.concatenate([jnp.sum(m * m, (1, 2)), jnp.sum(n * n, 1)])
                for m, n in ((matrices, norm_params), (dir_mat, dir_norm))
            ]
        )
        squares = lax.psum(squares, AXES)
    ratios = jnp.sqrt(squares[0]) / jnp.sqrt(squares[1])
    scaled_mats = ratios[:6][:, None, None] * dir_mat
    scaled_norms = ratios[6:][:, None] * dir_norm
    return (
        result[None],
        grad_latents[None],
        grad_mats,
        grad_norms,
        scaled_mats,
        scaled_norms,
        m1_mat,
        m2_mat,
        m1_norm,
        m2_norm,
        ratios,
    )


def solution(mesh):
    return jax.shard_map(
        on_device,
        mesh=mesh,
        in_specs=(
            P(("dp", "fsdp"), None, None),
            P(("dp", "fsdp"), None),
            P(("dp", "fsdp"), None, None),
            P(None, ("dp", "fsdp"), None),
            P(None, ("dp", "fsdp")),
            P(None, ("dp", "fsdp"), None),
            P(None, ("dp", "fsdp"), None),
            P(None, ("dp", "fsdp")),
            P(None, ("dp", "fsdp")),
        ),
        out_specs=(
            P(("dp", "fsdp"), None, None),
            P(("dp", "fsdp"), None, None),
            P(None, ("dp", "fsdp"), None),
            P(None, ("dp", "fsdp")),
            P(None, ("dp", "fsdp"), None),
            P(None, ("dp", "fsdp")),
            P(None, ("dp", "fsdp"), None),
            P(None, ("dp", "fsdp"), None),
            P(None, ("dp", "fsdp")),
            P(None, ("dp", "fsdp")),
            P(),
        ),
        check_vma=False,
    )
```

```python
import functools
import math

import jax
import jax.numpy as jnp
from jax import lax
from jax.experimental import pallas as pl
from jax.experimental.pallas import tpu as pltpu
from jax.sharding import PartitionSpec as P

HEADS = 8
AXES = ("dp", "fsdp")
LANES = 128

ln_eps = 1e-05
beta_one = 0.9
beta_two = 0.999
adam_eps = 1e-06
decay_rate = 0.01
adam_step = 100.0
gelu_coef = 0.7978845608
cubic_coef = 0.044715
mask_depth = -1e30

F32 = jnp.float32
LOW = jnp.bfloat16
NT = (((1,), (1,)), ((), ()))
TN = (((0,), (0,)), ((), ()))
SMEM = pl.BlockSpec(memory_space=pltpu.SMEM)
VMEM = pl.BlockSpec(memory_space=pltpu.VMEM)


def params(mib):
    return pltpu.CompilerParams(vmem_limit_bytes=mib * 2**20)


def shape(dims, kind):
    return jax.ShapeDtypeStruct(dims, kind)


def product(left, right, dims=(((1,), (0,)), ((), ()))):
    return lax.dot_general(left, right, dims, preferred_element_type=F32)


def cost(flops, moved):
    return pl.CostEstimate(flops=int(flops), bytes_accessed=int(moved), transcendentals=0)


def whole(array):
    return pl.BlockSpec(
        array.shape, lambda i: (0,) * len(array.shape), pipeline_mode=pl.Buffered(1)
    )


def rows_of(array, block):
    lead = array.shape[:-2]
    return pl.BlockSpec((*lead, block, array.shape[-1]), lambda i: (*(0,) * len(lead), i, 0))


def swap(value, mask, count):
    return lax.ppermute(value, AXES, [(i, i ^ mask) for i in range(count)])


def swap_all(values, bits, count):
    return [swap(v, b, count) for v, b in zip(values, bits)]


def hyper_sum(value, count):
    mask = 1
    while mask < count:
        value = value + swap(value, mask, count)
        mask *= 2
    return value


def after(value, *others):
    return lax.optimization_barrier((value, others))[0]


def mask_order(order, inner):
    masks = list(range(inner))
    for bit in order:
        masks = masks + [m ^ bit for m in masks]
    return masks


def by_columns(shards, parts):
    mats, rows, columns = shards.shape
    blocks = columns // parts // LANES
    split = shards.reshape(mats, rows, parts, blocks, LANES)
    return split.transpose(2, 0, 3, 1, 4).reshape(parts, mats * blocks, rows, LANES)


def normalize(value):
    centered = value - jnp.mean(value, -1, keepdims=True)
    inv_std = lax.rsqrt(jnp.mean(centered * centered, -1, keepdims=True) + ln_eps)
    return centered * inv_std, inv_std


def norm_back(grad_out, normed, inv_std, gain):
    grad_normed = grad_out * gain
    return inv_std * (
        grad_normed
        - jnp.mean(grad_normed, -1, keepdims=True)
        - normed * jnp.mean(grad_normed * normed, -1, keepdims=True)
    )


def place_all(table_ref, layout, rows, refs, weight_ref, sem):
    def each(act):
        for (line, start, first), ref in zip(layout, refs):

            @pl.loop(0, ref.shape[0])
            def _(n, line=line, start=start, first=first, ref=ref):
                row = pl.multiple_of(table_ref[line, start + n] * rows, rows)
                act(
                    pltpu.make_async_copy(
                        ref.at[n],
                        weight_ref.at[first : first + ref.shape[1], pl.ds(row, rows)],
                        sem,
                    )
                )

    each(lambda copy: copy.start())
    each(lambda copy: copy.wait())


def matrix(weight_ref, blocks, first=0, size=None):
    size = weight_ref.shape[1] if size is None else size
    return jnp.concatenate([weight_ref[b, first : first + size, :] for b in blocks], 1)


def lane_rows(low, first, number):
    lane = lax.broadcasted_iota(jnp.int32, low, 1)
    return (lane >= first) & (lane < first + number)


def spread_norms(rows, weight_ref, block, held_ref, norm_ref):
    for n in range(held_ref.shape[0]):
        held_ref[n : n + 1, :] = weight_ref[block, n * rows : n * rows + 16, :].astype(F32)[0:1]
    near = LANES // 32
    blocks = held_ref.shape[0] // near
    for i in range(4):
        total = jnp.zeros((blocks, LANES), F32)
        for z in range(near):
            value = held_ref[pl.ds(z, blocks, stride=near), :]
            value = pltpu.roll(value, (32 * (z - i)) % LANES, 1)
            total = total + jnp.where(lane_rows(total.shape, 32 * z, 32), value, 0.0)
        for b in range(blocks):
            norm_ref[i : i + 1, b * LANES : (b + 1) * LANES] = total[b : b + 1]


def pack_norms(norms, held_ref):
    near = LANES // 32
    blocks = held_ref.shape[0] // near
    held = [jnp.zeros((blocks, LANES), F32) for _ in range(near)]
    for i, norm in enumerate(norms):
        stacked = jnp.concatenate(
            [norm[:, b * LANES : (b + 1) * LANES] for b in range(blocks)], 0
        )
        for z in range(near):
            value = pltpu.roll(stacked, (32 * (i - z)) % LANES, 1)
            held[z] = held[z] + jnp.where(lane_rows(value.shape, 32 * i, 32), value, 0.0)
    for z in range(near):
        held_ref[pl.ds(z, blocks, stride=near), :] = held[z]


def project_kernel(layout, rows, blocks, norm_block, parts, table_ref, x_ref, *refs):
    chunks = refs[:parts]
    hidden_ref, out_ref, norm_ref, weight_ref, held_ref, sem = refs[-6:]
    width = x_ref.shape[1]

    @pl.when(pl.program_id(0) == 0)
    def _():
        place_all(table_ref, layout, rows, chunks, weight_ref, sem)
        if norm_block is None:
            norm_ref[...] = refs[parts][...]
        else:
            spread_norms(rows, weight_ref, norm_block, held_ref, norm_ref)

    normed, _ = normalize(x_ref[...].astype(F32))
    hidden = (normed * norm_ref[0:1, :] + norm_ref[1:2, :]).astype(LOW)
    hidden_ref[...] = hidden
    for j, ids in enumerate(blocks):
        out_ref[:, j * width : (j + 1) * width] = product(
            hidden, matrix(weight_ref, ids)
        ).astype(LOW)


def attend_kernel(group, dim, power, q_ref, k_ref, v_ref, in_ref, out_ref, o_ref, lse_ref):
    for g in range(group):
        span = slice(g * dim, (g + 1) * dim)
        keys = jnp.concatenate([k_ref[:, span], out_ref[...]], 1)
        queries = jnp.concatenate([q_ref[:, span], in_ref[...]], 1)
        scores = product(keys, queries, NT)
        top = jnp.max(scores, 0, keepdims=True)
        weight = jnp.exp2((scores - top) * power)
        total = jnp.sum(weight, 0, keepdims=True)
        probs = (weight * (1.0 / total)).astype(LOW)
        o_ref[:, span] = product(v_ref[:, span].T, probs).T.astype(LOW)
        lse_ref[g] = top * power + jnp.log2(total)


def attend_back_kernel(
    group, dim, power, scale, base, extra, prior, place_ref,
    q_ref, k_ref, v_ref, do_ref, o_ref, in_ref, out_ref, lse_ref, hidden_ref, *refs,
):
    grad_ref, *outs = refs[prior:-2]
    held_ref, sem = refs[-2:]
    for g in range(group):
        span = slice(g * dim, (g + 1) * dim)
        queries, keys, grad = q_ref[:, span], k_ref[:, span], do_ref[:, span]
        both = grad.astype(F32) * o_ref[:, span].astype(F32)
        row_dot = lax.dot_general(
            jnp.ones((8, dim), F32), both, NT,
            preferred_element_type=F32, precision=lax.Precision.HIGHEST,
        )[0:1]
        scores = product(
            jnp.concatenate([keys, out_ref[...]], 1),
            jnp.concatenate([queries, in_ref[...]], 1),
            NT,
        )
        probs = jnp.exp2(scores * power - lse_ref[g])
        grad_probs = product(v_ref[:, span], grad, NT)
        grad_scores = (probs * (grad_probs - row_dot)).astype(LOW)
        grad_ref[2, :, span] = product(probs.astype(LOW), grad).astype(LOW)
        grad_ref[1, :, span] = (product(grad_scores, queries) * scale).astype(LOW)
        grad_ref[0, :, span] = (product(keys.T, grad_scores).T * scale).astype(LOW)
    parts = outs[0].shape[0]
    total = held_ref.shape[0] // 2
    size = total // parts
    step = pl.program_id(0)
    slot = lax.rem(step, 2) * total

    @pl.when(step > 1)
    def _():
        wait_rows(held_ref, 0, size, outs, sem)

    for s in range(2):

        @pl.when(slot == s * total)
        def _(s=s):
            weight_grad(
                hidden_ref, [grad_ref[j] for j in range(3)],
                place_ref, held_ref, s * total, outs, (base + step) * size, sem,
            )

    @pl.when(step == pl.num_programs(0) - 1)
    def _():
        wait_rows(held_ref, 0, size, outs, sem)

        @pl.when(step > 0)
        def _():
            wait_rows(held_ref, 0, size, outs, sem)

        if extra:
            empty = held_ref.at[0:1, 0 : outs[0].shape[3]]
            held_ref[0] = jnp.zeros(held_ref.shape[1:], LOW)
            copies = [
                pltpu.make_async_copy(empty, ref.at[h, n, pl.ds(ref.shape[2] - 1, 1)], sem)
                for ref in outs
                for h in range(parts)
                for n in range(ref.shape[1])
            ]
            for copy in copies:
                copy.start()
            for copy in copies:
                copy.wait()


def middle_kernel(
    layout, rows, blocks, atts, sides, table_ref, place_ref, x_ref, dz_ref, live_ref, norm_ref, *refs
):
    att_refs, chunks = refs[:atts], refs[atts : -9 - sides]
    dnorm_ref, result_ref, dmid_ref, datt_ref = refs[-9 - sides : -5 - sides]
    outs, (weight_ref, left_ref, right_ref, held_ref, sem) = refs[-5 - sides : -5], refs[-5:]
    block = x_ref.shape[0]
    here = pl.ds(pl.multiple_of(pl.program_id(0) * block, block), block)

    @pl.when(pl.program_id(0) == 0)
    def _():
        place_all(table_ref, layout, rows, chunks, weight_ref, sem)
        dnorm_ref[...] = jnp.zeros_like(dnorm_ref)

    gain, shift = norm_ref[2:3, :], norm_ref[3:4, :]
    live = live_ref[...]
    branch, first = None, 0
    for ref in att_refs:
        left_ref[0, here, first : first + ref.shape[1]] = ref[...]
        part = product(ref[...], matrix(weight_ref, blocks[0], first, ref.shape[1]))
        branch = part if branch is None else branch + part
        first += ref.shape[1]
    middle = x_ref[...].astype(F32) + live * branch
    normed, inv_std = normalize(middle)
    hidden = (normed * gain + shift).astype(LOW)
    left_ref[1, here, :] = hidden
    upward = product(hidden, matrix(weight_ref, blocks[1]))
    square = upward * upward
    bend = jnp.tanh(gelu_coef * (upward + cubic_coef * square * upward))
    half = 0.5 * (1.0 + bend)
    active = (upward * half).astype(LOW)
    left_ref[2, here, :] = active
    slope = half + (0.5 * gelu_coef) * upward * (1.0 - bend * bend) * (
        1.0 + (3.0 * cubic_coef) * square
    )
    result_ref[...] = (middle + live * product(active, matrix(weight_ref, blocks[2]))).astype(LOW)
    grad = dz_ref[...].astype(F32)
    dmlp = (live * grad).astype(LOW)
    right_ref[2, here, :] = dmlp
    dup = (product(dmlp, matrix(weight_ref, blocks[2]), NT) * slope).astype(LOW)
    right_ref[1, here, :] = dup
    dhidden = product(dup, matrix(weight_ref, blocks[1]), NT)
    dnorm_ref[0:1, :] += jnp.sum(dhidden * normed, 0, keepdims=True)
    dnorm_ref[1:2, :] += jnp.sum(dhidden, 0, keepdims=True)
    dmid = grad + norm_back(dhidden, normed, inv_std, gain)
    dmid_ref[...] = dmid
    dbranch = (live * dmid).astype(LOW)
    right_ref[0, here, :] = dbranch
    datt_ref[...] = product(dbranch, matrix(weight_ref, blocks[0]), NT).astype(LOW)

    @pl.when(pl.program_id(0) == pl.num_programs(0) - 1)
    def _():
        mats = left_ref.shape[0]
        total = held_ref.shape[0] // mats
        size = total // outs[0].shape[0]
        for j in range(mats):
            weight_grad(
                left_ref.at[j], [right_ref[j]], place_ref, held_ref, j * total, outs, j * size, sem
            )
        for j in range(mats):
            wait_rows(held_ref, j * total, size, outs, sem)


def last_kernel(layout, rows, blocks, parts, sides, table_ref, x_ref, dmid_ref, norm_ref, other_ref, *refs):
    chunks, grads = refs[:parts], refs[parts : -5 - sides]
    out_ref, dnorm_ref = refs[-5 - sides : -3 - sides]
    packs, (weight_ref, held_ref, sem) = refs[-3 - sides : -3], refs[-3:]

    @pl.when(pl.program_id(0) == 0)
    def _():
        place_all(table_ref, layout, rows, chunks, weight_ref, sem)
        dnorm_ref[...] = jnp.zeros_like(dnorm_ref)

    total = None
    for j, ids in enumerate(blocks):
        value = jnp.concatenate([ref[j] for ref in grads], 1)
        part = product(value, matrix(weight_ref, ids), NT)
        total = part if total is None else total + part
    normed, inv_std = normalize(x_ref[...].astype(F32))
    dnorm_ref[0:1, :] += jnp.sum(total * normed, 0, keepdims=True)
    dnorm_ref[1:2, :] += jnp.sum(total, 0, keepdims=True)
    out_ref[...] = (
        dmid_ref[...] + norm_back(total, normed, inv_std, norm_ref[0:1, :])
    ).astype(LOW)

    if packs:

        @pl.when(pl.program_id(0) == pl.num_programs(0) - 1)
        def _():
            pack_norms([ref[i : i + 1, :] for ref in (dnorm_ref, other_ref) for i in range(2)], held_ref)
            for side, ref in enumerate(packs):

                @pl.loop(0, ref.shape[0])
                def _(n, ref=ref, side=side):
                    row = held_ref[pl.ds(table_ref[0, side * ref.shape[0] + n], 1), :]
                    ref[n, 0] = jnp.broadcast_to(row, ref.shape[2:]).astype(LOW)


def send_rows(place_ref, held_ref, first, size, outs, block, sem, low, high):
    parts, number, _, rows, _ = outs[0].shape
    for chunk in range(held_ref.shape[1] // rows):
        if not low < (chunk + 1) * rows <= high:
            continue
        for h in range(parts):
            start = first + h * size
            source = held_ref.at[start : start + size, chunk * rows : (chunk + 1) * rows]
            place = place_ref[h, chunk]
            for side, ref in enumerate(outs):

                @pl.when((place >= side * number) & (place < (side + 1) * number))
                def _(source=source, ref=ref, side=side, h=h, place=place):
                    target = ref.at[h, place - side * number, pl.ds(block, size)]
                    pltpu.make_async_copy(source, target, sem).start()


def wait_rows(held_ref, first, size, outs, sem):
    parts, _, _, rows, _ = outs[0].shape
    for chunk in range(held_ref.shape[1] // rows):
        for h in range(parts):
            source = held_ref.at[first : first + size, chunk * rows : (chunk + 1) * rows]
            pltpu.make_async_copy(source, outs[0].at[h, 0, pl.ds(0, size)], sem).wait()


def weight_grad(left_ref, rights, place_ref, held_ref, first, outs, block, sem):
    parts = outs[0].shape[0]
    width = left_ref.shape[1]
    step = min(256, width)
    blocks = [r.shape[1] // LANES // parts for r in rights]
    size = sum(blocks)
    for c in range(0, width, step):
        left = left_ref[:, c : c + step]
        at = first
        for right, number in zip(rights, blocks):
            grad = product(left, right, TN).astype(LOW)
            for h in range(parts):
                for b in range(number):
                    lane = (h * number + b) * LANES
                    held_ref[at + h * size + b, c : c + step, :] = grad[:, lane : lane + LANES]
            at += number
        send_rows(place_ref, held_ref, first, size, outs, block, sem, c, c + step)


def slots_of(jobs, parts):
    slots = [[] for _ in range(parts)]
    for which, column, wide in jobs:
        blocks = wide // LANES // parts
        for h in range(parts):
            slots[h] += [(which, column + (h * blocks + b) * LANES) for b in range(blocks)]
    return slots


def sum_kernel(plans, *refs):
    ins, outs = refs[: -len(plans)], refs[-len(plans) :]
    for plan, out in zip(plans, outs):
        for at, terms, ends in plan:
            total = sum(ins[number][entry].astype(F32) for number, entry in terms)
            out[at] = total.astype(out.dtype)
            if ends:
                end = total.shape[0] - 1
                last = total[end:] + sum(ins[n][entry].astype(F32) for n, entry in ends)
                out[at, end:] = last.astype(out.dtype)


def stage_sums(inputs, plans, outs):
    return pl.pallas_call(
        functools.partial(sum_kernel, plans),
        out_shape=outs,
        in_specs=[VMEM] * len(inputs),
        out_specs=[VMEM] * len(outs),
        compiler_params=params(24),
        cost_estimate=cost(0, 2**22),
    )(*inputs)


def terms_of(parts, earlier, h, entry):
    return [(0, (h, entry)), (1, (h, entry))] + [
        (2 + parts * e + h, entry) for e in range(earlier)
    ]


def far_sums(keep, taken, earlier, ends=()):
    parts, chunks, *block = keep.shape
    half = chunks // 2 ** (len(earlier) + 1)
    base = 2 + parts * len(earlier)
    plans = [
        [
            (
                n,
                terms_of(parts, len(earlier), h, half + n),
                [(base + e, half + n) for e in range(len(ends))] if h == 0 else [],
            )
            for n in range(half)
        ]
        for h in range(parts)
    ]
    outs = [shape((half, *block), LOW)] * parts
    return stage_sums([keep, taken, *[t for e in earlier for t in e], *ends], plans, outs)


def near_sums(keep, taken, earlier, inner, ends=()):
    parts, _, *block = keep.shape
    base = 2 + parts * len(earlier)
    plans = [
        [
            (
                h,
                terms_of(parts, len(earlier), h, k),
                [(base + e, k) for e in range(len(ends))] if h == 0 else [],
            )
            for h in range(parts)
        ]
        for k in range(inner)
    ]
    outs = [shape((parts, *block), F32 if k == 0 else LOW) for k in range(inner)]
    return stage_sums([keep, taken, *[t for e in earlier for t in e], *ends], plans, outs)


def lamb_values(weight, grad, first, second):
    m_one = beta_one * first + (1.0 - beta_one) * grad
    m_two = beta_two * second + (1.0 - beta_two) * grad * grad
    step_dir = (
        m_one
        / (1.0 - beta_one**adam_step)
        / (jnp.sqrt(m_two / (1.0 - beta_two**adam_step)) + adam_eps)
        + decay_rate * weight
    )
    return m_one, m_two, step_dir


def whole_sum(value):
    return jnp.sum(jnp.sum(value, 0, keepdims=True), 1, keepdims=True)


def lamb_kernel(base, mats, groups, terms, norm_ends, prior, *refs):
    weight_ref, one_ref, two_ref = refs[:3]
    norm_refs = refs[3:6] if norm_ends else ()
    first = 3 + len(norm_refs)
    term_refs = refs[first : first + terms]
    prior_refs = refs[first + terms : first + terms + prior]
    outs = refs[first + terms + prior :]
    rows = weight_ref.shape[1]
    lane = lax.broadcasted_iota(jnp.int32, (8, LANES), 1)
    line = lax.broadcasted_iota(jnp.int32, (8, LANES), 0)
    squares = jnp.zeros((8, LANES), F32)
    weight_sq = [jnp.zeros((1, LANES), F32)] * mats
    update_sq = [jnp.zeros((1, LANES), F32)] * mats
    for used, entry, slots in groups:
        for at, (which, column) in enumerate(slots):
            grad = sum(term_refs[t][entry, at].astype(F32) for t in used)
            span = slice(column, column + LANES)
            weight = weight_ref[which, :, span]
            m_one, m_two, step = lamb_values(
                weight, grad, one_ref[which, :, span], two_ref[which, :, span]
            )
            j = which - base
            for ref, value in zip(outs, (grad, m_one, m_two, step)):
                ref[j, :, span] = value
            weight_sq[j] += jnp.sum(weight * weight, 0, keepdims=True)
            update_sq[j] += jnp.sum(step * step, 0, keepdims=True)
    for j in range(mats):
        spot = lane == base + j
        squares += jnp.where(spot & (line == 0), jnp.sum(weight_sq[j], 1, keepdims=True), 0.0)
        squares += jnp.where(spot & (line == 1), jnp.sum(update_sq[j], 1, keepdims=True), 0.0)
    if prior:
        for ref, old in zip(outs[:4], prior_refs[:4]):
            ref[mats:] = old[...]
        squares += prior_refs[4][...]
    if norm_ends:
        used, entry = norm_ends
        last = term_refs[used[0]].shape[1] - 1
        row = sum(term_refs[t][entry, last].astype(F32)[0:1] for t in used)
        for i in range(4):
            weight = norm_refs[0][i : i + 1, :]
            grad = row[:, i * rows : (i + 1) * rows]
            m_one, m_two, step = lamb_values(
                weight, grad, norm_refs[1][i : i + 1, :], norm_refs[2][i : i + 1, :]
            )
            for ref, value in zip(outs[5:], (grad, m_one, m_two, step)):
                ref[i : i + 1, :] = value
            spot = lane == 6 + i
            squares += jnp.where(spot & (line == 0), whole_sum(weight * weight), 0.0)
            squares += jnp.where(spot & (line == 1), whole_sum(step * step), 0.0)
    outs[4][...] = squares


def lamb_call(base, mats, groups, terms, state, norm_state=(), norm_ends=None, prior=()):
    total, rows, width = state[0].shape
    outs = [shape((total if prior else mats, rows, width), F32)] * 4 + [shape((8, LANES), F32)]
    if norm_ends:
        outs += [shape(norm_state[0].shape, F32)] * 4
    inputs = [*state, *norm_state, *terms, *prior]
    return pl.pallas_call(
        functools.partial(lamb_kernel, base, mats, groups, len(terms), norm_ends, len(prior)),
        out_shape=outs,
        in_specs=[VMEM] * len(inputs),
        out_specs=[VMEM] * len(outs),
        compiler_params=params(24),
        cost_estimate=cost(0, 2**22),
    )(*inputs)


def on_device(
    latents,
    lengths,
    cotangent,
    matrices,
    norm_params,
    moment1_mat,
    moment2_mat,
    moment1_norm,
    moment2_norm,
):
    _, length, width = latents.shape
    dim = width // HEADS
    scale = 1.0 / math.sqrt(dim)
    power = scale * math.log2(math.e)
    dp, fsdp = lax.axis_size("dp"), lax.axis_size("fsdp")
    count = dp * fsdp
    rows = matrices.shape[1]
    index = lax.axis_index("dp") * fsdp + lax.axis_index("fsdp")
    ring = dp == 8 and fsdp == 4 and rows == 32
    inner, pair = fsdp, fsdp
    block = 256 if length % 256 == 0 else length
    low_mats = matrices.astype(LOW)
    low_norms = norm_params.astype(LOW)

    if ring:
        firsts, seconds = (2 * fsdp, 4 * fsdp), (4 * fsdp, 2 * fsdp)
        half_blocks = width // 2 // LANES
        order_end = (2 * fsdp, 4 * fsdp)
        masks = [
            [m ^ side for side in (0, pair) for m in mask_order(o, inner)]
            for o in zip(firsts, seconds)
        ] + [
            [m ^ side ^ k for side in (0, pair) for k in range(inner) for m in mask_order(order_end, 1)]
        ]
        table = jnp.bitwise_xor(jnp.array(masks, jnp.int32), index.astype(jnp.int32))
        away = jnp.bitwise_xor(jnp.arange(count, dtype=jnp.int32), index.astype(jnp.int32))[None]

        def bit(mask, weight):
            return jnp.where(away & jnp.array(mask, jnp.int32)[:, None] != 0, weight, 0)

        places = (
            (away & (inner - 1))
            + bit(firsts, inner)
            + bit(seconds, 2 * inner)
            + bit([pair] * 2, count // 2)
        ).astype(jnp.int32)
        norm_rows = jnp.pad(
            low_norms.reshape(1, 1, 1, 4 * rows), ((0, 1), (0, 0), (0, rows - 1), (0, 0))
        )
        shard = jnp.concatenate([by_columns(low_mats[:3], 2), norm_rows], 1)
        in_size, mid_size = 3 * half_blocks + 1, 2 * half_blocks
        eighth = count // 4
        halves = [
            (h, side * count // 2 + part * eighth)
            for h in range(2)
            for side in range(2)
            for part in range(2)
        ]
        layout_in = tuple((h, start, h * in_size) for h, start in halves)
        layout_out = tuple((h, start, h * mid_size) for h, start in halves)
        layout_out += tuple((2, n * 4, 2 * mid_size) for n in range(2 * inner))

        def ids(size, j):
            return [h * size + j * half_blocks + b for h in range(2) for b in range(half_blocks)]

        blocks_in = [ids(in_size, j) for j in range(3)]
        blocks_out = [ids(mid_size, j) for j in range(2)]
        blocks_out.append([2 * mid_size + b for b in range(2 * half_blocks)])
        norm_block = in_size - 1
        scratch_blocks = (2 * in_size, 2 * mid_size + 2 * half_blocks)

        def near_of(value):
            return [value] + [swap(value, k, count) for k in range(1, inner)]

        def halves_of(near):
            return [jnp.stack([n[h] for n in near]) for h in range(2)]

        def grow(held, taken):
            return [jnp.concatenate(both) for both in zip(held, taken)]

        def with_pairs(held, taken, early):
            late = swap_all(taken, [pair, pair], count)
            return [a for h in range(2) for a in (held[h], taken[h], early[h], late[h])]

        near = near_of(shard)
        end = by_columns(low_mats[5:], 1)
        for mask in order_end:
            end = jnp.concatenate([end, swap(end, mask, count)])
        held = halves_of(after(near, end))
        taken = swap_all(held, firsts, count)
        mid = near_of(after(by_columns(low_mats[3:5], 2), *held))
        held = after(grow(held, taken), *mid)
        end = near_of(after(end, *mid))
        taken = swap_all(held, seconds, count)
        early = swap_all(held, [pair, pair], count)
        mid = halves_of(mid)
        parts_in = with_pairs(held, taken, early)
        norm_vals = []
    else:
        weights_in = lax.all_gather(low_mats[:3], AXES, axis=1, tiled=True)
        weights_out = lax.all_gather(low_mats[3:], AXES, axis=1, tiled=True)
        norm_vals = [lax.all_gather(low_norms, AXES, axis=1, tiled=True).astype(F32)]
        table = places = jnp.zeros((1, 1), jnp.int32)
        rows = width
        parts_in, parts_out = [by_columns(weights_in, 1)], [by_columns(weights_out, 1)]
        layout_in = layout_out = ((0, 0, 0),)
        per = width // LANES
        blocks_in = blocks_out = [list(range(j * per, (j + 1) * per)) for j in range(3)]
        scratch_blocks = (3 * per, 3 * per)
        norm_block = None

    ends = jnp.cumsum(lengths[0, :-1])
    sets = ends.shape[0]
    segment = jnp.sum(
        (jnp.arange(length, dtype=jnp.int32)[:, None] >= ends[None, :]).astype(jnp.int32), axis=1
    )
    live = (segment < sets).astype(F32)[:, None]
    lanes = jnp.arange(LANES, dtype=jnp.int32)[None, :]
    same = segment[:, None] == lanes
    mark_in = same.astype(LOW)
    mark_out = jnp.where(same | (lanes > sets), 0.0, mask_depth).astype(LOW)

    x, dz = latents[0], cotangent[0]
    steps = (length // block,)
    if ring:
        taken = swap_all(mid, firsts, count)
        x = after(x, *mid)
    held_rows = pl.BlockSpec((4, width), lambda i: (0, 0))
    two_rows = pl.BlockSpec((2, width), lambda i: (0, 0))
    anywhere = pl.BlockSpec(memory_space=pl.ANY)
    scratch_in, scratch_out = (pltpu.VMEM((n, width, LANES), LOW) for n in scratch_blocks)
    norm_scratch, sem_scratch = pltpu.VMEM((count, LANES), F32), pltpu.SemaphoreType.DMA
    hidden_one, qkv, norm_vals = pl.pallas_call(
        functools.partial(
            project_kernel, layout_in, rows, blocks_in, norm_block, len(parts_in)
        ),
        grid=steps,
        out_shape=[
            shape((length, width), LOW),
            shape((length, 3 * width), LOW),
            shape((4, width), F32),
        ],
        in_specs=[SMEM, rows_of(x, block)]
        + [anywhere] * len(parts_in)
        + [held_rows] * len(norm_vals),
        out_specs=[
            pl.BlockSpec((block, width), lambda i: (i, 0)),
            pl.BlockSpec((block, 3 * width), lambda i: (i, 0)),
            held_rows,
        ],
        scratch_shapes=[scratch_in, norm_scratch, sem_scratch],
        compiler_params=params(28),
        cost_estimate=cost(6 * length * width * width, 12 * width * width),
    )(table, x, *parts_in, *norm_vals)
    x = latents[0]

    group = 2
    marks = [pl.BlockSpec((length, LANES), lambda h: (0, 0))] * 2

    def heads_at(first):
        return pl.BlockSpec((length, dim * group), lambda h: (0, first // group + h))

    def sums_at(first):
        return pl.BlockSpec((group, 1, length), lambda h: (first // group + h, 0, 0))

    def attend(first, number, qkv):
        return pl.pallas_call(
            functools.partial(attend_kernel, group, dim, power),
            grid=(number // group,),
            in_specs=[heads_at(first + i * HEADS) for i in range(3)] + marks,
            out_specs=[heads_at(0), sums_at(0)],
            out_shape=[shape((length, number * dim), LOW), shape((number, 1, length), F32)],
            compiler_params=params(28),
            cost_estimate=cost(8 * length * length * number * dim, 8 * length * number * dim),
        )(qkv, qkv, qkv, mark_in, mark_out)

    ahead = HEADS // 2
    if ring:
        mid = grow(mid, after(taken, hidden_one))
        taken = swap_all(mid, seconds, count)
        early = swap_all(mid, [pair, pair], count)
        end_late = [swap(e, pair, count) for e in after(end, hidden_one)]
        attended, log_sums = zip(*[attend(f, ahead, after(qkv, *mid)) for f in (0, ahead)])
        parts_out = with_pairs(mid, after(taken, *attended), early) + end + end_late
    else:
        attended, log_sums = zip(*[attend(f, ahead, qkv) for f in (0, ahead)])

    row_block = pl.BlockSpec((block, width), lambda i: (i, 0))
    low_rows = shape((length, width), LOW)
    sides, parts = (2, 2) if ring else (1, 1)
    chunk_shape = (parts, count // sides if ring else 1)
    mat_blocks = width // LANES

    def chunks_of(blocks, extra=0):
        size = blocks // parts + extra
        return [shape((*chunk_shape, size, rows, LANES), LOW)] * sides

    dnorm_two, result, dmid, dattended, *out_grads = pl.pallas_call(
        functools.partial(middle_kernel, layout_out, rows, blocks_out, len(attended), sides),
        grid=steps,
        out_shape=[
            shape((2, width), F32),
            low_rows,
            shape((length, width), F32),
            low_rows,
            *chunks_of(3 * mat_blocks),
        ],
        in_specs=[SMEM, SMEM, row_block, row_block, rows_of(live, block), held_rows]
        + [rows_of(a, block) for a in attended]
        + [anywhere] * len(parts_out),
        out_specs=[two_rows] + [row_block] * 3 + [anywhere] * sides,
        scratch_shapes=[
            scratch_out,
            *[pltpu.VMEM((3, length, width), LOW)] * 2,
            pltpu.VMEM((3 * mat_blocks, width, LANES), LOW),
            sem_scratch,
        ],
        compiler_params=params(50),
        cost_estimate=cost(18 * length * width * width, 24 * width * width),
    )(table, places, x, dz, live, norm_vals, *attended, *parts_out)

    def attend_back(first, number, dattended, base, total, extra=0, prior=()):
        side = first // ahead
        inside = first - side * ahead
        blocks = 3 * group * dim // LANES
        outs = chunks_of(blocks * total, extra)
        return pl.pallas_call(
            functools.partial(
                attend_back_kernel, group, dim, power, scale, base, extra, len(prior)
            ),
            grid=(number // group,),
            in_specs=[SMEM]
            + [heads_at(first + i * HEADS) for i in range(3)]
            + [heads_at(first), heads_at(inside), *marks, sums_at(inside), whole(hidden_one)]
            + [anywhere] * len(prior),
            out_specs=[pl.BlockSpec((3, length, dim * group), lambda h: (0, 0, h))]
            + [anywhere] * sides,
            out_shape=[shape((3, length, number * dim), LOW), *outs],
            input_output_aliases={10 + n: 1 + n for n in range(len(prior))},
            scratch_shapes=[pltpu.VMEM((2 * blocks, width, LANES), LOW), sem_scratch],
            compiler_params=params(34),
            cost_estimate=cost(
                20 * length * length * number * dim + 6 * length * width * number * dim,
                16 * length * number * dim,
            ),
        )(
            places, qkv, qkv, qkv, dattended, attended[side], mark_in, mark_out,
            log_sums[side], hidden_one, *prior,
        )

    def last(dmid, grads, sides):
        packs = [shape((count // max(sides, 1), 1, rows, LANES), LOW)] * sides
        return pl.pallas_call(
            functools.partial(last_kernel, layout_in, rows, blocks_in, len(parts_in), sides),
            grid=steps,
            out_shape=[low_rows, shape((2, width), F32), *packs],
            in_specs=[SMEM, row_block, row_block, held_rows, two_rows]
            + [anywhere] * len(parts_in)
            + [rows_of(g, block) for g in grads],
            out_specs=[row_block, two_rows]
            + [pl.BlockSpec(p.shape, lambda i: (0, 0, 0, 0)) for p in packs],
            scratch_shapes=[scratch_in, norm_scratch, sem_scratch],
            compiler_params=params(28),
            cost_estimate=cost(6 * length * width * width, 6 * width * width),
        )(table, x, dmid, norm_vals, dnorm_two, *parts_in, *grads)

    state, norm_state = (matrices, moment1_mat, moment2_mat), (norm_params, moment1_norm, moment2_norm)
    if ring:
        pairs = range(1, inner)
        heads_w = group * dim

        def slots(firsts, number):
            return slots_of(
                [(j, n * heads_w, heads_w) for n in range(firsts, firsts + number) for j in range(3)], 2
            )

        def from_near(near):
            return [near[0]] + swap_all(near[1:], pairs, count)

        most = HEADS // group - 1
        keep, send = out_grads
        taken = swap(send, pair, count)
        found, *one = attend_back(0, group, after(dattended, keep), 0, most)
        grads = [found]

        sent = far_sums(keep, after(taken, found), [])
        far = [swap_all(sent, seconds, count)]
        for n in range(1, most):
            found, *one = attend_back(
                n * group, group, after(dattended, *sent, found), n, most, 0, one
            )
            grads.append(found)
        keep_one, send_one = one

        sent = far_sums(keep, taken, after(far, keep_one))
        far.append(swap_all(sent, firsts, count))
        taken_one = swap(after(send_one, *sent), pair, count)
        found, keep_two, send_two = attend_back(
            most * group, group, after(dattended, *sent, keep_one), 0, 1, 1
        )
        grads.append(found)

        near = from_near(near_sums(keep, taken, [far[0], after(far[1], grads[-1])], inner))
        sent_one = far_sums(keep_one, after(taken_one, grads[-1]), [])
        far_one = [swap_all(sent_one, seconds, count)]
        grad_latents, dnorm_one, *packs = last(after(dmid, near[0], *sent_one), grads, 2)

        sent_one = far_sums(keep_one, taken_one, after(far_one, grad_latents, *near))
        far_one.append(swap_all(sent_one, firsts, count))
        taken_two, ends = swap_all(after((send_two, packs[1]), *sent_one), [pair, pair], count)
        ends = [packs[0], ends]
        groups = [(range(inner), h, s) for h, s in enumerate(slots_of([(j, 0, width) for j in (3, 4, 5)], 2))]
        prior = lamb_call(3, 3, groups, after(near, *sent_one), state)

        sent_two = far_sums(keep_two, after(taken_two, prior[4]), [], ends)
        far_two = [swap_all(sent_two, seconds, count)]
        near_one = near_sums(
            keep_one, taken_one, [far_one[0], after(far_one[1], *sent_two)], inner
        )
        near_one = from_near(near_one)
        sent_two = far_sums(keep_two, taken_two, after(far_two, near_one[0]), ends)
        far_two.append(swap_all(sent_two, firsts, count))
        near_two = from_near(near_sums(keep_two, taken_two, far_two, inner, ends))
        groups = [(range(inner), h, s) for h, s in enumerate(slots(0, most))]
        groups += [(range(inner, 2 * inner), h, s) for h, s in enumerate(slots(most, 1))]
        norm_ends = (range(inner, 2 * inner), 0)
        found = lamb_call(
            0, 3, groups, [*near_one, *near_two], state, norm_state, norm_ends, prior
        )
        grad_mats, m1_mat, m2_mat, dir_mat, squares, grad_norms, m1_norm, m2_norm, dir_norm = found
        squares = hyper_sum(squares, count)[:2, :10]
    else:
        first, *one = attend_back(0, ahead, dattended, 0, HEADS // group)
        second, in_grads = attend_back(
            ahead, ahead, dattended, ahead // group, HEADS // group, 0, one
        )
        grads = [first, second]
        grad_latents, dnorm_one = last(dmid, grads, 0)
        norms_local = jnp.concatenate([dnorm_one, dnorm_two], 0)
        per = group * dim // LANES
        local = in_grads[0, 0].reshape(HEADS // group, 3, per, width, LANES)
        local = local.transpose(1, 0, 2, 3, 4).reshape(3 * mat_blocks, width, LANES)
        local = jnp.concatenate([local, out_grads[0][0, 0]], 0).astype(F32)
        local = local.reshape(6, mat_blocks, width, LANES)
        local = local.transpose(0, 2, 1, 3).reshape(6, width, width)
        grad_mats = lax.psum_scatter(local, AXES, scatter_dimension=1, tiled=True)
        grad_norms = lax.psum_scatter(norms_local, AXES, scatter_dimension=1, tiled=True)
        m1_mat, m2_mat, dir_mat = lamb_values(matrices, grad_mats, moment1_mat, moment2_mat)
        m1_norm, m2_norm, dir_norm = lamb_values(norm_params, grad_norms, moment1_norm, moment2_norm)
        squares = jnp.stack(
            [
                jnp.concatenate([jnp.sum(m * m, (1, 2)), jnp.sum(n * n, 1)])
                for m, n in ((matrices, norm_params), (dir_mat, dir_norm))
            ]
        )
        squares = lax.psum(squares, AXES)
    ratios = jnp.sqrt(squares[0]) / jnp.sqrt(squares[1])
    scaled_mats = ratios[:6][:, None, None] * dir_mat
    scaled_norms = ratios[6:][:, None] * dir_norm
    return (
        result[None],
        grad_latents[None],
        grad_mats,
        grad_norms,
        scaled_mats,
        scaled_norms,
        m1_mat,
        m2_mat,
        m1_norm,
        m2_norm,
        ratios,
    )


def solution(mesh):
    return jax.shard_map(
        on_device,
        mesh=mesh,
        in_specs=(
            P(("dp", "fsdp"), None, None),
            P(("dp", "fsdp"), None),
            P(("dp", "fsdp"), None, None),
            P(None, ("dp", "fsdp"), None),
            P(None, ("dp", "fsdp")),
            P(None, ("dp", "fsdp"), None),
            P(None, ("dp", "fsdp"), None),
            P(None, ("dp", "fsdp")),
            P(None, ("dp", "fsdp")),
        ),
        out_specs=(
            P(("dp", "fsdp"), None, None),
            P(("dp", "fsdp"), None, None),
            P(None, ("dp", "fsdp"), None),
            P(None, ("dp", "fsdp")),
            P(None, ("dp", "fsdp"), None),
            P(None, ("dp", "fsdp")),
            P(None, ("dp", "fsdp"), None),
            P(None, ("dp", "fsdp"), None),
            P(None, ("dp", "fsdp")),
            P(None, ("dp", "fsdp")),
            P(),
        ),
        check_vma=False,
    )
```

```python
import functools
import math

import jax
import jax.numpy as jnp
from jax import lax
from jax.experimental import pallas as pl
from jax.experimental.pallas import tpu as pltpu
from jax.sharding import PartitionSpec as P

HEADS = 8
AXES = ("dp", "fsdp")
LANES = 128

ln_eps = 1e-05
beta_one = 0.9
beta_two = 0.999
adam_eps = 1e-06
decay_rate = 0.01
adam_step = 100.0
gelu_coef = 0.7978845608
cubic_coef = 0.044715
mask_depth = -1e30

F32 = jnp.float32
LOW = jnp.bfloat16
NT = (((1,), (1,)), ((), ()))
TN = (((0,), (0,)), ((), ()))
SMEM = pl.BlockSpec(memory_space=pltpu.SMEM)
VMEM = pl.BlockSpec(memory_space=pltpu.VMEM)


def params(mib):
    return pltpu.CompilerParams(vmem_limit_bytes=mib * 2**20)


def shape(dims, kind):
    return jax.ShapeDtypeStruct(dims, kind)


def product(left, right, dims=(((1,), (0,)), ((), ()))):
    return lax.dot_general(left, right, dims, preferred_element_type=F32)


def cost(flops, moved):
    return pl.CostEstimate(flops=int(flops), bytes_accessed=int(moved), transcendentals=0)


def whole(array):
    return pl.BlockSpec(
        array.shape, lambda i: (0,) * len(array.shape), pipeline_mode=pl.Buffered(1)
    )


def rows_of(array, block):
    lead = array.shape[:-2]
    return pl.BlockSpec((*lead, block, array.shape[-1]), lambda i: (*(0,) * len(lead), i, 0))


def swap(value, mask, count):
    return lax.ppermute(value, AXES, [(i, i ^ mask) for i in range(count)])


def swap_all(values, bits, count):
    return [swap(v, b, count) for v, b in zip(values, bits)]


def hyper_sum(value, count):
    mask = 1
    while mask < count:
        value = value + swap(value, mask, count)
        mask *= 2
    return value


def after(value, *others):
    return lax.optimization_barrier((value, others))[0]


def mask_order(order, inner):
    masks = list(range(inner))
    for bit in order:
        masks = masks + [m ^ bit for m in masks]
    return masks


def by_columns(shards, parts):
    mats, rows, columns = shards.shape
    blocks = columns // parts // LANES
    split = shards.reshape(mats, rows, parts, blocks, LANES)
    return split.transpose(2, 0, 3, 1, 4).reshape(parts, mats * blocks, rows, LANES)


def normalize(value):
    centered = value - jnp.mean(value, -1, keepdims=True)
    inv_std = lax.rsqrt(jnp.mean(centered * centered, -1, keepdims=True) + ln_eps)
    return centered * inv_std, inv_std


def norm_back(grad_out, normed, inv_std, gain):
    grad_normed = grad_out * gain
    return inv_std * (
        grad_normed
        - jnp.mean(grad_normed, -1, keepdims=True)
        - normed * jnp.mean(grad_normed * normed, -1, keepdims=True)
    )


def place_all(table_ref, layout, rows, refs, weight_ref, sem):
    for (line, start, first), ref in zip(layout, refs):

        @pl.loop(0, ref.shape[0])
        def _(n, line=line, start=start, first=first, ref=ref):
            row = pl.multiple_of(table_ref[line, start + n] * rows, rows)
            target = weight_ref.at[first : first + ref.shape[1], pl.ds(row, rows)]
            pltpu.make_async_copy(ref.at[n], target, sem).start()

    for (_, _, first), ref in zip(layout, refs):
        wait_for(weight_ref.at[first : first + ref.shape[1], 0 : ref.shape[0] * rows], sem)


def wait_for(ref, sem):
    pltpu.make_async_copy(ref, ref, sem).wait()


def matrix(weight_ref, blocks, first=0, size=None):
    size = weight_ref.shape[1] if size is None else size
    return jnp.concatenate([weight_ref[b, first : first + size, :] for b in blocks], 1)


def lane_rows(low, first, number):
    lane = lax.broadcasted_iota(jnp.int32, low, 1)
    return (lane >= first) & (lane < first + number)


def spread_norms(rows, weight_ref, block, held_ref, norm_ref):
    for n in range(held_ref.shape[0]):
        held_ref[n : n + 1, :] = weight_ref[block, n * rows : n * rows + 16, :].astype(F32)[0:1]
    near = LANES // 32
    blocks = held_ref.shape[0] // near
    for i in range(4):
        total = jnp.zeros((blocks, LANES), F32)
        for z in range(near):
            value = held_ref[pl.ds(z, blocks, stride=near), :]
            value = pltpu.roll(value, (32 * (z - i)) % LANES, 1)
            total = total + jnp.where(lane_rows(total.shape, 32 * z, 32), value, 0.0)
        for b in range(blocks):
            norm_ref[i : i + 1, b * LANES : (b + 1) * LANES] = total[b : b + 1]


def pack_norms(norms, held_ref):
    near = LANES // 32
    blocks = held_ref.shape[0] // near
    held = [jnp.zeros((blocks, LANES), F32) for _ in range(near)]
    for i, norm in enumerate(norms):
        stacked = jnp.concatenate(
            [norm[:, b * LANES : (b + 1) * LANES] for b in range(blocks)], 0
        )
        for z in range(near):
            value = pltpu.roll(stacked, (32 * (i - z)) % LANES, 1)
            held[z] = held[z] + jnp.where(lane_rows(value.shape, 32 * i, 32), value, 0.0)
    for z in range(near):
        held_ref[pl.ds(z, blocks, stride=near), :] = held[z]


def project_kernel(layout, rows, blocks, norm_block, parts, table_ref, x_ref, *refs):
    chunks = refs[:parts]
    hidden_ref, out_ref, norm_ref, weight_ref, held_ref, sem = refs[-6:]
    width = x_ref.shape[1]

    @pl.when(pl.program_id(0) == 0)
    def _():
        place_all(table_ref, layout, rows, chunks, weight_ref, sem)
        if norm_block is None:
            norm_ref[...] = refs[parts][...]
        else:
            spread_norms(rows, weight_ref, norm_block, held_ref, norm_ref)

    normed, _ = normalize(x_ref[...].astype(F32))
    hidden = (normed * norm_ref[0:1, :] + norm_ref[1:2, :]).astype(LOW)
    hidden_ref[...] = hidden
    for j, ids in enumerate(blocks):
        out_ref[:, j * width : (j + 1) * width] = product(
            hidden, matrix(weight_ref, ids)
        ).astype(LOW)


def attend_kernel(group, dim, power, q_ref, k_ref, v_ref, in_ref, out_ref, o_ref, lse_ref):
    for g in range(group):
        span = slice(g * dim, (g + 1) * dim)
        keys = jnp.concatenate([k_ref[:, span], out_ref[...]], 1)
        queries = jnp.concatenate([q_ref[:, span], in_ref[...]], 1)
        scores = product(keys, queries, NT)
        top = jnp.max(scores, 0, keepdims=True)
        weight = jnp.exp2((scores - top) * power)
        total = jnp.sum(weight, 0, keepdims=True)
        probs = (weight * (1.0 / total)).astype(LOW)
        o_ref[:, span] = product(v_ref[:, span].T, probs).T.astype(LOW)
        lse_ref[g] = top * power + jnp.log2(total)


def attend_back_kernel(
    group, dim, power, scale, base, extra, prior, pair, place_ref,
    q_ref, k_ref, v_ref, do_ref, o_ref, in_ref, out_ref, lse_ref, hidden_ref, *refs,
):
    grad_ref, *outs = refs[prior:-2]
    held_ref, sem = refs[-2:]
    for g in range(group):
        span = slice(g * dim, (g + 1) * dim)
        queries, keys, grad = q_ref[:, span], k_ref[:, span], do_ref[:, span]
        both = grad.astype(F32) * o_ref[:, span].astype(F32)
        row_dot = lax.dot_general(
            jnp.ones((8, dim), F32), both, NT,
            preferred_element_type=F32, precision=lax.Precision.HIGHEST,
        )[0:1]
        scores = product(
            jnp.concatenate([keys, out_ref[...]], 1),
            jnp.concatenate([queries, in_ref[...]], 1),
            NT,
        )
        probs = jnp.exp2(scores * power - lse_ref[g])
        grad_probs = product(v_ref[:, span], grad, NT)
        grad_scores = (probs * (grad_probs - row_dot)).astype(LOW)
        grad_ref[2, :, span] = product(probs.astype(LOW), grad).astype(LOW)
        grad_ref[1, :, span] = (product(grad_scores, queries) * scale).astype(LOW)
        grad_ref[0, :, span] = (product(keys.T, grad_scores).T * scale).astype(LOW)
    parts = outs[0].shape[0]
    total = held_ref.shape[0] // 2
    size = total // parts
    step = pl.program_id(0)
    slot = lax.rem(step, 2) * total

    @pl.when(step > 1)
    def _():
        wait_rows(held_ref, 0, size, outs, sem)

    for s in range(2):

        @pl.when(slot == s * total)
        def _(s=s):
            weight_grad(
                hidden_ref, [grad_ref[j] for j in range(3)],
                place_ref, held_ref, s * total, outs, (base + step) * size, sem, pair,
            )

    @pl.when(step == pl.num_programs(0) - 1)
    def _():
        wait_rows(held_ref, 0, size, outs, sem)

        @pl.when(step > 0)
        def _():
            wait_rows(held_ref, 0, size, outs, sem)

        if extra:
            empty = held_ref.at[0:1, 0 : outs[0].shape[3]]
            held_ref[0] = jnp.zeros(held_ref.shape[1:], LOW)
            copies = [
                pltpu.make_async_copy(empty, ref.at[h, n, pl.ds(ref.shape[2] - 1, 1)], sem)
                for ref in outs
                for h in range(parts)
                for n in range(ref.shape[1])
            ]
            for copy in copies:
                copy.start()
            for copy in copies:
                copy.wait()


def middle_kernel(
    layout, rows, blocks, atts, sides, pair, table_ref, place_ref, x_ref, dz_ref, live_ref, norm_ref, *refs
):
    att_refs, chunks = refs[:atts], refs[atts : -9 - sides]
    dnorm_ref, result_ref, dmid_ref, datt_ref = refs[-9 - sides : -5 - sides]
    outs, (weight_ref, left_ref, right_ref, held_ref, sem) = refs[-5 - sides : -5], refs[-5:]
    block = x_ref.shape[0]
    here = pl.ds(pl.multiple_of(pl.program_id(0) * block, block), block)

    @pl.when(pl.program_id(0) == 0)
    def _():
        place_all(table_ref, layout, rows, chunks, weight_ref, sem)
        dnorm_ref[...] = jnp.zeros_like(dnorm_ref)

    gain, shift = norm_ref[2:3, :], norm_ref[3:4, :]
    live = live_ref[...]
    branch, first = None, 0
    for ref in att_refs:
        left_ref[0, here, first : first + ref.shape[1]] = ref[...]
        part = product(ref[...], matrix(weight_ref, blocks[0], first, ref.shape[1]))
        branch = part if branch is None else branch + part
        first += ref.shape[1]
    middle = x_ref[...].astype(F32) + live * branch
    normed, inv_std = normalize(middle)
    hidden = (normed * gain + shift).astype(LOW)
    left_ref[1, here, :] = hidden
    upward = product(hidden, matrix(weight_ref, blocks[1]))
    square = upward * upward
    bend = jnp.tanh(gelu_coef * (upward + cubic_coef * square * upward))
    half = 0.5 * (1.0 + bend)
    active = (upward * half).astype(LOW)
    left_ref[2, here, :] = active
    slope = half + (0.5 * gelu_coef) * upward * (1.0 - bend * bend) * (
        1.0 + (3.0 * cubic_coef) * square
    )
    result_ref[...] = (middle + live * product(active, matrix(weight_ref, blocks[2]))).astype(LOW)
    grad = dz_ref[...].astype(F32)
    dmlp = (live * grad).astype(LOW)
    right_ref[2, here, :] = dmlp
    dup = (product(dmlp, matrix(weight_ref, blocks[2]), NT) * slope).astype(LOW)
    right_ref[1, here, :] = dup
    dhidden = product(dup, matrix(weight_ref, blocks[1]), NT)
    dnorm_ref[0:1, :] += jnp.sum(dhidden * normed, 0, keepdims=True)
    dnorm_ref[1:2, :] += jnp.sum(dhidden, 0, keepdims=True)
    dmid = grad + norm_back(dhidden, normed, inv_std, gain)
    dmid_ref[...] = dmid
    dbranch = (live * dmid).astype(LOW)
    right_ref[0, here, :] = dbranch
    datt_ref[...] = product(dbranch, matrix(weight_ref, blocks[0]), NT).astype(LOW)

    @pl.when(pl.program_id(0) == pl.num_programs(0) - 1)
    def _():
        mats = left_ref.shape[0]
        total = held_ref.shape[0] // mats
        size = total // outs[0].shape[0]
        for j in range(mats):
            weight_grad(
                left_ref.at[j], [right_ref[j]], place_ref, held_ref, j * total, outs, j * size, sem,
                pair,
            )
        for j in range(mats):
            wait_rows(held_ref, j * total, size, outs, sem)


def last_kernel(layout, rows, blocks, parts, sides, table_ref, x_ref, dmid_ref, norm_ref, other_ref, *refs):
    chunks, grads = refs[:parts], refs[parts : -5 - sides]
    out_ref, dnorm_ref = refs[-5 - sides : -3 - sides]
    packs, (weight_ref, held_ref, sem) = refs[-3 - sides : -3], refs[-3:]

    @pl.when(pl.program_id(0) == 0)
    def _():
        place_all(table_ref, layout, rows, chunks, weight_ref, sem)
        dnorm_ref[...] = jnp.zeros_like(dnorm_ref)

    total = None
    for j, ids in enumerate(blocks):
        value = jnp.concatenate([ref[j] for ref in grads], 1)
        part = product(value, matrix(weight_ref, ids), NT)
        total = part if total is None else total + part
    normed, inv_std = normalize(x_ref[...].astype(F32))
    dnorm_ref[0:1, :] += jnp.sum(total * normed, 0, keepdims=True)
    dnorm_ref[1:2, :] += jnp.sum(total, 0, keepdims=True)
    out_ref[...] = (
        dmid_ref[...] + norm_back(total, normed, inv_std, norm_ref[0:1, :])
    ).astype(LOW)

    if packs:

        @pl.when(pl.program_id(0) == pl.num_programs(0) - 1)
        def _():
            pack_norms([ref[i : i + 1, :] for ref in (dnorm_ref, other_ref) for i in range(2)], held_ref)
            for side, ref in enumerate(packs):

                @pl.loop(0, ref.shape[0])
                def _(n, ref=ref, side=side):
                    row = held_ref[pl.ds(table_ref[0, side * ref.shape[0] + n], 1), :]
                    ref[n, 0] = jnp.broadcast_to(row, ref.shape[2:]).astype(LOW)


def send_rows(place_ref, held_ref, first, size, outs, block, sem, low, high, pair):
    parts, number, _, rows, _ = outs[0].shape
    chunks = [c for c in range(held_ref.shape[1] // rows) if low < (c + 1) * rows <= high]

    def start(flip):
        for chunk in chunks:
            side = int(bool((chunk ^ chunks[0]) & pair)) ^ flip if len(outs) > 1 else 0
            for h in range(parts):
                at = first + h * size
                source = held_ref.at[at : at + size, chunk * rows : (chunk + 1) * rows]
                place = place_ref[h, chunk] - side * number
                target = outs[side].at[h, place, pl.ds(block, size)]
                pltpu.make_async_copy(source, target, sem).start()

    if not chunks:
        return
    for flip in range(len(outs)):

        @pl.when((place_ref[0, chunks[0]] >= number) == (flip == 1))
        def _(flip=flip):
            start(flip)


def wait_rows(held_ref, first, size, outs, sem):
    wait_for(held_ref.at[first : first + size * outs[0].shape[0]], sem)


def weight_grad(left_ref, rights, place_ref, held_ref, first, outs, block, sem, pair):
    parts = outs[0].shape[0]
    width = left_ref.shape[1]
    step = min(256, width)
    blocks = [r.shape[1] // LANES // parts for r in rights]
    size = sum(blocks)
    for c in range(0, width, step):
        left = left_ref[:, c : c + step]
        at = first
        for right, number in zip(rights, blocks):
            grad = product(left, right, TN).astype(LOW)
            for h in range(parts):
                for b in range(number):
                    lane = (h * number + b) * LANES
                    held_ref[at + h * size + b, c : c + step, :] = grad[:, lane : lane + LANES]
            at += number
        send_rows(place_ref, held_ref, first, size, outs, block, sem, c, c + step, pair)


def slots_of(jobs, parts):
    slots = [[] for _ in range(parts)]
    for which, column, wide in jobs:
        blocks = wide // LANES // parts
        for h in range(parts):
            slots[h] += [(which, column + (h * blocks + b) * LANES) for b in range(blocks)]
    return slots


def sum_kernel(plans, *refs):
    ins, outs = refs[: -len(plans)], refs[-len(plans) :]
    for plan, out in zip(plans, outs):
        for at, terms, ends in plan:
            total = sum(ins[number][entry].astype(F32) for number, entry in terms)
            out[at] = total.astype(out.dtype)
            if ends:
                end = total.shape[0] - 1
                last = total[end:] + sum(ins[n][entry].astype(F32) for n, entry in ends)
                out[at, end:] = last.astype(out.dtype)


def stage_sums(inputs, plans, outs):
    return pl.pallas_call(
        functools.partial(sum_kernel, plans),
        out_shape=outs,
        in_specs=[VMEM] * len(inputs),
        out_specs=[VMEM] * len(outs),
        compiler_params=params(12),
        cost_estimate=cost(0, 2**22),
    )(*inputs)


def terms_of(parts, earlier, h, entry):
    return [(0, (h, entry)), (1, (h, entry))] + [
        (2 + parts * e + h, entry) for e in range(earlier)
    ]


def far_sums(keep, taken, earlier, ends=()):
    parts, chunks, *block = keep.shape
    half = chunks // 2 ** (len(earlier) + 1)
    base = 2 + parts * len(earlier)
    plans = [
        [
            (
                n,
                terms_of(parts, len(earlier), h, half + n),
                [(base + e, half + n) for e in range(len(ends))] if h == 0 else [],
            )
            for n in range(half)
        ]
        for h in range(parts)
    ]
    outs = [shape((half, *block), LOW)] * parts
    return stage_sums([keep, taken, *[t for e in earlier for t in e], *ends], plans, outs)


def near_sums(keep, taken, earlier, inner, ends=()):
    parts, _, *block = keep.shape
    base = 2 + parts * len(earlier)
    plans = [
        [
            (
                h,
                terms_of(parts, len(earlier), h, k),
                [(base + e, k) for e in range(len(ends))] if h == 0 else [],
            )
            for h in range(parts)
        ]
        for k in range(inner)
    ]
    outs = [shape((parts, *block), F32 if k == 0 else LOW) for k in range(inner)]
    return stage_sums([keep, taken, *[t for e in earlier for t in e], *ends], plans, outs)


def lamb_values(weight, grad, first, second):
    m_one = beta_one * first + (1.0 - beta_one) * grad
    m_two = beta_two * second + (1.0 - beta_two) * grad * grad
    step_dir = (
        m_one
        / (1.0 - beta_one**adam_step)
        / (jnp.sqrt(m_two / (1.0 - beta_two**adam_step)) + adam_eps)
        + decay_rate * weight
    )
    return m_one, m_two, step_dir


def whole_sum(value):
    return jnp.sum(jnp.sum(value, 0, keepdims=True), 1, keepdims=True)


def lamb_kernel(base, mats, groups, terms, norm_ends, prior, *refs):
    weight_ref, one_ref, two_ref = refs[:3]
    norm_refs = refs[3:6] if norm_ends else ()
    first = 3 + len(norm_refs)
    term_refs = refs[first : first + terms]
    prior_refs = refs[first + terms : first + terms + prior]
    outs = refs[first + terms + prior :]
    rows = weight_ref.shape[1]
    lane = lax.broadcasted_iota(jnp.int32, (8, LANES), 1)
    line = lax.broadcasted_iota(jnp.int32, (8, LANES), 0)
    squares = jnp.zeros((8, LANES), F32)
    weight_sq = [jnp.zeros((1, LANES), F32)] * mats
    update_sq = [jnp.zeros((1, LANES), F32)] * mats
    for used, entry, slots in groups:
        for at, (which, column) in enumerate(slots):
            grad = sum(term_refs[t][entry, at].astype(F32) for t in used)
            span = slice(column, column + LANES)
            weight = weight_ref[which, :, span]
            m_one, m_two, step = lamb_values(
                weight, grad, one_ref[which, :, span], two_ref[which, :, span]
            )
            j = which - base
            for ref, value in zip(outs, (grad, m_one, m_two, step)):
                ref[j, :, span] = value
            weight_sq[j] += jnp.sum(weight * weight, 0, keepdims=True)
            update_sq[j] += jnp.sum(step * step, 0, keepdims=True)
    for j in range(mats):
        spot = lane == base + j
        squares += jnp.where(spot & (line == 0), jnp.sum(weight_sq[j], 1, keepdims=True), 0.0)
        squares += jnp.where(spot & (line == 1), jnp.sum(update_sq[j], 1, keepdims=True), 0.0)
    if prior:
        for ref, old in zip(outs[:4], prior_refs[:4]):
            ref[mats:] = old[...]
        squares += prior_refs[4][...]
    if norm_ends:
        used, entry = norm_ends
        last = term_refs[used[0]].shape[1] - 1
        row = sum(term_refs[t][entry, last].astype(F32)[0:1] for t in used)
        for i in range(4):
            weight = norm_refs[0][i : i + 1, :]
            grad = row[:, i * rows : (i + 1) * rows]
            m_one, m_two, step = lamb_values(
                weight, grad, norm_refs[1][i : i + 1, :], norm_refs[2][i : i + 1, :]
            )
            for ref, value in zip(outs[5:], (grad, m_one, m_two, step)):
                ref[i : i + 1, :] = value
            spot = lane == 6 + i
            squares += jnp.where(spot & (line == 0), whole_sum(weight * weight), 0.0)
            squares += jnp.where(spot & (line == 1), whole_sum(step * step), 0.0)
    outs[4][...] = squares


def lamb_call(base, mats, groups, terms, state, norm_state=(), norm_ends=None, prior=()):
    total, rows, width = state[0].shape
    outs = [shape((total if prior else mats, rows, width), F32)] * 4 + [shape((8, LANES), F32)]
    if norm_ends:
        outs += [shape(norm_state[0].shape, F32)] * 4
    inputs = [*state, *norm_state, *terms, *prior]
    return pl.pallas_call(
        functools.partial(lamb_kernel, base, mats, groups, len(terms), norm_ends, len(prior)),
        out_shape=outs,
        in_specs=[VMEM] * len(inputs),
        out_specs=[VMEM] * len(outs),
        compiler_params=params(12),
        cost_estimate=cost(0, 2**22),
    )(*inputs)


def on_device(
    latents,
    lengths,
    cotangent,
    matrices,
    norm_params,
    moment1_mat,
    moment2_mat,
    moment1_norm,
    moment2_norm,
):
    _, length, width = latents.shape
    dim = width // HEADS
    scale = 1.0 / math.sqrt(dim)
    power = scale * math.log2(math.e)
    dp, fsdp = lax.axis_size("dp"), lax.axis_size("fsdp")
    count = dp * fsdp
    rows = matrices.shape[1]
    index = lax.axis_index("dp") * fsdp + lax.axis_index("fsdp")
    ring = dp == 8 and fsdp == 4 and rows == 32
    inner, pair = fsdp, fsdp
    block = 256 if length % 256 == 0 else length
    low_mats = matrices.astype(LOW)
    low_norms = norm_params.astype(LOW)

    if ring:
        firsts, seconds = (2 * fsdp, 4 * fsdp), (4 * fsdp, 2 * fsdp)
        half_blocks = width // 2 // LANES
        order_end = (2 * fsdp, 4 * fsdp)
        masks = [
            [m ^ side for side in (0, pair) for m in mask_order(o, inner)]
            for o in zip(firsts, seconds)
        ] + [
            [m ^ side ^ k for side in (0, pair) for k in range(inner) for m in mask_order(order_end, 1)]
        ]
        table = jnp.bitwise_xor(jnp.array(masks, jnp.int32), index.astype(jnp.int32))
        away = jnp.bitwise_xor(jnp.arange(count, dtype=jnp.int32), index.astype(jnp.int32))[None]

        def bit(mask, weight):
            return jnp.where(away & jnp.array(mask, jnp.int32)[:, None] != 0, weight, 0)

        places = (
            (away & (inner - 1))
            + bit(firsts, inner)
            + bit(seconds, 2 * inner)
            + bit([pair] * 2, count // 2)
        ).astype(jnp.int32)
        norm_rows = jnp.pad(
            low_norms.reshape(1, 1, 1, 4 * rows), ((0, 1), (0, 0), (0, rows - 1), (0, 0))
        )
        shard = jnp.concatenate([by_columns(low_mats[:3], 2), norm_rows], 1)
        in_size, mid_size = 3 * half_blocks + 1, 2 * half_blocks
        eighth = count // 4
        halves = [
            (h, side * count // 2 + part * eighth)
            for h in range(2)
            for side in range(2)
            for part in range(2)
        ]
        layout_in = tuple((h, start, h * in_size) for h, start in halves)
        layout_out = tuple((h, start, h * mid_size) for h, start in halves)
        layout_out += tuple((2, n * 4, 2 * mid_size) for n in range(2 * inner))

        def ids(size, j):
            return [h * size + j * half_blocks + b for h in range(2) for b in range(half_blocks)]

        blocks_in = [ids(in_size, j) for j in range(3)]
        blocks_out = [ids(mid_size, j) for j in range(2)]
        blocks_out.append([2 * mid_size + b for b in range(2 * half_blocks)])
        norm_block = in_size - 1
        scratch_blocks = (2 * in_size, 2 * mid_size + 2 * half_blocks)

        def near_of(value):
            return [value] + [swap(value, k, count) for k in range(1, inner)]

        def halves_of(near):
            return [jnp.stack([n[h] for n in near]) for h in range(2)]

        def grow(held, taken):
            return [jnp.concatenate(both) for both in zip(held, taken)]

        def with_pairs(held, taken, early):
            late = swap_all(taken, [pair, pair], count)
            return [a for h in range(2) for a in (held[h], taken[h], early[h], late[h])]

        near = near_of(shard)
        end = by_columns(low_mats[5:], 1)
        end = jnp.concatenate([end, swap(end, order_end[0], count)])
        held = halves_of(after(near, end))
        taken = swap_all(held, firsts, count)
        end = jnp.concatenate([end, swap(after(end, *held), order_end[1], count)])
        held = grow(held, after(taken, end))
        taken = swap_all(held, seconds, count)
        early = swap_all(held, [pair, pair], count)
        mid = near_of(after(by_columns(low_mats[3:5], 2), *held))
        late = swap_all(after(taken, *mid), [pair, pair], count)
        parts_in = [a for h in range(2) for a in (held[h], taken[h], early[h], late[h])]
        mid = halves_of(mid)
        end = near_of(after(end, *mid))
        norm_vals = []
    else:
        weights_in = lax.all_gather(low_mats[:3], AXES, axis=1, tiled=True)
        weights_out = lax.all_gather(low_mats[3:], AXES, axis=1, tiled=True)
        norm_vals = [lax.all_gather(low_norms, AXES, axis=1, tiled=True).astype(F32)]
        table = places = jnp.zeros((1, 1), jnp.int32)
        rows = width
        parts_in, parts_out = [by_columns(weights_in, 1)], [by_columns(weights_out, 1)]
        layout_in = layout_out = ((0, 0, 0),)
        per = width // LANES
        blocks_in = blocks_out = [list(range(j * per, (j + 1) * per)) for j in range(3)]
        scratch_blocks = (3 * per, 3 * per)
        norm_block = None

    ends = jnp.cumsum(lengths[0, :-1])
    sets = ends.shape[0]
    segment = jnp.sum(
        (jnp.arange(length, dtype=jnp.int32)[:, None] >= ends[None, :]).astype(jnp.int32), axis=1
    )
    live = (segment < sets).astype(F32)[:, None]
    lanes = jnp.arange(LANES, dtype=jnp.int32)[None, :]
    same = segment[:, None] == lanes
    mark_in = same.astype(LOW)
    mark_out = jnp.where(same | (lanes > sets), 0.0, mask_depth).astype(LOW)

    x, dz = latents[0], cotangent[0]
    steps = (length // block,)
    if ring:
        taken = swap_all(mid, firsts, count)
        x = after(x, *mid)
    held_rows = pl.BlockSpec((4, width), lambda i: (0, 0))
    two_rows = pl.BlockSpec((2, width), lambda i: (0, 0))
    anywhere = pl.BlockSpec(memory_space=pl.ANY)
    scratch_in, scratch_out = (pltpu.VMEM((n, width, LANES), LOW) for n in scratch_blocks)
    norm_scratch, sem_scratch = pltpu.VMEM((count, LANES), F32), pltpu.SemaphoreType.DMA
    hidden_one, qkv, norm_vals = pl.pallas_call(
        functools.partial(
            project_kernel, layout_in, rows, blocks_in, norm_block, len(parts_in)
        ),
        grid=steps,
        out_shape=[
            shape((length, width), LOW),
            shape((length, 3 * width), LOW),
            shape((4, width), F32),
        ],
        in_specs=[SMEM, rows_of(x, block)]
        + [anywhere] * len(parts_in)
        + [held_rows] * len(norm_vals),
        out_specs=[
            pl.BlockSpec((block, width), lambda i: (i, 0)),
            pl.BlockSpec((block, 3 * width), lambda i: (i, 0)),
            held_rows,
        ],
        scratch_shapes=[scratch_in, norm_scratch, sem_scratch],
        compiler_params=params(18),
        cost_estimate=cost(6 * length * width * width, 12 * width * width),
    )(table, x, *parts_in, *norm_vals)
    x = latents[0]

    group = 2
    marks = [pl.BlockSpec((length, LANES), lambda h: (0, 0))] * 2

    def heads_at(first):
        return pl.BlockSpec((length, dim * group), lambda h: (0, first // group + h))

    def sums_at(first):
        return pl.BlockSpec((group, 1, length), lambda h: (first // group + h, 0, 0))

    def attend(first, number, qkv):
        return pl.pallas_call(
            functools.partial(attend_kernel, group, dim, power),
            grid=(number // group,),
            in_specs=[heads_at(first + i * HEADS) for i in range(3)] + marks,
            out_specs=[heads_at(0), sums_at(0)],
            out_shape=[shape((length, number * dim), LOW), shape((number, 1, length), F32)],
            compiler_params=params(14),
            cost_estimate=cost(8 * length * length * number * dim, 8 * length * number * dim),
        )(qkv, qkv, qkv, mark_in, mark_out)

    ahead = HEADS // 2
    if ring:
        mid = grow(mid, after(taken, hidden_one))
        taken = swap_all(mid, seconds, count)
        early = swap_all(mid, [pair, pair], count)
        attended, log_sums = zip(*[attend(f, ahead, after(qkv, *mid)) for f in (0, ahead)])
        end_late = [swap(e, pair, count) for e in after(end, attended[0])]
        parts_out = with_pairs(mid, after(taken, *attended), early) + end + end_late
    else:
        attended, log_sums = zip(*[attend(f, ahead, qkv) for f in (0, ahead)])

    row_block = pl.BlockSpec((block, width), lambda i: (i, 0))
    low_rows = shape((length, width), LOW)
    sides, parts = (2, 2) if ring else (1, 1)
    chunk_shape = (parts, count // sides if ring else 1)
    mat_blocks = width // LANES

    def chunks_of(blocks, extra=0):
        size = blocks // parts + extra
        return [shape((*chunk_shape, size, rows, LANES), LOW)] * sides

    dnorm_two, result, dmid, dattended, *out_grads = pl.pallas_call(
        functools.partial(
            middle_kernel, layout_out, rows, blocks_out, len(attended), sides, pair
        ),
        grid=steps,
        out_shape=[
            shape((2, width), F32),
            low_rows,
            shape((length, width), F32),
            low_rows,
            *chunks_of(3 * mat_blocks),
        ],
        in_specs=[SMEM, SMEM, row_block, row_block, rows_of(live, block), held_rows]
        + [rows_of(a, block) for a in attended]
        + [anywhere] * len(parts_out),
        out_specs=[two_rows] + [row_block] * 3 + [anywhere] * sides,
        scratch_shapes=[
            scratch_out,
            *[pltpu.VMEM((3, length, width), LOW)] * 2,
            pltpu.VMEM((3 * mat_blocks, width, LANES), LOW),
            sem_scratch,
        ],
        compiler_params=params(42),
        cost_estimate=cost(18 * length * width * width, 24 * width * width),
    )(table, places, x, dz, live, norm_vals, *attended, *parts_out)

    def attend_back(first, number, dattended, base, total, extra=0, prior=()):
        side = first // ahead
        inside = first - side * ahead
        blocks = 3 * group * dim // LANES
        outs = chunks_of(blocks * total, extra)
        return pl.pallas_call(
            functools.partial(
                attend_back_kernel, group, dim, power, scale, base, extra, len(prior), pair
            ),
            grid=(number // group,),
            in_specs=[SMEM]
            + [heads_at(first + i * HEADS) for i in range(3)]
            + [heads_at(first), heads_at(inside), *marks, sums_at(inside), whole(hidden_one)]
            + [anywhere] * len(prior),
            out_specs=[pl.BlockSpec((3, length, dim * group), lambda h: (0, 0, h))]
            + [anywhere] * sides,
            out_shape=[shape((3, length, number * dim), LOW), *outs],
            input_output_aliases={10 + n: 1 + n for n in range(len(prior))},
            scratch_shapes=[pltpu.VMEM((2 * blocks, width, LANES), LOW), sem_scratch],
            compiler_params=params(20),
            cost_estimate=cost(
                20 * length * length * number * dim + 6 * length * width * number * dim,
                16 * length * number * dim,
            ),
        )(
            places, qkv, qkv, qkv, dattended, attended[side], mark_in, mark_out,
            log_sums[side], hidden_one, *prior,
        )

    def last(dmid, grads, sides):
        packs = [shape((count // max(sides, 1), 1, rows, LANES), LOW)] * sides
        return pl.pallas_call(
            functools.partial(last_kernel, layout_in, rows, blocks_in, len(parts_in), sides),
            grid=steps,
            out_shape=[low_rows, shape((2, width), F32), *packs],
            in_specs=[SMEM, row_block, row_block, held_rows, two_rows]
            + [anywhere] * len(parts_in)
            + [rows_of(g, block) for g in grads],
            out_specs=[row_block, two_rows]
            + [pl.BlockSpec(p.shape, lambda i: (0, 0, 0, 0)) for p in packs],
            scratch_shapes=[scratch_in, norm_scratch, sem_scratch],
            compiler_params=params(18),
            cost_estimate=cost(6 * length * width * width, 6 * width * width),
        )(table, x, dmid, norm_vals, dnorm_two, *parts_in, *grads)

    state, norm_state = (matrices, moment1_mat, moment2_mat), (norm_params, moment1_norm, moment2_norm)
    if ring:
        pairs = range(1, inner)
        heads_w = group * dim

        def slots(firsts, number):
            return slots_of(
                [(j, n * heads_w, heads_w) for n in range(firsts, firsts + number) for j in range(3)], 2
            )

        def from_near(near):
            return [near[0]] + swap_all(near[1:], pairs, count)

        per = ahead // group
        keep, send = out_grads
        taken = swap(send, pair, count)
        found, *one = attend_back(0, group, after(dattended, keep), 0, per)
        grads = [found]

        sent = far_sums(keep, after(taken, found), [])
        far = [swap_all(sent, seconds, count)]
        found, keep_one, send_one = attend_back(
            group, group, after(dattended, *sent, found), 1, per, 0, one
        )
        grads.append(found)
        found, *two = attend_back(ahead, group, after(dattended, found, keep_one), 0, per, 1)
        grads.append(found)

        sent = far_sums(keep, taken, after(far, found))
        far.append(swap_all(sent, firsts, count))
        taken_one = swap(after(send_one, *sent), pair, count)
        found, keep_two, send_two = attend_back(
            ahead + group, group, after(dattended, *sent, found), 1, per, 1, two
        )
        grads.append(found)

        near = from_near(near_sums(keep, taken, [far[0], after(far[1], grads[-1])], inner))
        sent_one = far_sums(keep_one, after(taken_one, grads[-1]), [])
        far_one = [swap_all(sent_one, seconds, count)]
        grad_latents, dnorm_one, *packs = last(after(dmid, near[0], *sent_one), grads, 2)

        sent_one = far_sums(keep_one, taken_one, after(far_one, grad_latents, *near))
        far_one.append(swap_all(sent_one, firsts, count))
        taken_two, ends = swap_all(after((send_two, packs[1]), *sent_one), [pair, pair], count)
        ends = [packs[0], ends]
        groups = [(range(inner), h, s) for h, s in enumerate(slots_of([(j, 0, width) for j in (3, 4, 5)], 2))]
        prior = lamb_call(3, 3, groups, after(near, *sent_one), state)

        far_one, taken_two, ends = after((far_one, taken_two, ends), prior[4], far_one, taken_two, ends)
        near_one = near_sums(keep_one, taken_one, far_one, inner)
        sent_two = far_sums(keep_two, taken_two, [], ends)
        near_one, sent_two = after((near_one, sent_two), near_one, sent_two)
        near_one = from_near(near_one)
        far_two = [swap_all(sent_two, seconds, count)]
        sent_two = far_sums(keep_two, taken_two, after(far_two, *near_one), ends)
        far_two.append(swap_all(sent_two, firsts, count))
        near_two = from_near(near_sums(keep_two, taken_two, far_two, inner, ends))
        groups = [(range(inner), h, s) for h, s in enumerate(slots(0, per))]
        groups += [(range(inner, 2 * inner), h, s) for h, s in enumerate(slots(per, per))]
        norm_ends = (range(inner, 2 * inner), 0)
        found = lamb_call(
            0, 3, groups, [*near_one, *near_two], state, norm_state, norm_ends, prior
        )
        grad_mats, m1_mat, m2_mat, dir_mat, squares, grad_norms, m1_norm, m2_norm, dir_norm = found
        squares = hyper_sum(squares, count)[:2, :10]
    else:
        first, *one = attend_back(0, ahead, dattended, 0, HEADS // group)
        second, in_grads = attend_back(
            ahead, ahead, dattended, ahead // group, HEADS // group, 0, one
        )
        grads = [first, second]
        grad_latents, dnorm_one = last(dmid, grads, 0)
        norms_local = jnp.concatenate([dnorm_one, dnorm_two], 0)
        per = group * dim // LANES
        local = in_grads[0, 0].reshape(HEADS // group, 3, per, width, LANES)
        local = local.transpose(1, 0, 2, 3, 4).reshape(3 * mat_blocks, width, LANES)
        local = jnp.concatenate([local, out_grads[0][0, 0]], 0).astype(F32)
        local = local.reshape(6, mat_blocks, width, LANES)
        local = local.transpose(0, 2, 1, 3).reshape(6, width, width)
        grad_mats = lax.psum_scatter(local, AXES, scatter_dimension=1, tiled=True)
        grad_norms = lax.psum_scatter(norms_local, AXES, scatter_dimension=1, tiled=True)
        m1_mat, m2_mat, dir_mat = lamb_values(matrices, grad_mats, moment1_mat, moment2_mat)
        m1_norm, m2_norm, dir_norm = lamb_values(norm_params, grad_norms, moment1_norm, moment2_norm)
        squares = jnp.stack(
            [
                jnp.concatenate([jnp.sum(m * m, (1, 2)), jnp.sum(n * n, 1)])
                for m, n in ((matrices, norm_params), (dir_mat, dir_norm))
            ]
        )
        squares = lax.psum(squares, AXES)
    ratios = jnp.sqrt(squares[0]) / jnp.sqrt(squares[1])
    scaled_mats = ratios[:6][:, None, None] * dir_mat
    scaled_norms = ratios[6:][:, None] * dir_norm
    return (
        result[None],
        grad_latents[None],
        grad_mats,
        grad_norms,
        scaled_mats,
        scaled_norms,
        m1_mat,
        m2_mat,
        m1_norm,
        m2_norm,
        ratios,
    )


def solution(mesh):
    return jax.shard_map(
        on_device,
        mesh=mesh,
        in_specs=(
            P(("dp", "fsdp"), None, None),
            P(("dp", "fsdp"), None),
            P(("dp", "fsdp"), None, None),
            P(None, ("dp", "fsdp"), None),
            P(None, ("dp", "fsdp")),
            P(None, ("dp", "fsdp"), None),
            P(None, ("dp", "fsdp"), None),
            P(None, ("dp", "fsdp")),
            P(None, ("dp", "fsdp")),
        ),
        out_specs=(
            P(("dp", "fsdp"), None, None),
            P(("dp", "fsdp"), None, None),
            P(None, ("dp", "fsdp"), None),
            P(None, ("dp", "fsdp")),
            P(None, ("dp", "fsdp"), None),
            P(None, ("dp", "fsdp")),
            P(None, ("dp", "fsdp"), None),
            P(None, ("dp", "fsdp"), None),
            P(None, ("dp", "fsdp")),
            P(None, ("dp", "fsdp")),
            P(),
        ),
        check_vma=False,
    )
```

```python
import functools
import math

import jax
import jax.numpy as jnp
from jax import lax
from jax.experimental import pallas as pl
from jax.experimental.pallas import tpu as pltpu
from jax.sharding import PartitionSpec as P

HEADS = 8
AXES = ("dp", "fsdp")
LANES = 128

ln_eps = 1e-05
beta_one = 0.9
beta_two = 0.999
adam_eps = 1e-06
decay_rate = 0.01
adam_step = 100.0
gelu_coef = 0.7978845608
cubic_coef = 0.044715
mask_depth = -1e30

F32 = jnp.float32
LOW = jnp.bfloat16
NT = (((1,), (1,)), ((), ()))
TN = (((0,), (0,)), ((), ()))
SMEM = pl.BlockSpec(memory_space=pltpu.SMEM)
VMEM = pl.BlockSpec(memory_space=pltpu.VMEM)


def params(mib):
    return pltpu.CompilerParams(vmem_limit_bytes=mib * 2**20)


def shape(dims, kind):
    return jax.ShapeDtypeStruct(dims, kind)


def product(left, right, dims=(((1,), (0,)), ((), ()))):
    return lax.dot_general(left, right, dims, preferred_element_type=F32)


def cost(flops, moved):
    return pl.CostEstimate(flops=int(flops), bytes_accessed=int(moved), transcendentals=0)


def whole(array):
    return pl.BlockSpec(
        array.shape, lambda i: (0,) * len(array.shape), pipeline_mode=pl.Buffered(1)
    )


def rows_of(array, block):
    lead = array.shape[:-2]
    return pl.BlockSpec((*lead, block, array.shape[-1]), lambda i: (*(0,) * len(lead), i, 0))


def swap(value, mask, count):
    return lax.ppermute(value, AXES, [(i, i ^ mask) for i in range(count)])


def swap_all(values, bits, count):
    return [swap(v, b, count) for v, b in zip(values, bits)]


def hyper_sum(value, count):
    mask = 1
    while mask < count:
        value = value + swap(value, mask, count)
        mask *= 2
    return value


def after(value, *others):
    return lax.optimization_barrier((value, others))[0]


def mask_order(order, inner):
    masks = list(range(inner))
    for bit in order:
        masks = masks + [m ^ bit for m in masks]
    return masks


def by_columns(shards, parts):
    mats, rows, columns = shards.shape
    blocks = columns // parts // LANES
    split = shards.reshape(mats, rows, parts, blocks, LANES)
    return split.transpose(2, 0, 3, 1, 4).reshape(parts, mats * blocks, rows, LANES)


def normalize(value):
    centered = value - jnp.mean(value, -1, keepdims=True)
    inv_std = lax.rsqrt(jnp.mean(centered * centered, -1, keepdims=True) + ln_eps)
    return centered * inv_std, inv_std


def norm_back(grad_out, normed, inv_std, gain):
    grad_normed = grad_out * gain
    return inv_std * (
        grad_normed
        - jnp.mean(grad_normed, -1, keepdims=True)
        - normed * jnp.mean(grad_normed * normed, -1, keepdims=True)
    )


def pieces_of(ref, rows):
    number, height = ref.shape[1:3]
    if height == rows:
        return [(0, number, 0, 0)]
    blocks = number // 2
    return [(0, blocks, 0, 0), (blocks, blocks, 0, height), (number - 1, 1, blocks, 0)]


def place_start(table_ref, layout, rows, refs, weight_ref, sem):
    for (line, start, first), ref in zip(layout, refs):

        @pl.loop(0, ref.shape[0])
        def _(n, line=line, start=start, first=first, ref=ref):
            row = pl.multiple_of(table_ref[line, start + n] * rows, rows)
            for at, number, block, lower in pieces_of(ref, rows):
                block += first
                target = weight_ref.at[block : block + number, pl.ds(row + lower, ref.shape[2])]
                pltpu.make_async_copy(ref.at[n, at : at + number], target, sem).start()


def place_wait(layout, rows, refs, weight_ref, sem):
    for (_, _, first), ref in zip(layout, refs):
        for _, number, block, _ in pieces_of(ref, rows):
            block += first
            wait_for(weight_ref.at[block : block + number, 0 : ref.shape[0] * ref.shape[2]], sem)


def wait_for(ref, sem):
    pltpu.make_async_copy(ref, ref, sem).wait()


def matrix(weight_ref, blocks, first=0, size=None):
    size = weight_ref.shape[1] if size is None else size
    return jnp.concatenate([weight_ref[b, first : first + size, :] for b in blocks], 1)


def lane_rows(low, first, number):
    lane = lax.broadcasted_iota(jnp.int32, low, 1)
    return (lane >= first) & (lane < first + number)


def spread_norms(rows, weight_ref, block, held_ref, norm_ref):
    for n in range(held_ref.shape[0]):
        held_ref[n : n + 1, :] = weight_ref[block, n * rows : n * rows + 16, :].astype(F32)[0:1]
    near = LANES // 32
    blocks = held_ref.shape[0] // near
    for i in range(4):
        total = jnp.zeros((blocks, LANES), F32)
        for z in range(near):
            value = held_ref[pl.ds(z, blocks, stride=near), :]
            value = pltpu.roll(value, (32 * (z - i)) % LANES, 1)
            total = total + jnp.where(lane_rows(total.shape, 32 * z, 32), value, 0.0)
        for b in range(blocks):
            norm_ref[i : i + 1, b * LANES : (b + 1) * LANES] = total[b : b + 1]


def pack_norms(norms, held_ref):
    near = LANES // 32
    blocks = held_ref.shape[0] // near
    held = [jnp.zeros((blocks, LANES), F32) for _ in range(near)]
    for i, norm in enumerate(norms):
        stacked = jnp.concatenate(
            [norm[:, b * LANES : (b + 1) * LANES] for b in range(blocks)], 0
        )
        for z in range(near):
            value = pltpu.roll(stacked, (32 * (i - z)) % LANES, 1)
            held[z] = held[z] + jnp.where(lane_rows(value.shape, 32 * i, 32), value, 0.0)
    for z in range(near):
        held_ref[pl.ds(z, blocks, stride=near), :] = held[z]


def project_kernel(layout, rows, blocks, norm_block, parts, table_ref, x_ref, *refs):
    chunks = refs[:parts]
    hidden_ref, out_ref, norm_ref, weight_ref, held_ref, sem = refs[-6:]
    width = x_ref.shape[1]

    @pl.when(pl.program_id(0) == 0)
    def _():
        place_start(table_ref, layout, rows, chunks, weight_ref, sem)

    normed, _ = normalize(x_ref[...].astype(F32))

    @pl.when(pl.program_id(0) == 0)
    def _():
        place_wait(layout, rows, chunks, weight_ref, sem)
        if norm_block is None:
            norm_ref[...] = refs[parts][...]
        else:
            spread_norms(rows, weight_ref, norm_block, held_ref, norm_ref)

    hidden = (normed * norm_ref[0:1, :] + norm_ref[1:2, :]).astype(LOW)
    hidden_ref[...] = hidden
    for j, ids in enumerate(blocks):
        out_ref[:, j * width : (j + 1) * width] = product(
            hidden, matrix(weight_ref, ids)
        ).astype(LOW)


def attend_kernel(group, dim, power, q_ref, k_ref, v_ref, in_ref, out_ref, o_ref, lse_ref):
    for g in range(group):
        span = slice(g * dim, (g + 1) * dim)
        keys = jnp.concatenate([k_ref[:, span], out_ref[...]], 1)
        queries = jnp.concatenate([q_ref[:, span], in_ref[...]], 1)
        scores = product(keys, queries, NT)
        top = jnp.max(scores, 0, keepdims=True)
        weight = jnp.exp2((scores - top) * power)
        total = jnp.sum(weight, 0, keepdims=True)
        probs = (weight * (1.0 / total)).astype(LOW)
        o_ref[:, span] = product(v_ref[:, span].T, probs).T.astype(LOW)
        lse_ref[g] = top * power + jnp.log2(total)


def attend_back_kernel(
    group, dim, power, scale, base, extra, prior, pair, place_ref,
    q_ref, k_ref, v_ref, do_ref, o_ref, in_ref, out_ref, lse_ref, hidden_ref, *refs,
):
    grad_ref, *outs = refs[prior:-2]
    held_ref, sem = refs[-2:]
    for g in range(group):
        span = slice(g * dim, (g + 1) * dim)
        queries, keys, grad = q_ref[:, span], k_ref[:, span], do_ref[:, span]
        both = grad.astype(F32) * o_ref[:, span].astype(F32)
        row_dot = lax.dot_general(
            jnp.ones((8, dim), F32), both, NT,
            preferred_element_type=F32, precision=lax.Precision.HIGHEST,
        )[0:1]
        scores = product(
            jnp.concatenate([keys, out_ref[...]], 1),
            jnp.concatenate([queries, in_ref[...]], 1),
            NT,
        )
        probs = jnp.exp2(scores * power - lse_ref[g])
        grad_probs = product(v_ref[:, span], grad, NT)
        grad_scores = (probs * (grad_probs - row_dot)).astype(LOW)
        grad_ref[2, :, span] = product(probs.astype(LOW), grad).astype(LOW)
        grad_ref[1, :, span] = (product(grad_scores, queries) * scale).astype(LOW)
        grad_ref[0, :, span] = (product(keys.T, grad_scores).T * scale).astype(LOW)
    parts = outs[0].shape[0]
    total = held_ref.shape[0] // 2
    size = total // parts
    step = pl.program_id(0)
    slot = lax.rem(step, 2) * total

    @pl.when(step > 1)
    def _():
        wait_rows(held_ref, 0, size, outs, sem)

    for s in range(2):

        @pl.when(slot == s * total)
        def _(s=s):
            weight_grad(
                hidden_ref, [grad_ref[j] for j in range(3)],
                place_ref, held_ref, s * total, outs, (base + step) * size, sem, pair,
            )

    @pl.when(step == pl.num_programs(0) - 1)
    def _():
        wait_rows(held_ref, 0, size, outs, sem)

        @pl.when(step > 0)
        def _():
            wait_rows(held_ref, 0, size, outs, sem)

        if extra:
            empty = held_ref.at[0:1, 0 : outs[0].shape[3]]
            held_ref[0] = jnp.zeros(held_ref.shape[1:], LOW)
            copies = [
                pltpu.make_async_copy(empty, ref.at[h, n, pl.ds(ref.shape[2] - 1, 1)], sem)
                for ref in outs
                for h in range(parts)
                for n in range(ref.shape[1])
            ]
            for copy in copies:
                copy.start()
            for copy in copies:
                copy.wait()


def middle_kernel(
    layout, rows, blocks, atts, sides, pair, table_ref, place_ref, x_ref, dz_ref, live_ref, norm_ref, *refs
):
    att_refs, chunks = refs[:atts], refs[atts : -9 - sides]
    dnorm_ref, result_ref, dmid_ref, datt_ref = refs[-9 - sides : -5 - sides]
    outs, (weight_ref, left_ref, right_ref, held_ref, sem) = refs[-5 - sides : -5], refs[-5:]
    block = x_ref.shape[0]
    here = pl.ds(pl.multiple_of(pl.program_id(0) * block, block), block)

    @pl.when(pl.program_id(0) == 0)
    def _():
        place_start(table_ref, layout, rows, chunks, weight_ref, sem)
        dnorm_ref[...] = jnp.zeros_like(dnorm_ref)

    gain, shift = norm_ref[2:3, :], norm_ref[3:4, :]
    live = live_ref[...]
    grad = dz_ref[...].astype(F32)
    dmlp = (live * grad).astype(LOW)
    right_ref[2, here, :] = dmlp

    @pl.when(pl.program_id(0) == 0)
    def _():
        place_wait(layout, rows, chunks, weight_ref, sem)

    branch, first = None, 0
    for ref in att_refs:
        left_ref[0, here, first : first + ref.shape[1]] = ref[...]
        part = product(ref[...], matrix(weight_ref, blocks[0], first, ref.shape[1]))
        branch = part if branch is None else branch + part
        first += ref.shape[1]
    middle = x_ref[...].astype(F32) + live * branch
    normed, inv_std = normalize(middle)
    hidden = (normed * gain + shift).astype(LOW)
    left_ref[1, here, :] = hidden
    upward = product(hidden, matrix(weight_ref, blocks[1]))
    square = upward * upward
    bend = jnp.tanh(gelu_coef * (upward + cubic_coef * square * upward))
    half = 0.5 * (1.0 + bend)
    active = (upward * half).astype(LOW)
    left_ref[2, here, :] = active
    slope = half + (0.5 * gelu_coef) * upward * (1.0 - bend * bend) * (
        1.0 + (3.0 * cubic_coef) * square
    )
    result_ref[...] = (middle + live * product(active, matrix(weight_ref, blocks[2]))).astype(LOW)
    dup = (product(dmlp, matrix(weight_ref, blocks[2]), NT) * slope).astype(LOW)
    right_ref[1, here, :] = dup
    dhidden = product(dup, matrix(weight_ref, blocks[1]), NT)
    dnorm_ref[0:1, :] += jnp.sum(dhidden * normed, 0, keepdims=True)
    dnorm_ref[1:2, :] += jnp.sum(dhidden, 0, keepdims=True)
    dmid = grad + norm_back(dhidden, normed, inv_std, gain)
    dmid_ref[...] = dmid
    dbranch = (live * dmid).astype(LOW)
    right_ref[0, here, :] = dbranch
    datt_ref[...] = product(dbranch, matrix(weight_ref, blocks[0]), NT).astype(LOW)

    @pl.when(pl.program_id(0) == pl.num_programs(0) - 1)
    def _():
        mats = left_ref.shape[0]
        total = held_ref.shape[0] // mats
        size = total // outs[0].shape[0]
        for j in range(mats):
            weight_grad(
                left_ref.at[j], [right_ref[j]], place_ref, held_ref, j * total, outs, j * size, sem,
                pair,
            )
        for j in range(mats):
            wait_rows(held_ref, j * total, size, outs, sem)


def last_kernel(layout, rows, blocks, parts, sides, table_ref, x_ref, dmid_ref, norm_ref, other_ref, *refs):
    chunks, grads = refs[:parts], refs[parts : -5 - sides]
    out_ref, dnorm_ref = refs[-5 - sides : -3 - sides]
    packs, (weight_ref, held_ref, sem) = refs[-3 - sides : -3], refs[-3:]

    @pl.when(pl.program_id(0) == 0)
    def _():
        place_start(table_ref, layout, rows, chunks, weight_ref, sem)
        dnorm_ref[...] = jnp.zeros_like(dnorm_ref)

    normed, inv_std = normalize(x_ref[...].astype(F32))

    @pl.when(pl.program_id(0) == 0)
    def _():
        place_wait(layout, rows, chunks, weight_ref, sem)

    total = None
    for j, ids in enumerate(blocks):
        value = jnp.concatenate([ref[j] for ref in grads], 1)
        part = product(value, matrix(weight_ref, ids), NT)
        total = part if total is None else total + part
    dnorm_ref[0:1, :] += jnp.sum(total * normed, 0, keepdims=True)
    dnorm_ref[1:2, :] += jnp.sum(total, 0, keepdims=True)
    out_ref[...] = (
        dmid_ref[...] + norm_back(total, normed, inv_std, norm_ref[0:1, :])
    ).astype(LOW)

    if packs:

        @pl.when(pl.program_id(0) == pl.num_programs(0) - 1)
        def _():
            pack_norms([ref[i : i + 1, :] for ref in (dnorm_ref, other_ref) for i in range(2)], held_ref)
            for side, ref in enumerate(packs):

                @pl.loop(0, ref.shape[0])
                def _(n, ref=ref, side=side):
                    row = held_ref[pl.ds(table_ref[0, side * ref.shape[0] + n], 1), :]
                    ref[n, 0] = jnp.broadcast_to(row, ref.shape[2:]).astype(LOW)


def send_rows(place_ref, held_ref, first, size, outs, block, sem, low, high, pair):
    parts, number, _, rows, _ = outs[0].shape
    chunks = [c for c in range(held_ref.shape[1] // rows) if low < (c + 1) * rows <= high]

    def start(flip):
        for chunk in chunks:
            side = int(bool((chunk ^ chunks[0]) & pair)) ^ flip if len(outs) > 1 else 0
            for h in range(parts):
                at = first + h * size
                source = held_ref.at[at : at + size, chunk * rows : (chunk + 1) * rows]
                place = place_ref[h, chunk] - side * number
                target = outs[side].at[h, place, pl.ds(block, size)]
                pltpu.make_async_copy(source, target, sem).start()

    if not chunks:
        return
    for flip in range(len(outs)):

        @pl.when((place_ref[0, chunks[0]] >= number) == (flip == 1))
        def _(flip=flip):
            start(flip)


def wait_rows(held_ref, first, size, outs, sem):
    wait_for(held_ref.at[first : first + size * outs[0].shape[0]], sem)


def weight_grad(left_ref, rights, place_ref, held_ref, first, outs, block, sem, pair):
    parts = outs[0].shape[0]
    width = left_ref.shape[1]
    step = min(256, width)
    blocks = [r.shape[1] // LANES // parts for r in rights]
    size = sum(blocks)
    for c in range(0, width, step):
        left = left_ref[:, c : c + step]
        at = first
        for right, number in zip(rights, blocks):
            grad = product(left, right, TN).astype(LOW)
            for h in range(parts):
                for b in range(number):
                    lane = (h * number + b) * LANES
                    held_ref[at + h * size + b, c : c + step, :] = grad[:, lane : lane + LANES]
            at += number
        send_rows(place_ref, held_ref, first, size, outs, block, sem, c, c + step, pair)


def slots_of(jobs, parts):
    slots = [[] for _ in range(parts)]
    for which, column, wide in jobs:
        blocks = wide // LANES // parts
        for h in range(parts):
            slots[h] += [(which, column + (h * blocks + b) * LANES) for b in range(blocks)]
    return slots


def sum_kernel(plans, *refs):
    ins, outs = refs[: -len(plans)], refs[-len(plans) :]
    for plan, out in zip(plans, outs):
        for at, terms, ends in plan:
            total = sum(ins[number][entry].astype(F32) for number, entry in terms)
            out[at] = total.astype(out.dtype)
            if ends:
                end = total.shape[0] - 1
                last = total[end:] + sum(ins[n][entry].astype(F32) for n, entry in ends)
                out[at, end:] = last.astype(out.dtype)


def stage_sums(inputs, plans, outs):
    return pl.pallas_call(
        functools.partial(sum_kernel, plans),
        out_shape=outs,
        in_specs=[VMEM] * len(inputs),
        out_specs=[VMEM] * len(outs),
        compiler_params=params(12),
        cost_estimate=cost(0, 2**22),
    )(*inputs)


def terms_of(parts, earlier, h, entry):
    return [(0, (h, entry)), (1, (h, entry))] + [
        (2 + parts * e + h, entry) for e in range(earlier)
    ]


def far_sums(keep, taken, earlier, ends=()):
    parts, chunks, *block = keep.shape
    half = chunks // 2 ** (len(earlier) + 1)
    base = 2 + parts * len(earlier)
    plans = [
        [
            (
                n,
                terms_of(parts, len(earlier), h, half + n),
                [(base + e, half + n) for e in range(len(ends))] if h == 0 else [],
            )
            for n in range(half)
        ]
        for h in range(parts)
    ]
    outs = [shape((half, *block), LOW)] * parts
    return stage_sums([keep, taken, *[t for e in earlier for t in e], *ends], plans, outs)


def near_sums(keep, taken, earlier, inner, ends=()):
    parts, _, *block = keep.shape
    base = 2 + parts * len(earlier)
    plans = [
        [
            (
                h,
                terms_of(parts, len(earlier), h, k),
                [(base + e, k) for e in range(len(ends))] if h == 0 else [],
            )
            for h in range(parts)
        ]
        for k in range(inner)
    ]
    outs = [shape((parts, *block), F32 if k == 0 else LOW) for k in range(inner)]
    return stage_sums([keep, taken, *[t for e in earlier for t in e], *ends], plans, outs)


def lamb_values(weight, grad, first, second):
    m_one = beta_one * first + (1.0 - beta_one) * grad
    m_two = beta_two * second + (1.0 - beta_two) * grad * grad
    step_dir = (
        m_one
        / (1.0 - beta_one**adam_step)
        / (jnp.sqrt(m_two / (1.0 - beta_two**adam_step)) + adam_eps)
        + decay_rate * weight
    )
    return m_one, m_two, step_dir


def whole_sum(value):
    return jnp.sum(jnp.sum(value, 0, keepdims=True), 1, keepdims=True)


def lamb_kernel(base, mats, groups, terms, norm_ends, prior, *refs):
    weight_ref, one_ref, two_ref = refs[:3]
    norm_refs = refs[3:6] if norm_ends else ()
    first = 3 + len(norm_refs)
    term_refs = refs[first : first + terms]
    prior_refs = refs[first + terms : first + terms + prior]
    outs = refs[first + terms + prior :]
    rows = weight_ref.shape[1]
    lane = lax.broadcasted_iota(jnp.int32, (8, LANES), 1)
    line = lax.broadcasted_iota(jnp.int32, (8, LANES), 0)
    squares = jnp.zeros((8, LANES), F32)
    weight_sq = [jnp.zeros((1, LANES), F32)] * mats
    update_sq = [jnp.zeros((1, LANES), F32)] * mats
    for used, entry, slots in groups:
        for at, (which, column) in enumerate(slots):
            grad = sum(term_refs[t][entry, at].astype(F32) for t in used)
            span = slice(column, column + LANES)
            weight = weight_ref[which, :, span]
            m_one, m_two, step = lamb_values(
                weight, grad, one_ref[which, :, span], two_ref[which, :, span]
            )
            j = which - base
            for ref, value in zip(outs, (grad, m_one, m_two, step)):
                ref[j, :, span] = value
            weight_sq[j] += jnp.sum(weight * weight, 0, keepdims=True)
            update_sq[j] += jnp.sum(step * step, 0, keepdims=True)
    for j in range(mats):
        spot = lane == base + j
        squares += jnp.where(spot & (line == 0), jnp.sum(weight_sq[j], 1, keepdims=True), 0.0)
        squares += jnp.where(spot & (line == 1), jnp.sum(update_sq[j], 1, keepdims=True), 0.0)
    if prior:
        for ref, old in zip(outs[:4], prior_refs[:4]):
            ref[mats:] = old[...]
        squares += prior_refs[4][...]
    if norm_ends:
        used, entry = norm_ends
        last = term_refs[used[0]].shape[1] - 1
        row = sum(term_refs[t][entry, last].astype(F32)[0:1] for t in used)
        for i in range(4):
            weight = norm_refs[0][i : i + 1, :]
            grad = row[:, i * rows : (i + 1) * rows]
            m_one, m_two, step = lamb_values(
                weight, grad, norm_refs[1][i : i + 1, :], norm_refs[2][i : i + 1, :]
            )
            for ref, value in zip(outs[5:], (grad, m_one, m_two, step)):
                ref[i : i + 1, :] = value
            spot = lane == 6 + i
            squares += jnp.where(spot & (line == 0), whole_sum(weight * weight), 0.0)
            squares += jnp.where(spot & (line == 1), whole_sum(step * step), 0.0)
    outs[4][...] = squares


def lamb_call(base, mats, groups, terms, state, norm_state=(), norm_ends=None, prior=()):
    total, rows, width = state[0].shape
    outs = [shape((total if prior else mats, rows, width), F32)] * 4 + [shape((8, LANES), F32)]
    if norm_ends:
        outs += [shape(norm_state[0].shape, F32)] * 4
    inputs = [*state, *norm_state, *terms, *prior]
    return pl.pallas_call(
        functools.partial(lamb_kernel, base, mats, groups, len(terms), norm_ends, len(prior)),
        out_shape=outs,
        in_specs=[VMEM] * len(inputs),
        out_specs=[VMEM] * len(outs),
        compiler_params=params(12),
        cost_estimate=cost(0, 2**22),
    )(*inputs)


def on_device(
    latents,
    lengths,
    cotangent,
    matrices,
    norm_params,
    moment1_mat,
    moment2_mat,
    moment1_norm,
    moment2_norm,
):
    _, length, width = latents.shape
    dim = width // HEADS
    scale = 1.0 / math.sqrt(dim)
    power = scale * math.log2(math.e)
    dp, fsdp = lax.axis_size("dp"), lax.axis_size("fsdp")
    count = dp * fsdp
    rows = matrices.shape[1]
    index = lax.axis_index("dp") * fsdp + lax.axis_index("fsdp")
    ring = dp == 8 and fsdp == 4 and rows == 32
    inner, pair = fsdp, fsdp
    block = 256 if length % 256 == 0 else length
    low_mats = matrices.astype(LOW)
    low_norms = norm_params.astype(LOW)

    if ring:
        firsts, seconds = (2 * fsdp, 4 * fsdp), (4 * fsdp, 2 * fsdp)
        half_blocks = width // 2 // LANES
        order_end = (2 * fsdp, 4 * fsdp)
        masks = [
            [m ^ side for side in (0, pair) for m in mask_order(o, inner)]
            for o in zip(firsts, seconds)
        ] + [
            [m ^ side ^ k for side in (0, pair) for k in range(inner) for m in mask_order(order_end, 1)]
        ]
        table = jnp.bitwise_xor(jnp.array(masks, jnp.int32), index.astype(jnp.int32))
        away = jnp.bitwise_xor(jnp.arange(count, dtype=jnp.int32), index.astype(jnp.int32))[None]

        def bit(mask, weight):
            return jnp.where(away & jnp.array(mask, jnp.int32)[:, None] != 0, weight, 0)

        places = (
            (away & (inner - 1))
            + bit(firsts, inner)
            + bit(seconds, 2 * inner)
            + bit([pair] * 2, count // 2)
        ).astype(jnp.int32)
        lower = rows // 2
        shard = by_columns(low_mats[:3], 2).reshape(2, 3 * half_blocks, 2, lower, LANES)
        shard = shard.transpose(0, 2, 1, 3, 4).reshape(2, 6 * half_blocks, lower, LANES)
        norm_rows = jnp.pad(
            low_norms.reshape(1, 1, 1, 4 * rows), ((0, 1), (0, 0), (0, lower - 1), (0, 0))
        )
        shard = jnp.concatenate([shard, norm_rows], 1)
        in_size, mid_size = 3 * half_blocks + 1, 2 * half_blocks
        eighth = count // 4
        halves = [
            (h, side * count // 2 + part * eighth)
            for h in range(2)
            for side in range(2)
            for part in range(2)
        ]
        layout_in = tuple((h, start, h * in_size) for h, start in halves)
        layout_out = tuple((h, start, h * mid_size) for h, start in halves)
        layout_out += tuple((2, n * eighth, 2 * mid_size) for n in range(4))

        def ids(size, j):
            return [h * size + j * half_blocks + b for h in range(2) for b in range(half_blocks)]

        blocks_in = [ids(in_size, j) for j in range(3)]
        blocks_out = [ids(mid_size, j) for j in range(2)]
        blocks_out.append([2 * mid_size + b for b in range(2 * half_blocks)])
        norm_block = in_size - 1
        scratch_blocks = (2 * in_size, 2 * mid_size + 2 * half_blocks)

        def near_of(value):
            return [value] + [swap(value, k, count) for k in range(1, inner)]

        def halves_of(near):
            return [jnp.stack([n[h] for n in near]) for h in range(2)]

        def grow(held, taken):
            return [jnp.concatenate(both) for both in zip(held, taken)]

        def with_pairs(held, taken, early):
            late = swap_all(taken, [pair, pair], count)
            return [a for h in range(2) for a in (held[h], taken[h], early[h], late[h])]

        near = near_of(shard)
        end = by_columns(low_mats[5:], 1)
        end = jnp.concatenate([end, swap(end, order_end[0], count)])
        held = halves_of(after(near, end))
        taken = swap_all(held, firsts, count)
        end = jnp.concatenate([end, swap(after(end, *held), order_end[1], count)])
        held = grow(held, after(taken, end))
        taken = swap_all(held, seconds, count)
        early = swap_all(held, [pair, pair], count)
        mid = near_of(after(by_columns(low_mats[3:5], 2), *held))
        end = jnp.concatenate([end, swap(after(end, *held), 1, count)])
        late = swap_all(after(taken, end, *mid), [pair, pair], count)
        parts_in = [a for h in range(2) for a in (held[h], taken[h], early[h], late[h])]
        mid = halves_of(mid)
        end = [end, swap(after(end, *mid), 2, count)]
        norm_vals = []
    else:
        weights_in = lax.all_gather(low_mats[:3], AXES, axis=1, tiled=True)
        weights_out = lax.all_gather(low_mats[3:], AXES, axis=1, tiled=True)
        norm_vals = [lax.all_gather(low_norms, AXES, axis=1, tiled=True).astype(F32)]
        table = places = jnp.zeros((1, 1), jnp.int32)
        rows = width
        parts_in, parts_out = [by_columns(weights_in, 1)], [by_columns(weights_out, 1)]
        layout_in = layout_out = ((0, 0, 0),)
        per = width // LANES
        blocks_in = blocks_out = [list(range(j * per, (j + 1) * per)) for j in range(3)]
        scratch_blocks = (3 * per, 3 * per)
        norm_block = None

    ends = jnp.cumsum(lengths[0, :-1])
    sets = ends.shape[0]
    segment = jnp.sum(
        (jnp.arange(length, dtype=jnp.int32)[:, None] >= ends[None, :]).astype(jnp.int32), axis=1
    )
    live = (segment < sets).astype(F32)[:, None]
    lanes = jnp.arange(LANES, dtype=jnp.int32)[None, :]
    same = segment[:, None] == lanes
    mark_in = same.astype(LOW)
    mark_out = jnp.where(same | (lanes > sets), 0.0, mask_depth).astype(LOW)

    x, dz = latents[0], cotangent[0]
    steps = (length // block,)
    if ring:
        taken = swap_all(mid, firsts, count)
        x = after(x, *mid)
    held_rows = pl.BlockSpec((4, width), lambda i: (0, 0))
    two_rows = pl.BlockSpec((2, width), lambda i: (0, 0))
    anywhere = pl.BlockSpec(memory_space=pl.ANY)
    scratch_in, scratch_out = (pltpu.VMEM((n, width, LANES), LOW) for n in scratch_blocks)
    norm_scratch, sem_scratch = pltpu.VMEM((count, LANES), F32), pltpu.SemaphoreType.DMA
    hidden_one, qkv, norm_vals = pl.pallas_call(
        functools.partial(
            project_kernel, layout_in, rows, blocks_in, norm_block, len(parts_in)
        ),
        grid=steps,
        out_shape=[
            shape((length, width), LOW),
            shape((length, 3 * width), LOW),
            shape((4, width), F32),
        ],
        in_specs=[SMEM, rows_of(x, block)]
        + [anywhere] * len(parts_in)
        + [held_rows] * len(norm_vals),
        out_specs=[
            pl.BlockSpec((block, width), lambda i: (i, 0)),
            pl.BlockSpec((block, 3 * width), lambda i: (i, 0)),
            held_rows,
        ],
        scratch_shapes=[scratch_in, norm_scratch, sem_scratch],
        compiler_params=params(18),
        cost_estimate=cost(6 * length * width * width, 12 * width * width),
    )(table, x, *parts_in, *norm_vals)
    x = latents[0]

    group = 2
    marks = [pl.BlockSpec((length, LANES), lambda h: (0, 0))] * 2

    def heads_at(first):
        return pl.BlockSpec((length, dim * group), lambda h: (0, first // group + h))

    def sums_at(first):
        return pl.BlockSpec((group, 1, length), lambda h: (first // group + h, 0, 0))

    def attend(first, number, qkv):
        return pl.pallas_call(
            functools.partial(attend_kernel, group, dim, power),
            grid=(number // group,),
            in_specs=[heads_at(first + i * HEADS) for i in range(3)] + marks,
            out_specs=[heads_at(0), sums_at(0)],
            out_shape=[shape((length, number * dim), LOW), shape((number, 1, length), F32)],
            compiler_params=params(14),
            cost_estimate=cost(8 * length * length * number * dim, 8 * length * number * dim),
        )(qkv, qkv, qkv, mark_in, mark_out)

    ahead = HEADS // 2
    if ring:
        mid = grow(mid, after(taken, hidden_one))
        taken = swap_all(mid, seconds, count)
        early = swap_all(mid, [pair, pair], count)
        attended, log_sums = zip(*[attend(f, ahead, after(qkv, *mid)) for f in (0, ahead)])
        end_late = [swap(e, pair, count) for e in after(end, *attended)]
        parts_out = with_pairs(mid, after(taken, *attended), early) + end + end_late
    else:
        attended, log_sums = zip(*[attend(f, ahead, qkv) for f in (0, ahead)])

    row_block = pl.BlockSpec((block, width), lambda i: (i, 0))
    low_rows = shape((length, width), LOW)
    sides, parts = (2, 2) if ring else (1, 1)
    chunk_shape = (parts, count // sides if ring else 1)
    mat_blocks = width // LANES

    def chunks_of(blocks, extra=0):
        size = blocks // parts + extra
        return [shape((*chunk_shape, size, rows, LANES), LOW)] * sides

    dnorm_two, result, dmid, dattended, *out_grads = pl.pallas_call(
        functools.partial(
            middle_kernel, layout_out, rows, blocks_out, len(attended), sides, pair
        ),
        grid=steps,
        out_shape=[
            shape((2, width), F32),
            low_rows,
            shape((length, width), F32),
            low_rows,
            *chunks_of(3 * mat_blocks),
        ],
        in_specs=[SMEM, SMEM, row_block, row_block, rows_of(live, block), held_rows]
        + [rows_of(a, block) for a in attended]
        + [anywhere] * len(parts_out),
        out_specs=[two_rows] + [row_block] * 3 + [anywhere] * sides,
        scratch_shapes=[
            scratch_out,
            *[pltpu.VMEM((3, length, width), LOW)] * 2,
            pltpu.VMEM((3 * mat_blocks, width, LANES), LOW),
            sem_scratch,
        ],
        compiler_params=params(42),
        cost_estimate=cost(18 * length * width * width, 24 * width * width),
    )(table, places, x, dz, live, norm_vals, *attended, *parts_out)

    def attend_back(first, number, dattended, base, total, extra=0, prior=()):
        side = first // ahead
        inside = first - side * ahead
        blocks = 3 * group * dim // LANES
        outs = chunks_of(blocks * total, extra)
        return pl.pallas_call(
            functools.partial(
                attend_back_kernel, group, dim, power, scale, base, extra, len(prior), pair
            ),
            grid=(number // group,),
            in_specs=[SMEM]
            + [heads_at(first + i * HEADS) for i in range(3)]
            + [heads_at(first), heads_at(inside), *marks, sums_at(inside), whole(hidden_one)]
            + [anywhere] * len(prior),
            out_specs=[pl.BlockSpec((3, length, dim * group), lambda h: (0, 0, h))]
            + [anywhere] * sides,
            out_shape=[shape((3, length, number * dim), LOW), *outs],
            input_output_aliases={10 + n: 1 + n for n in range(len(prior))},
            scratch_shapes=[pltpu.VMEM((2 * blocks, width, LANES), LOW), sem_scratch],
            compiler_params=params(20),
            cost_estimate=cost(
                20 * length * length * number * dim + 6 * length * width * number * dim,
                16 * length * number * dim,
            ),
        )(
            places, qkv, qkv, qkv, dattended, attended[side], mark_in, mark_out,
            log_sums[side], hidden_one, *prior,
        )

    def last(dmid, grads, sides):
        packs = [shape((count // max(sides, 1), 1, rows, LANES), LOW)] * sides
        return pl.pallas_call(
            functools.partial(last_kernel, layout_in, rows, blocks_in, len(parts_in), sides),
            grid=steps,
            out_shape=[low_rows, shape((2, width), F32), *packs],
            in_specs=[SMEM, row_block, row_block, held_rows, two_rows]
            + [anywhere] * len(parts_in)
            + [rows_of(g, block) for g in grads],
            out_specs=[row_block, two_rows]
            + [pl.BlockSpec(p.shape, lambda i: (0, 0, 0, 0)) for p in packs],
            scratch_shapes=[scratch_in, norm_scratch, sem_scratch],
            compiler_params=params(18),
            cost_estimate=cost(6 * length * width * width, 6 * width * width),
        )(table, x, dmid, norm_vals, dnorm_two, *parts_in, *grads)

    state, norm_state = (matrices, moment1_mat, moment2_mat), (norm_params, moment1_norm, moment2_norm)
    if ring:
        pairs = range(1, inner)
        heads_w = group * dim

        def slots(firsts, number):
            return slots_of(
                [(j, n * heads_w, heads_w) for n in range(firsts, firsts + number) for j in range(3)], 2
            )

        def from_near(near):
            return [near[0]] + swap_all(near[1:], pairs, count)

        per = ahead // group
        keep, send = out_grads
        taken = swap(send, pair, count)
        found, *one = attend_back(0, group, after(dattended, keep), 0, per)
        grads = [found]

        sent = far_sums(keep, after(taken, found), [])
        far = [swap_all(sent, seconds, count)]
        found, keep_one, send_one = attend_back(
            group, group, after(dattended, *sent, found), 1, per, 0, one
        )
        grads.append(found)
        found, *two = attend_back(ahead, group, after(dattended, found, keep_one), 0, per, 1)
        grads.append(found)

        sent = far_sums(keep, taken, after(far, found))
        far.append(swap_all(sent, firsts, count))
        taken_one = swap(after(send_one, *sent), pair, count)
        found, keep_two, send_two = attend_back(
            ahead + group, group, after(dattended, *sent, found), 1, per, 1, two
        )
        grads.append(found)

        near = from_near(near_sums(keep, taken, [far[0], after(far[1], grads[-1])], inner))
        sent_one = far_sums(keep_one, after(taken_one, grads[-1]), [])
        far_one = [swap_all(sent_one, seconds, count)]
        grad_latents, dnorm_one, *packs = last(after(dmid, near[0], *sent_one), grads, 2)

        sent_one = far_sums(keep_one, taken_one, after(far_one, grad_latents, *near))
        far_one.append(swap_all(sent_one, firsts, count))
        taken_two, ends = swap_all(after((send_two, packs[1]), *sent_one), [pair, pair], count)
        ends = [packs[0], ends]
        groups = [(range(inner), h, s) for h, s in enumerate(slots_of([(j, 0, width) for j in (3, 4, 5)], 2))]
        prior = lamb_call(3, 3, groups, after(near, *sent_one), state)

        far_one, taken_two, ends = after((far_one, taken_two, ends), prior[4], far_one, taken_two, ends)
        near_one = near_sums(keep_one, taken_one, far_one, inner)
        sent_two = far_sums(keep_two, taken_two, [], ends)
        near_one, sent_two = after((near_one, sent_two), near_one, sent_two)
        near_one = from_near(near_one)
        far_two = [swap_all(sent_two, seconds, count)]
        sent_two = far_sums(keep_two, taken_two, after(far_two, *near_one), ends)
        far_two.append(swap_all(sent_two, firsts, count))
        near_two = from_near(near_sums(keep_two, taken_two, far_two, inner, ends))
        groups = [(range(inner), h, s) for h, s in enumerate(slots(0, per))]
        groups += [(range(inner, 2 * inner), h, s) for h, s in enumerate(slots(per, per))]
        norm_ends = (range(inner, 2 * inner), 0)
        found = lamb_call(
            0, 3, groups, [*near_one, *near_two], state, norm_state, norm_ends, prior
        )
        grad_mats, m1_mat, m2_mat, dir_mat, squares, grad_norms, m1_norm, m2_norm, dir_norm = found
        squares = hyper_sum(squares, count)[:2, :10]
    else:
        first, *one = attend_back(0, ahead, dattended, 0, HEADS // group)
        second, in_grads = attend_back(
            ahead, ahead, dattended, ahead // group, HEADS // group, 0, one
        )
        grads = [first, second]
        grad_latents, dnorm_one = last(dmid, grads, 0)
        norms_local = jnp.concatenate([dnorm_one, dnorm_two], 0)
        per = group * dim // LANES
        local = in_grads[0, 0].reshape(HEADS // group, 3, per, width, LANES)
        local = local.transpose(1, 0, 2, 3, 4).reshape(3 * mat_blocks, width, LANES)
        local = jnp.concatenate([local, out_grads[0][0, 0]], 0).astype(F32)
        local = local.reshape(6, mat_blocks, width, LANES)
        local = local.transpose(0, 2, 1, 3).reshape(6, width, width)
        grad_mats = lax.psum_scatter(local, AXES, scatter_dimension=1, tiled=True)
        grad_norms = lax.psum_scatter(norms_local, AXES, scatter_dimension=1, tiled=True)
        m1_mat, m2_mat, dir_mat = lamb_values(matrices, grad_mats, moment1_mat, moment2_mat)
        m1_norm, m2_norm, dir_norm = lamb_values(norm_params, grad_norms, moment1_norm, moment2_norm)
        squares = jnp.stack(
            [
                jnp.concatenate([jnp.sum(m * m, (1, 2)), jnp.sum(n * n, 1)])
                for m, n in ((matrices, norm_params), (dir_mat, dir_norm))
            ]
        )
        squares = lax.psum(squares, AXES)
    ratios = jnp.sqrt(squares[0]) / jnp.sqrt(squares[1])
    scaled_mats = ratios[:6][:, None, None] * dir_mat
    scaled_norms = ratios[6:][:, None] * dir_norm
    return (
        result[None],
        grad_latents[None],
        grad_mats,
        grad_norms,
        scaled_mats,
        scaled_norms,
        m1_mat,
        m2_mat,
        m1_norm,
        m2_norm,
        ratios,
    )


def solution(mesh):
    return jax.shard_map(
        on_device,
        mesh=mesh,
        in_specs=(
            P(("dp", "fsdp"), None, None),
            P(("dp", "fsdp"), None),
            P(("dp", "fsdp"), None, None),
            P(None, ("dp", "fsdp"), None),
            P(None, ("dp", "fsdp")),
            P(None, ("dp", "fsdp"), None),
            P(None, ("dp", "fsdp"), None),
            P(None, ("dp", "fsdp")),
            P(None, ("dp", "fsdp")),
        ),
        out_specs=(
            P(("dp", "fsdp"), None, None),
            P(("dp", "fsdp"), None, None),
            P(None, ("dp", "fsdp"), None),
            P(None, ("dp", "fsdp")),
            P(None, ("dp", "fsdp"), None),
            P(None, ("dp", "fsdp")),
            P(None, ("dp", "fsdp"), None),
            P(None, ("dp", "fsdp"), None),
            P(None, ("dp", "fsdp")),
            P(None, ("dp", "fsdp")),
            P(),
        ),
        check_vma=False,
    )
```

```python
import functools
import math

import jax
import jax.numpy as jnp
from jax import lax
from jax.experimental import pallas as pl
from jax.experimental.pallas import tpu as pltpu
from jax.sharding import PartitionSpec as P

HEADS = 8
AXES = ("dp", "fsdp")
LANES = 128

ln_eps = 1e-05
beta_one = 0.9
beta_two = 0.999
adam_eps = 1e-06
decay_rate = 0.01
adam_step = 100.0
gelu_coef = 0.7978845608
cubic_coef = 0.044715
mask_depth = -1e30

F32 = jnp.float32
LOW = jnp.bfloat16
NT = (((1,), (1,)), ((), ()))
TN = (((0,), (0,)), ((), ()))
SMEM = pl.BlockSpec(memory_space=pltpu.SMEM)
VMEM = pl.BlockSpec(memory_space=pltpu.VMEM)


def params(mib):
    return pltpu.CompilerParams(vmem_limit_bytes=mib * 2**20)


def shape(dims, kind):
    return jax.ShapeDtypeStruct(dims, kind)


def product(left, right, dims=(((1,), (0,)), ((), ()))):
    return lax.dot_general(left, right, dims, preferred_element_type=F32)


def cost(flops, moved):
    return pl.CostEstimate(flops=int(flops), bytes_accessed=int(moved), transcendentals=0)


def whole(array):
    return pl.BlockSpec(
        array.shape, lambda i: (0,) * len(array.shape), pipeline_mode=pl.Buffered(1)
    )


def rows_of(array, block):
    lead = array.shape[:-2]
    return pl.BlockSpec((*lead, block, array.shape[-1]), lambda i: (*(0,) * len(lead), i, 0))


def swap(value, mask, count):
    return lax.ppermute(value, AXES, [(i, i ^ mask) for i in range(count)])


def swap_all(values, bits, count):
    return [swap(v, b, count) for v, b in zip(values, bits)]


def add_up(values):
    while len(values) > 1:
        values = [a + b for a, b in zip(values[::2], values[1::2])]
    return values[0]


def rounds_sum(value, rounds, count):
    for masks in rounds:
        value = add_up([value] + [swap(value, mask, count) for mask in masks])
    return value


def after(value, *others):
    return lax.optimization_barrier((value, others))[0]


def mask_order(order, inner):
    masks = list(range(inner))
    for bit in order:
        masks = masks + [m ^ bit for m in masks]
    return masks


def by_columns(shards, parts):
    mats, rows, columns = shards.shape
    blocks = columns // parts // LANES
    split = shards.reshape(mats, rows, parts, blocks, LANES)
    return split.transpose(2, 0, 3, 1, 4).reshape(parts, mats * blocks, rows, LANES)


def normalize(value):
    centered = value - jnp.mean(value, -1, keepdims=True)
    inv_std = lax.rsqrt(jnp.mean(centered * centered, -1, keepdims=True) + ln_eps)
    return centered * inv_std, inv_std


def norm_back(grad_out, normed, inv_std, gain):
    grad_normed = grad_out * gain
    return inv_std * (
        grad_normed
        - jnp.mean(grad_normed, -1, keepdims=True)
        - normed * jnp.mean(grad_normed * normed, -1, keepdims=True)
    )


def pieces_of(ref, rows):
    number, height = ref.shape[1:3]
    if height == rows:
        return [(0, number, 0, 0)]
    blocks = number // 2
    return [(0, blocks, 0, 0), (blocks, blocks, 0, height), (number - 1, 1, blocks, 0)]


def place_start(table_ref, layout, rows, refs, weight_ref, sem):
    for (line, start, first), ref in zip(layout, refs):

        @pl.loop(0, ref.shape[0], unroll=4)
        def _(n, line=line, start=start, first=first, ref=ref):
            row = pl.multiple_of(table_ref[line, start + n] * rows, rows)
            for at, number, block, lower in pieces_of(ref, rows):
                block += first
                target = weight_ref.at[block : block + number, pl.ds(row + lower, ref.shape[2])]
                pltpu.make_async_copy(ref.at[n, at : at + number], target, sem).start()


def place_wait(layout, rows, refs, weight_ref, sem):
    for (_, _, first), ref in zip(layout, refs):
        for _, number, block, _ in pieces_of(ref, rows):
            block += first
            wait_for(weight_ref.at[block : block + number, 0 : ref.shape[0] * ref.shape[2]], sem)


def wait_for(ref, sem):
    pltpu.make_async_copy(ref, ref, sem).wait()


def matrix(weight_ref, blocks, first=0, size=None):
    size = weight_ref.shape[1] if size is None else size
    return jnp.concatenate([weight_ref[b, first : first + size, :] for b in blocks], 1)


def lane_rows(low, first, number):
    lane = lax.broadcasted_iota(jnp.int32, low, 1)
    return (lane >= first) & (lane < first + number)


def spread_norms(rows, weight_ref, block, held_ref, norm_ref):
    for n in range(held_ref.shape[0]):
        held_ref[n : n + 1, :] = weight_ref[block, n * rows : n * rows + 16, :].astype(F32)[0:1]
    near = LANES // 32
    blocks = held_ref.shape[0] // near
    for i in range(4):
        total = jnp.zeros((blocks, LANES), F32)
        for z in range(near):
            value = held_ref[pl.ds(z, blocks, stride=near), :]
            value = pltpu.roll(value, (32 * (z - i)) % LANES, 1)
            total = total + jnp.where(lane_rows(total.shape, 32 * z, 32), value, 0.0)
        for b in range(blocks):
            norm_ref[i : i + 1, b * LANES : (b + 1) * LANES] = total[b : b + 1]


def pack_norms(norms, held_ref):
    near = LANES // 32
    blocks = held_ref.shape[0] // near
    held = [jnp.zeros((blocks, LANES), F32) for _ in range(near)]
    for i, norm in enumerate(norms):
        stacked = jnp.concatenate(
            [norm[:, b * LANES : (b + 1) * LANES] for b in range(blocks)], 0
        )
        for z in range(near):
            value = pltpu.roll(stacked, (32 * (i - z)) % LANES, 1)
            held[z] = held[z] + jnp.where(lane_rows(value.shape, 32 * i, 32), value, 0.0)
    for z in range(near):
        held_ref[pl.ds(z, blocks, stride=near), :] = held[z]


def project_kernel(layout, rows, blocks, norm_block, parts, table_ref, x_ref, *refs):
    chunks = refs[:parts]
    hidden_ref, out_ref, norm_ref, weight_ref, held_ref, sem = refs[-6:]
    width = x_ref.shape[1]

    @pl.when(pl.program_id(0) == 0)
    def _():
        place_start(table_ref, layout, rows, chunks, weight_ref, sem)

    normed, _ = normalize(x_ref[...].astype(F32))

    @pl.when(pl.program_id(0) == 0)
    def _():
        place_wait(layout, rows, chunks, weight_ref, sem)
        if norm_block is None:
            norm_ref[...] = refs[parts][...]
        else:
            spread_norms(rows, weight_ref, norm_block, held_ref, norm_ref)

    hidden = (normed * norm_ref[0:1, :] + norm_ref[1:2, :]).astype(LOW)
    hidden_ref[...] = hidden
    for j, ids in enumerate(blocks):
        out_ref[:, j * width : (j + 1) * width] = product(
            hidden, matrix(weight_ref, ids)
        ).astype(LOW)


def attend_kernel(group, dim, power, q_ref, k_ref, v_ref, in_ref, out_ref, o_ref, lse_ref):
    for g in range(group):
        span = slice(g * dim, (g + 1) * dim)
        keys = jnp.concatenate([k_ref[:, span], out_ref[...]], 1)
        queries = jnp.concatenate([q_ref[:, span], in_ref[...]], 1)
        scores = product(keys, queries, NT)
        top = jnp.max(scores, 0, keepdims=True)
        weight = jnp.exp2((scores - top) * power)
        total = jnp.sum(weight, 0, keepdims=True)
        probs = (weight * (1.0 / total)).astype(LOW)
        o_ref[:, span] = product(v_ref[:, span].T, probs).T.astype(LOW)
        lse_ref[g] = top * power + jnp.log2(total)


def attend_back_kernel(
    group, dim, power, scale, base, extra, prior, pair, place_ref,
    q_ref, k_ref, v_ref, do_ref, o_ref, in_ref, out_ref, lse_ref, hidden_ref, *refs,
):
    grad_ref, *outs = refs[prior:-2]
    held_ref, sem = refs[-2:]
    for g in range(group):
        span = slice(g * dim, (g + 1) * dim)
        queries, keys, grad = q_ref[:, span], k_ref[:, span], do_ref[:, span]
        both = grad.astype(F32) * o_ref[:, span].astype(F32)
        row_dot = lax.dot_general(
            jnp.ones((8, dim), F32), both, NT,
            preferred_element_type=F32, precision=lax.Precision.HIGHEST,
        )[0:1]
        scores = product(
            jnp.concatenate([keys, out_ref[...]], 1),
            jnp.concatenate([queries, in_ref[...]], 1),
            NT,
        )
        probs = jnp.exp2(scores * power - lse_ref[g])
        grad_probs = product(v_ref[:, span], grad, NT)
        grad_scores = (probs * (grad_probs - row_dot)).astype(LOW)
        grad_ref[2, :, span] = product(probs.astype(LOW), grad).astype(LOW)
        grad_ref[1, :, span] = (product(grad_scores, queries) * scale).astype(LOW)
        grad_ref[0, :, span] = (product(keys.T, grad_scores).T * scale).astype(LOW)
    parts = outs[0].shape[0]
    total = held_ref.shape[0] // 2
    size = total // parts
    step = pl.program_id(0)
    slot = lax.rem(step, 2) * total

    @pl.when(step > 1)
    def _():
        wait_rows(held_ref, 0, size, outs, sem)

    for s in range(2):

        @pl.when(slot == s * total)
        def _(s=s):
            weight_grad(
                hidden_ref, [grad_ref[j] for j in range(3)],
                place_ref, held_ref, s * total, outs, (base + step) * size, sem, pair,
            )

    @pl.when(step == pl.num_programs(0) - 1)
    def _():
        wait_rows(held_ref, 0, size, outs, sem)

        @pl.when(step > 0)
        def _():
            wait_rows(held_ref, 0, size, outs, sem)

        if extra:
            empty = held_ref.at[0:1, 0 : outs[0].shape[3]]
            held_ref[0] = jnp.zeros(held_ref.shape[1:], LOW)
            copies = [
                pltpu.make_async_copy(empty, ref.at[h, n, pl.ds(ref.shape[2] - 1, 1)], sem)
                for ref in outs
                for h in range(parts)
                for n in range(ref.shape[1])
            ]
            for copy in copies:
                copy.start()
            for copy in copies:
                copy.wait()


def middle_kernel(
    layout, rows, blocks, atts, sides, pair, table_ref, place_ref, x_ref, dz_ref, live_ref, norm_ref, *refs
):
    att_refs, chunks = refs[:atts], refs[atts : -9 - sides]
    dnorm_ref, result_ref, dmid_ref, datt_ref = refs[-9 - sides : -5 - sides]
    outs, (weight_ref, left_ref, right_ref, held_ref, sem) = refs[-5 - sides : -5], refs[-5:]
    block = x_ref.shape[0]
    here = pl.ds(pl.multiple_of(pl.program_id(0) * block, block), block)

    @pl.when(pl.program_id(0) == 0)
    def _():
        place_start(table_ref, layout, rows, chunks, weight_ref, sem)
        dnorm_ref[...] = jnp.zeros_like(dnorm_ref)

    gain, shift = norm_ref[2:3, :], norm_ref[3:4, :]
    live = live_ref[...]
    grad = dz_ref[...].astype(F32)
    dmlp = (live * grad).astype(LOW)
    right_ref[2, here, :] = dmlp

    @pl.when(pl.program_id(0) == 0)
    def _():
        place_wait(layout, rows, chunks, weight_ref, sem)

    branch, first = None, 0
    for ref in att_refs:
        left_ref[0, here, first : first + ref.shape[1]] = ref[...]
        part = product(ref[...], matrix(weight_ref, blocks[0], first, ref.shape[1]))
        branch = part if branch is None else branch + part
        first += ref.shape[1]
    middle = x_ref[...].astype(F32) + live * branch
    normed, inv_std = normalize(middle)
    hidden = (normed * gain + shift).astype(LOW)
    left_ref[1, here, :] = hidden
    upward = product(hidden, matrix(weight_ref, blocks[1]))
    square = upward * upward
    bend = jnp.tanh(gelu_coef * (upward + cubic_coef * square * upward))
    half = 0.5 * (1.0 + bend)
    active = (upward * half).astype(LOW)
    left_ref[2, here, :] = active
    slope = half + (0.5 * gelu_coef) * upward * (1.0 - bend * bend) * (
        1.0 + (3.0 * cubic_coef) * square
    )
    result_ref[...] = (middle + live * product(active, matrix(weight_ref, blocks[2]))).astype(LOW)
    dup = (product(dmlp, matrix(weight_ref, blocks[2]), NT) * slope).astype(LOW)
    right_ref[1, here, :] = dup
    dhidden = product(dup, matrix(weight_ref, blocks[1]), NT)
    dnorm_ref[0:1, :] += jnp.sum(dhidden * normed, 0, keepdims=True)
    dnorm_ref[1:2, :] += jnp.sum(dhidden, 0, keepdims=True)
    dmid = grad + norm_back(dhidden, normed, inv_std, gain)
    dmid_ref[...] = dmid
    dbranch = (live * dmid).astype(LOW)
    right_ref[0, here, :] = dbranch
    datt_ref[...] = product(dbranch, matrix(weight_ref, blocks[0]), NT).astype(LOW)

    @pl.when(pl.program_id(0) == pl.num_programs(0) - 1)
    def _():
        mats = left_ref.shape[0]
        total = held_ref.shape[0] // mats
        size = total // outs[0].shape[0]
        for j in range(mats):
            weight_grad(
                left_ref.at[j], [right_ref[j]], place_ref, held_ref, j * total, outs, j * size, sem,
                pair,
            )
        for j in range(mats):
            wait_rows(held_ref, j * total, size, outs, sem)


def last_kernel(layout, rows, blocks, parts, sides, table_ref, x_ref, dmid_ref, norm_ref, other_ref, *refs):
    chunks, grads = refs[:parts], refs[parts : -5 - sides]
    out_ref, dnorm_ref = refs[-5 - sides : -3 - sides]
    packs, (weight_ref, held_ref, sem) = refs[-3 - sides : -3], refs[-3:]

    @pl.when(pl.program_id(0) == 0)
    def _():
        place_start(table_ref, layout, rows, chunks, weight_ref, sem)
        dnorm_ref[...] = jnp.zeros_like(dnorm_ref)

    normed, inv_std = normalize(x_ref[...].astype(F32))

    @pl.when(pl.program_id(0) == 0)
    def _():
        place_wait(layout, rows, chunks, weight_ref, sem)

    total = None
    for j, ids in enumerate(blocks):
        value = jnp.concatenate([ref[j] for ref in grads], 1)
        part = product(value, matrix(weight_ref, ids), NT)
        total = part if total is None else total + part
    dnorm_ref[0:1, :] += jnp.sum(total * normed, 0, keepdims=True)
    dnorm_ref[1:2, :] += jnp.sum(total, 0, keepdims=True)
    out_ref[...] = (
        dmid_ref[...] + norm_back(total, normed, inv_std, norm_ref[0:1, :])
    ).astype(LOW)

    if packs:

        @pl.when(pl.program_id(0) == pl.num_programs(0) - 1)
        def _():
            pack_norms([ref[i : i + 1, :] for ref in (dnorm_ref, other_ref) for i in range(2)], held_ref)
            for side, ref in enumerate(packs):

                @pl.loop(0, ref.shape[0], unroll=8)
                def _(n, ref=ref, side=side):
                    row = held_ref[pl.ds(table_ref[0, side * ref.shape[0] + n], 1), :]
                    ref[n, 0] = jnp.broadcast_to(row, ref.shape[2:]).astype(LOW)


def send_rows(place_ref, held_ref, first, size, outs, block, sem, low, high, pair):
    parts, number, _, rows, _ = outs[0].shape
    chunks = [c for c in range(held_ref.shape[1] // rows) if low < (c + 1) * rows <= high]

    def start(flip):
        for chunk in chunks:
            side = int(bool((chunk ^ chunks[0]) & pair)) ^ flip if len(outs) > 1 else 0
            for h in range(parts):
                at = first + h * size
                source = held_ref.at[at : at + size, chunk * rows : (chunk + 1) * rows]
                place = place_ref[h, chunk] - side * number
                target = outs[side].at[h, place, pl.ds(block, size)]
                pltpu.make_async_copy(source, target, sem).start()

    if not chunks:
        return
    for flip in range(len(outs)):

        @pl.when((place_ref[0, chunks[0]] >= number) == (flip == 1))
        def _(flip=flip):
            start(flip)


def wait_rows(held_ref, first, size, outs, sem):
    wait_for(held_ref.at[first : first + size * outs[0].shape[0]], sem)


def weight_grad(left_ref, rights, place_ref, held_ref, first, outs, block, sem, pair):
    parts = outs[0].shape[0]
    width = left_ref.shape[1]
    step = min(256, width)
    blocks = [r.shape[1] // LANES // parts for r in rights]
    size = sum(blocks)
    for c in range(0, width, step):
        left = left_ref[:, c : c + step]
        at = first
        for right, number in zip(rights, blocks):
            grad = product(left, right, TN).astype(LOW)
            for h in range(parts):
                for b in range(number):
                    lane = (h * number + b) * LANES
                    held_ref[at + h * size + b, c : c + step, :] = grad[:, lane : lane + LANES]
            at += number
        send_rows(place_ref, held_ref, first, size, outs, block, sem, c, c + step, pair)


def slots_of(jobs, parts):
    slots = [[] for _ in range(parts)]
    for which, column, wide in jobs:
        blocks = wide // LANES // parts
        for h in range(parts):
            slots[h] += [(which, column + (h * blocks + b) * LANES) for b in range(blocks)]
    return slots


def sum_kernel(plans, *refs):
    ins, outs = refs[: -len(plans)], refs[-len(plans) :]
    for plan, out in zip(plans, outs):
        for at, terms, ends in plan:
            total = sum(ins[number][entry].astype(F32) for number, entry in terms)
            out[at] = total.astype(out.dtype)
            if ends:
                end = total.shape[0] - 1
                last = total[end:] + sum(ins[n][entry].astype(F32) for n, entry in ends)
                out[at, end:] = last.astype(out.dtype)


def stage_sums(inputs, plans, outs):
    return pl.pallas_call(
        functools.partial(sum_kernel, plans),
        out_shape=outs,
        in_specs=[VMEM] * len(inputs),
        out_specs=[VMEM] * len(outs),
        compiler_params=params(12),
        cost_estimate=cost(0, 2**22),
    )(*inputs)


def terms_of(parts, earlier, h, entry):
    return [(0, (h, entry)), (1, (h, entry))] + [
        (2 + parts * e + h, entry) for e in range(earlier)
    ]


def far_sums(keep, taken, earlier, ends=()):
    parts, chunks, *block = keep.shape
    half = chunks // 2 ** (len(earlier) + 1)
    base = 2 + parts * len(earlier)
    plans = [
        [
            (
                n,
                terms_of(parts, len(earlier), h, half + n),
                [(base + e, half + n) for e in range(len(ends))] if h == 0 else [],
            )
            for n in range(half)
        ]
        for h in range(parts)
    ]
    outs = [shape((half, *block), LOW)] * parts
    return stage_sums([keep, taken, *[t for e in earlier for t in e], *ends], plans, outs)


def near_sums(keep, taken, earlier, inner, ends=()):
    parts, _, *block = keep.shape
    base = 2 + parts * len(earlier)
    plans = [
        [
            (
                h,
                terms_of(parts, len(earlier), h, k),
                [(base + e, k) for e in range(len(ends))] if h == 0 else [],
            )
            for h in range(parts)
        ]
        for k in range(inner)
    ]
    outs = [shape((parts, *block), F32 if k == 0 else LOW) for k in range(inner)]
    return stage_sums([keep, taken, *[t for e in earlier for t in e], *ends], plans, outs)


def lamb_values(weight, grad, first, second):
    m_one = beta_one * first + (1.0 - beta_one) * grad
    m_two = beta_two * second + (1.0 - beta_two) * grad * grad
    step_dir = (
        m_one
        / (1.0 - beta_one**adam_step)
        / (jnp.sqrt(m_two / (1.0 - beta_two**adam_step)) + adam_eps)
        + decay_rate * weight
    )
    return m_one, m_two, step_dir


def whole_sum(value):
    return jnp.sum(jnp.sum(value, 0, keepdims=True), 1, keepdims=True)


def lamb_kernel(spans, groups, terms, norm_ends, prior, *refs):
    weight_ref, one_ref, two_ref = refs[:3]
    norm_refs = refs[3:6] if norm_ends else ()
    first = 3 + len(norm_refs)
    term_refs = refs[first : first + terms]
    prior_refs = refs[first + terms : first + terms + prior]
    outs = refs[first + terms + prior :]
    mats, rows, _ = weight_ref.shape
    base, start = spans
    lane = lax.broadcasted_iota(jnp.int32, (8, LANES), 1)
    line = lax.broadcasted_iota(jnp.int32, (8, LANES), 0)
    squares = prior_refs[0][...] if prior else jnp.zeros((8, LANES), F32)
    weight_sq = [jnp.zeros((1, LANES), F32)] * mats
    update_sq = [jnp.zeros((1, LANES), F32)] * mats
    for used, entry, slots in groups:
        for at, (which, column) in enumerate(slots):
            grad = sum(term_refs[t][entry, at].astype(F32) for t in used)
            j, column = which - base, column - start
            span = slice(column, column + LANES)
            weight = weight_ref[j, :, span]
            m_one, m_two, step = lamb_values(weight, grad, one_ref[j, :, span], two_ref[j, :, span])
            for ref, value in zip(outs, (grad, m_one, m_two, step)):
                ref[j, :, span] = value
            weight_sq[j] += jnp.sum(weight * weight, 0, keepdims=True)
            update_sq[j] += jnp.sum(step * step, 0, keepdims=True)
    for j in range(mats):
        spot = lane == base + j
        squares += jnp.where(spot & (line == 0), jnp.sum(weight_sq[j], 1, keepdims=True), 0.0)
        squares += jnp.where(spot & (line == 1), jnp.sum(update_sq[j], 1, keepdims=True), 0.0)
    if norm_ends:
        used, entry = norm_ends
        last = term_refs[used[0]].shape[1] - 1
        row = sum(term_refs[t][entry, last].astype(F32)[0:1] for t in used)
        for i in range(4):
            weight = norm_refs[0][i : i + 1, :]
            grad = row[:, i * rows : (i + 1) * rows]
            m_one, m_two, step = lamb_values(
                weight, grad, norm_refs[1][i : i + 1, :], norm_refs[2][i : i + 1, :]
            )
            for ref, value in zip(outs[5:], (grad, m_one, m_two, step)):
                ref[i : i + 1, :] = value
            spot = lane == 6 + i
            squares += jnp.where(spot & (line == 0), whole_sum(weight * weight), 0.0)
            squares += jnp.where(spot & (line == 1), whole_sum(step * step), 0.0)
    outs[4][...] = squares


def lamb_call(groups, terms, state, norm_state=(), norm_ends=None, prior=(), at=None):
    total, rows, width = state[0].shape
    mats, wide = at or (total, width)
    spans = (0, width - wide)
    part = pl.BlockSpec((mats, rows, wide), lambda i: (0, 0, width // wide - 1))
    outs = [shape((total, rows, width), F32)] * 4 + [shape((8, LANES), F32)]
    if norm_ends:
        outs += [shape(norm_state[0].shape, F32)] * 4
    others, kept = [*norm_state, *terms, *prior[4:]], prior[:4]
    return pl.pallas_call(
        lambda *refs: lamb_kernel(
            spans, groups, len(terms), norm_ends, len(prior[4:]),
            *refs[: 3 + len(others)], *refs[3 + len(others) + len(kept) :],
        ),
        out_shape=outs,
        grid=(1,),
        in_specs=[part] * 3
        + [whole(a) for a in others]
        + [pl.BlockSpec(memory_space=pl.ANY)] * len(kept),
        out_specs=[part] * 4 + [whole(a) for a in outs[4:]],
        input_output_aliases={3 + len(others) + n: n for n in range(len(kept))},
        compiler_params=params(12),
        cost_estimate=cost(0, 2**22),
    )(*state, *others, *kept)


def on_device(
    latents,
    lengths,
    cotangent,
    matrices,
    norm_params,
    moment1_mat,
    moment2_mat,
    moment1_norm,
    moment2_norm,
):
    _, length, width = latents.shape
    dim = width // HEADS
    scale = 1.0 / math.sqrt(dim)
    power = scale * math.log2(math.e)
    dp, fsdp = lax.axis_size("dp"), lax.axis_size("fsdp")
    count = dp * fsdp
    rows = matrices.shape[1]
    index = lax.axis_index("dp") * fsdp + lax.axis_index("fsdp")
    ring = dp == 8 and fsdp == 4 and rows == 32
    inner, pair = fsdp, fsdp
    block = 256 if length % 256 == 0 else length
    low_mats = matrices.astype(LOW)
    low_norms = norm_params.astype(LOW)

    if ring:
        firsts, seconds = (2 * fsdp, 4 * fsdp), (4 * fsdp, 2 * fsdp)
        half_blocks = width // 2 // LANES
        order_end = (2 * fsdp, 4 * fsdp)
        masks = [
            [m ^ side for side in (0, pair) for m in mask_order(o, inner)]
            for o in zip(firsts, seconds)
        ] + [
            [m ^ side ^ k for side in (0, pair) for k in range(inner) for m in mask_order(order_end, 1)]
        ]
        table = jnp.bitwise_xor(jnp.array(masks, jnp.int32), index.astype(jnp.int32))
        away = jnp.bitwise_xor(jnp.arange(count, dtype=jnp.int32), index.astype(jnp.int32))[None]

        def bit(mask, weight):
            return jnp.where(away & jnp.array(mask, jnp.int32)[:, None] != 0, weight, 0)

        places = (
            (away & (inner - 1))
            + bit(firsts, inner)
            + bit(seconds, 2 * inner)
            + bit([pair] * 2, count // 2)
        ).astype(jnp.int32)
        lower = rows // 2
        shard = by_columns(low_mats[:3], 2).reshape(2, 3 * half_blocks, 2, lower, LANES)
        shard = shard.transpose(0, 2, 1, 3, 4).reshape(2, 6 * half_blocks, lower, LANES)
        norm_rows = jnp.pad(
            low_norms.reshape(1, 1, 1, 4 * rows), ((0, 1), (0, 0), (0, lower - 1), (0, 0))
        )
        shard = jnp.concatenate([shard, norm_rows], 1)
        in_size, mid_size = 3 * half_blocks + 1, 2 * half_blocks
        eighth = count // 4
        halves = [
            (h, side * count // 2 + part * eighth)
            for h in range(2)
            for side in range(2)
            for part in range(2)
        ]
        layout_in = tuple((h, start, h * in_size) for h, start in halves)
        layout_out = tuple((h, start, h * mid_size) for h, start in halves)
        layout_out += tuple((2, n * eighth, 2 * mid_size) for n in range(4))

        def ids(size, j):
            return [h * size + j * half_blocks + b for h in range(2) for b in range(half_blocks)]

        blocks_in = [ids(in_size, j) for j in range(3)]
        blocks_out = [ids(mid_size, j) for j in range(2)]
        blocks_out.append([2 * mid_size + b for b in range(2 * half_blocks)])
        norm_block = in_size - 1
        scratch_blocks = (2 * in_size, 2 * mid_size + 2 * half_blocks)

        def near_of(value):
            return [value] + [swap(value, k, count) for k in range(1, inner)]

        def halves_of(near):
            return [jnp.stack([n[h] for n in near]) for h in range(2)]

        def grow(held, taken):
            return [jnp.concatenate(both) for both in zip(held, taken)]

        def with_pairs(held, taken, early):
            late = swap_all(taken, [pair, pair], count)
            return [a for h in range(2) for a in (held[h], taken[h], early[h], late[h])]

        near = near_of(shard)
        end = by_columns(low_mats[5:], 1)
        end = jnp.concatenate([end, swap(end, order_end[0], count)])
        held = halves_of(after(near, end))
        taken = swap_all(held, firsts, count)
        end = jnp.concatenate([end, swap(after(end, *held), order_end[1], count)])
        held = grow(held, after(taken, end))
        taken = swap_all(held, seconds, count)
        early = swap_all(held, [pair, pair], count)
        mid = near_of(after(by_columns(low_mats[3:5], 2), *held))
        end = jnp.concatenate([end, swap(after(end, *held), 1, count)])
        late = swap_all(after(taken, end, *mid), [pair, pair], count)
        parts_in = [a for h in range(2) for a in (held[h], taken[h], early[h], late[h])]
        mid = halves_of(mid)
        end = [end, swap(after(end, *mid), 2, count)]
        norm_vals = []
    else:
        weights_in = lax.all_gather(low_mats[:3], AXES, axis=1, tiled=True)
        weights_out = lax.all_gather(low_mats[3:], AXES, axis=1, tiled=True)
        norm_vals = [lax.all_gather(low_norms, AXES, axis=1, tiled=True).astype(F32)]
        table = places = jnp.zeros((1, 1), jnp.int32)
        rows = width
        parts_in, parts_out = [by_columns(weights_in, 1)], [by_columns(weights_out, 1)]
        layout_in = layout_out = ((0, 0, 0),)
        per = width // LANES
        blocks_in = blocks_out = [list(range(j * per, (j + 1) * per)) for j in range(3)]
        scratch_blocks = (3 * per, 3 * per)
        norm_block = None

    ends = jnp.cumsum(lengths[0, :-1])
    sets = ends.shape[0]
    segment = jnp.sum(
        (jnp.arange(length, dtype=jnp.int32)[:, None] >= ends[None, :]).astype(jnp.int32), axis=1
    )
    live = (segment < sets).astype(F32)[:, None]
    lanes = jnp.arange(LANES, dtype=jnp.int32)[None, :]
    same = segment[:, None] == lanes
    mark_in = same.astype(LOW)
    mark_out = jnp.where(same | (lanes > sets), 0.0, mask_depth).astype(LOW)

    x, dz = latents[0], cotangent[0]
    steps = (length // block,)
    if ring:
        taken = swap_all(mid, firsts, count)
        x = after(x, *mid)
    held_rows = pl.BlockSpec((4, width), lambda i: (0, 0))
    two_rows = pl.BlockSpec((2, width), lambda i: (0, 0))
    anywhere = pl.BlockSpec(memory_space=pl.ANY)
    scratch_in, scratch_out = (pltpu.VMEM((n, width, LANES), LOW) for n in scratch_blocks)
    norm_scratch, sem_scratch = pltpu.VMEM((count, LANES), F32), pltpu.SemaphoreType.DMA
    hidden_one, qkv, norm_vals = pl.pallas_call(
        functools.partial(
            project_kernel, layout_in, rows, blocks_in, norm_block, len(parts_in)
        ),
        grid=steps,
        out_shape=[
            shape((length, width), LOW),
            shape((length, 3 * width), LOW),
            shape((4, width), F32),
        ],
        in_specs=[SMEM, rows_of(x, block)]
        + [anywhere] * len(parts_in)
        + [held_rows] * len(norm_vals),
        out_specs=[
            pl.BlockSpec((block, width), lambda i: (i, 0)),
            pl.BlockSpec((block, 3 * width), lambda i: (i, 0)),
            held_rows,
        ],
        scratch_shapes=[scratch_in, norm_scratch, sem_scratch],
        compiler_params=params(18),
        cost_estimate=cost(6 * length * width * width, 12 * width * width),
    )(table, x, *parts_in, *norm_vals)
    x = latents[0]

    group = 2
    marks = [pl.BlockSpec((length, LANES), lambda h: (0, 0))] * 2

    def heads_at(first):
        return pl.BlockSpec((length, dim * group), lambda h: (0, first // group + h))

    def sums_at(first):
        return pl.BlockSpec((group, 1, length), lambda h: (first // group + h, 0, 0))

    def attend(first, number, qkv):
        return pl.pallas_call(
            functools.partial(attend_kernel, group, dim, power),
            grid=(number // group,),
            in_specs=[heads_at(first + i * HEADS) for i in range(3)] + marks,
            out_specs=[heads_at(0), sums_at(0)],
            out_shape=[shape((length, number * dim), LOW), shape((number, 1, length), F32)],
            compiler_params=params(14),
            cost_estimate=cost(8 * length * length * number * dim, 8 * length * number * dim),
        )(qkv, qkv, qkv, mark_in, mark_out)

    ahead = HEADS // 2
    if ring:
        mid = grow(mid, after(taken, hidden_one))
        taken = swap_all(mid, seconds, count)
        early = swap_all(mid, [pair, pair], count)
        attended, log_sums = zip(*[attend(f, ahead, after(qkv, *mid)) for f in (0, ahead)])
        end_late = [swap(e, pair, count) for e in after(end, *attended)]
        parts_out = with_pairs(mid, after(taken, *attended), early) + end + end_late
    else:
        attended, log_sums = zip(*[attend(f, ahead, qkv) for f in (0, ahead)])

    row_block = pl.BlockSpec((block, width), lambda i: (i, 0))
    low_rows = shape((length, width), LOW)
    sides, parts = (2, 2) if ring else (1, 1)
    chunk_shape = (parts, count // sides if ring else 1)
    mat_blocks = width // LANES

    def chunks_of(blocks, extra=0):
        size = blocks // parts + extra
        return [shape((*chunk_shape, size, rows, LANES), LOW)] * sides

    dnorm_two, result, dmid, dattended, *out_grads = pl.pallas_call(
        functools.partial(
            middle_kernel, layout_out, rows, blocks_out, len(attended), sides, pair
        ),
        grid=steps,
        out_shape=[
            shape((2, width), F32),
            low_rows,
            shape((length, width), F32),
            low_rows,
            *chunks_of(3 * mat_blocks),
        ],
        in_specs=[SMEM, SMEM, row_block, row_block, rows_of(live, block), held_rows]
        + [rows_of(a, block) for a in attended]
        + [anywhere] * len(parts_out),
        out_specs=[two_rows] + [row_block] * 3 + [anywhere] * sides,
        scratch_shapes=[
            scratch_out,
            *[pltpu.VMEM((3, length, width), LOW)] * 2,
            pltpu.VMEM((3 * mat_blocks, width, LANES), LOW),
            sem_scratch,
        ],
        compiler_params=params(42),
        cost_estimate=cost(18 * length * width * width, 24 * width * width),
    )(table, places, x, dz, live, norm_vals, *attended, *parts_out)

    def attend_back(first, number, dattended, base, total, extra=0, prior=()):
        side = first // ahead
        inside = first - side * ahead
        blocks = 3 * group * dim // LANES
        outs = chunks_of(blocks * total, extra)
        return pl.pallas_call(
            functools.partial(
                attend_back_kernel, group, dim, power, scale, base, extra, len(prior), pair
            ),
            grid=(number // group,),
            in_specs=[SMEM]
            + [heads_at(first + i * HEADS) for i in range(3)]
            + [heads_at(first), heads_at(inside), *marks, sums_at(inside), whole(hidden_one)]
            + [anywhere] * len(prior),
            out_specs=[pl.BlockSpec((3, length, dim * group), lambda h: (0, 0, h))]
            + [anywhere] * sides,
            out_shape=[shape((3, length, number * dim), LOW), *outs],
            input_output_aliases={10 + n: 1 + n for n in range(len(prior))},
            scratch_shapes=[pltpu.VMEM((2 * blocks, width, LANES), LOW), sem_scratch],
            compiler_params=params(20),
            cost_estimate=cost(
                20 * length * length * number * dim + 6 * length * width * number * dim,
                16 * length * number * dim,
            ),
        )(
            places, qkv, qkv, qkv, dattended, attended[side], mark_in, mark_out,
            log_sums[side], hidden_one, *prior,
        )

    def last(dmid, grads, sides):
        packs = [shape((count // max(sides, 1), 1, rows, LANES), LOW)] * sides
        return pl.pallas_call(
            functools.partial(last_kernel, layout_in, rows, blocks_in, len(parts_in), sides),
            grid=steps,
            out_shape=[low_rows, shape((2, width), F32), *packs],
            in_specs=[SMEM, row_block, row_block, held_rows, two_rows]
            + [anywhere] * len(parts_in)
            + [rows_of(g, block) for g in grads],
            out_specs=[row_block, two_rows]
            + [pl.BlockSpec(p.shape, lambda i: (0, 0, 0, 0)) for p in packs],
            scratch_shapes=[scratch_in, norm_scratch, sem_scratch],
            compiler_params=params(18),
            cost_estimate=cost(6 * length * width * width, 6 * width * width),
        )(table, x, dmid, norm_vals, dnorm_two, *parts_in, *grads)

    state, norm_state = (matrices, moment1_mat, moment2_mat), (norm_params, moment1_norm, moment2_norm)
    if ring:
        pairs = range(1, inner)
        heads_w = group * dim

        def slots(firsts, number):
            return slots_of(
                [(j, n * heads_w, heads_w) for n in range(firsts, firsts + number) for j in range(3)], 2
            )

        def from_near(near):
            return [near[0]] + swap_all(near[1:], pairs, count)

        per = ahead // group
        keep, send = out_grads
        taken = swap(send, pair, count)
        found, *one = attend_back(0, group, after(dattended, keep), 0, per)
        grads = [found]

        sent = far_sums(keep, after(taken, found), [])
        far = [swap_all(sent, seconds, count)]
        found, keep_one, send_one = attend_back(
            group, group, after(dattended, *sent, found), 1, per, 0, one
        )
        grads.append(found)
        found, *two = attend_back(ahead, group, after(dattended, found, keep_one), 0, per, 1)
        grads.append(found)

        sent = far_sums(keep, taken, after(far, found))
        far.append(swap_all(sent, firsts, count))
        taken_one = swap(after(send_one, *sent), pair, count)
        found, keep_two, send_two = attend_back(
            ahead + group, group, after(dattended, *sent, found), 1, per, 1, two
        )
        grads.append(found)

        near = from_near(near_sums(keep, taken, [far[0], after(far[1], grads[-1])], inner))
        sent_one = far_sums(keep_one, after(taken_one, grads[-1]), [])
        far_one = [swap_all(sent_one, seconds, count)]
        grad_latents, dnorm_one, *packs = last(after(dmid, near[0], *sent_one), grads, 2)

        sent_one = far_sums(keep_one, taken_one, after(far_one, grad_latents, *near))
        far_one.append(swap_all(sent_one, firsts, count))
        taken_two, ends = swap_all(after((send_two, packs[1]), *sent_one), [pair, pair], count)
        ends = [packs[0], ends]

        far_one, taken_two, ends = after((far_one, taken_two, ends), far_one, taken_two, ends)
        near_one = near_sums(keep_one, taken_one, far_one, inner)
        sent_two = far_sums(keep_two, taken_two, [], ends)
        near_one, sent_two = after((near_one, sent_two), near_one, sent_two)
        near_one = from_near(near_one)
        far_two = [swap_all(sent_two, seconds, count)]
        sent_two = far_sums(keep_two, taken_two, after(far_two, *near_one), ends)
        far_two.append(swap_all(sent_two, firsts, count))
        near_two = near_sums(keep_two, taken_two, far_two, inner, ends)
        groups = [(range(inner), h, s) for h, s in enumerate(slots_of([(j, 0, width) for j in (3, 4, 5)], 2))]
        groups += [(range(inner, 2 * inner), h, s) for h, s in enumerate(slots(0, per))]
        prior = lamb_call(groups, after([*near, *near_one], near_two[0]), state)
        near_two = from_near(near_two)
        near_two = after(near_two, prior[4])
        groups = [(range(inner), h, s) for h, s in enumerate(slots(per, per))]
        norm_ends = (range(inner), 0)
        found = lamb_call(
            groups, near_two, state, norm_state, norm_ends, prior, (3, per * heads_w)
        )
        grad_mats, m1_mat, m2_mat, dir_mat, squares, grad_norms, m1_norm, m2_norm, dir_norm = found
        x_bit, y_bit = order_end
        rounds = ((pair,), (x_bit, y_bit, x_bit ^ y_bit), tuple(pairs))
        squares = rounds_sum(squares, rounds, count)[:2, :10]
    else:
        first, *one = attend_back(0, ahead, dattended, 0, HEADS // group)
        second, in_grads = attend_back(
            ahead, ahead, dattended, ahead // group, HEADS // group, 0, one
        )
        grads = [first, second]
        grad_latents, dnorm_one = last(dmid, grads, 0)
        norms_local = jnp.concatenate([dnorm_one, dnorm_two], 0)
        per = group * dim // LANES
        local = in_grads[0, 0].reshape(HEADS // group, 3, per, width, LANES)
        local = local.transpose(1, 0, 2, 3, 4).reshape(3 * mat_blocks, width, LANES)
        local = jnp.concatenate([local, out_grads[0][0, 0]], 0).astype(F32)
        local = local.reshape(6, mat_blocks, width, LANES)
        local = local.transpose(0, 2, 1, 3).reshape(6, width, width)
        grad_mats = lax.psum_scatter(local, AXES, scatter_dimension=1, tiled=True)
        grad_norms = lax.psum_scatter(norms_local, AXES, scatter_dimension=1, tiled=True)
        m1_mat, m2_mat, dir_mat = lamb_values(matrices, grad_mats, moment1_mat, moment2_mat)
        m1_norm, m2_norm, dir_norm = lamb_values(norm_params, grad_norms, moment1_norm, moment2_norm)
        squares = jnp.stack(
            [
                jnp.concatenate([jnp.sum(m * m, (1, 2)), jnp.sum(n * n, 1)])
                for m, n in ((matrices, norm_params), (dir_mat, dir_norm))
            ]
        )
        squares = lax.psum(squares, AXES)
    ratios = jnp.sqrt(squares[0]) / jnp.sqrt(squares[1])
    scaled_mats = ratios[:6][:, None, None] * dir_mat
    scaled_norms = ratios[6:][:, None] * dir_norm
    return (
        result[None],
        grad_latents[None],
        grad_mats,
        grad_norms,
        scaled_mats,
        scaled_norms,
        m1_mat,
        m2_mat,
        m1_norm,
        m2_norm,
        ratios,
    )


def solution(mesh):
    return jax.shard_map(
        on_device,
        mesh=mesh,
        in_specs=(
            P(("dp", "fsdp"), None, None),
            P(("dp", "fsdp"), None),
            P(("dp", "fsdp"), None, None),
            P(None, ("dp", "fsdp"), None),
            P(None, ("dp", "fsdp")),
            P(None, ("dp", "fsdp"), None),
            P(None, ("dp", "fsdp"), None),
            P(None, ("dp", "fsdp")),
            P(None, ("dp", "fsdp")),
        ),
        out_specs=(
            P(("dp", "fsdp"), None, None),
            P(("dp", "fsdp"), None, None),
            P(None, ("dp", "fsdp"), None),
            P(None, ("dp", "fsdp")),
            P(None, ("dp", "fsdp"), None),
            P(None, ("dp", "fsdp")),
            P(None, ("dp", "fsdp"), None),
            P(None, ("dp", "fsdp"), None),
            P(None, ("dp", "fsdp")),
            P(None, ("dp", "fsdp")),
            P(),
        ),
        check_vma=False,
    )
```

```python
import functools
import math

import jax
import jax.numpy as jnp
from jax import lax
from jax.experimental import pallas as pl
from jax.experimental.pallas import tpu as pltpu
from jax.sharding import PartitionSpec as P

HEADS = 8
AXES = ("dp", "fsdp")
LANES = 128

ln_eps = 1e-05
beta_one = 0.9
beta_two = 0.999
adam_eps = 1e-06
decay_rate = 0.01
adam_step = 100.0
gelu_coef = 0.7978845608
cubic_coef = 0.044715
mask_depth = -1e30

F32 = jnp.float32
LOW = jnp.bfloat16
NT = (((1,), (1,)), ((), ()))
TN = (((0,), (0,)), ((), ()))
SMEM = pl.BlockSpec(memory_space=pltpu.SMEM)
VMEM = pl.BlockSpec(memory_space=pltpu.VMEM)


def params(mib):
    return pltpu.CompilerParams(vmem_limit_bytes=mib * 2**20)


def shape(dims, kind):
    return jax.ShapeDtypeStruct(dims, kind)


def product(left, right, dims=(((1,), (0,)), ((), ()))):
    return lax.dot_general(left, right, dims, preferred_element_type=F32)


def cost(flops, moved):
    return pl.CostEstimate(flops=int(flops), bytes_accessed=int(moved), transcendentals=0)


def whole(array):
    return pl.BlockSpec(
        array.shape, lambda i: (0,) * len(array.shape), pipeline_mode=pl.Buffered(1)
    )


def rows_of(array, block):
    lead = array.shape[:-2]
    return pl.BlockSpec((*lead, block, array.shape[-1]), lambda i: (*(0,) * len(lead), i, 0))


def swap(value, mask, count):
    return lax.ppermute(value, AXES, [(i, i ^ mask) for i in range(count)])


def swap_all(values, bits, count):
    return [swap(v, b, count) for v, b in zip(values, bits)]


def add_up(values):
    while len(values) > 1:
        values = [a + b for a, b in zip(values[::2], values[1::2])]
    return values[0]


def rounds_sum(value, rounds, count):
    for masks in rounds:
        value = add_up([value] + [swap(value, mask, count) for mask in masks])
    return value


def after(value, *others):
    return lax.optimization_barrier((value, others))[0]


def mask_order(order, inner):
    masks = list(range(inner))
    for bit in order:
        masks = masks + [m ^ bit for m in masks]
    return masks


def by_columns(shards, parts):
    mats, rows, columns = shards.shape
    blocks = columns // parts // LANES
    split = shards.reshape(mats, rows, parts, blocks, LANES)
    return split.transpose(2, 0, 3, 1, 4).reshape(parts, mats * blocks, rows, LANES)


def normalize(value):
    centered = value - jnp.mean(value, -1, keepdims=True)
    inv_std = lax.rsqrt(jnp.mean(centered * centered, -1, keepdims=True) + ln_eps)
    return centered * inv_std, inv_std


def norm_back(grad_out, normed, inv_std, gain):
    grad_normed = grad_out * gain
    return inv_std * (
        grad_normed
        - jnp.mean(grad_normed, -1, keepdims=True)
        - normed * jnp.mean(grad_normed * normed, -1, keepdims=True)
    )


def pieces_of(ref, rows):
    number, height = ref.shape[1:3]
    if height == rows:
        return [(0, number, 0, 0)]
    blocks = number // 2
    return [(0, blocks, 0, 0), (blocks, blocks, 0, height), (number - 1, 1, blocks, 0)]


def place_start(table_ref, layout, rows, refs, weight_ref, sem):
    for (line, start, first), ref in zip(layout, refs):

        @pl.loop(0, ref.shape[0], unroll=4)
        def _(n, line=line, start=start, first=first, ref=ref):
            row = pl.multiple_of(table_ref[line, start + n] * rows, rows)
            for at, number, block, lower in pieces_of(ref, rows):
                block += first
                target = weight_ref.at[block : block + number, pl.ds(row + lower, ref.shape[2])]
                pltpu.make_async_copy(ref.at[n, at : at + number], target, sem).start()


def place_wait(layout, rows, refs, weight_ref, sem):
    for (_, _, first), ref in zip(layout, refs):
        for _, number, block, _ in pieces_of(ref, rows):
            block += first
            wait_for(weight_ref.at[block : block + number, 0 : ref.shape[0] * ref.shape[2]], sem)


def wait_for(ref, sem):
    pltpu.make_async_copy(ref, ref, sem).wait()


def matrix(weight_ref, blocks, first=0, size=None):
    size = weight_ref.shape[1] if size is None else size
    return jnp.concatenate([weight_ref[b, first : first + size, :] for b in blocks], 1)


def lane_rows(low, first, number):
    lane = lax.broadcasted_iota(jnp.int32, low, 1)
    return (lane >= first) & (lane < first + number)


def spread_norms(rows, weight_ref, block, held_ref, norm_ref):
    for n in range(held_ref.shape[0]):
        held_ref[n : n + 1, :] = weight_ref[block, n * rows : n * rows + 16, :].astype(F32)[0:1]
    near = LANES // 32
    blocks = held_ref.shape[0] // near
    for i in range(4):
        total = jnp.zeros((blocks, LANES), F32)
        for z in range(near):
            value = held_ref[pl.ds(z, blocks, stride=near), :]
            value = pltpu.roll(value, (32 * (z - i)) % LANES, 1)
            total = total + jnp.where(lane_rows(total.shape, 32 * z, 32), value, 0.0)
        for b in range(blocks):
            norm_ref[i : i + 1, b * LANES : (b + 1) * LANES] = total[b : b + 1]


def pack_norms(norms, held_ref):
    near = LANES // 32
    blocks = held_ref.shape[0] // near
    held = [jnp.zeros((blocks, LANES), F32) for _ in range(near)]
    for i, norm in enumerate(norms):
        stacked = jnp.concatenate(
            [norm[:, b * LANES : (b + 1) * LANES] for b in range(blocks)], 0
        )
        for z in range(near):
            value = pltpu.roll(stacked, (32 * (i - z)) % LANES, 1)
            held[z] = held[z] + jnp.where(lane_rows(value.shape, 32 * i, 32), value, 0.0)
    for z in range(near):
        held_ref[pl.ds(z, blocks, stride=near), :] = held[z]


def project_kernel(layout, rows, blocks, norm_block, parts, table_ref, x_ref, *refs):
    chunks = refs[:parts]
    hidden_ref, out_ref, norm_ref, weight_ref, held_ref, sem = refs[-6:]
    width = x_ref.shape[1]

    @pl.when(pl.program_id(0) == 0)
    def _():
        place_start(table_ref, layout, rows, chunks, weight_ref, sem)

    normed, _ = normalize(x_ref[...].astype(F32))

    @pl.when(pl.program_id(0) == 0)
    def _():
        place_wait(layout, rows, chunks, weight_ref, sem)
        if norm_block is None:
            norm_ref[...] = refs[parts][...]
        else:
            spread_norms(rows, weight_ref, norm_block, held_ref, norm_ref)

    hidden = (normed * norm_ref[0:1, :] + norm_ref[1:2, :]).astype(LOW)
    hidden_ref[...] = hidden
    for j, ids in enumerate(blocks):
        out_ref[:, j * width : (j + 1) * width] = product(
            hidden, matrix(weight_ref, ids)
        ).astype(LOW)


def attend_kernel(group, dim, power, q_ref, k_ref, v_ref, in_ref, out_ref, o_ref, lse_ref):
    for g in range(group):
        span = slice(g * dim, (g + 1) * dim)
        keys = jnp.concatenate([k_ref[:, span], out_ref[...]], 1)
        queries = jnp.concatenate([q_ref[:, span], in_ref[...]], 1)
        scores = product(keys, queries, NT)
        top = jnp.max(scores, 0, keepdims=True)
        weight = jnp.exp2((scores - top) * power)
        total = jnp.sum(weight, 0, keepdims=True)
        probs = (weight * (1.0 / total)).astype(LOW)
        o_ref[:, span] = product(v_ref[:, span].T, probs).T.astype(LOW)
        lse_ref[g] = top * power + jnp.log2(total)


def attend_back_kernel(
    group, dim, power, scale, base, extra, prior, pair, place_ref,
    q_ref, k_ref, v_ref, do_ref, o_ref, in_ref, out_ref, lse_ref, hidden_ref, *refs,
):
    grad_ref, *outs = refs[prior:-2]
    held_ref, sem = refs[-2:]
    for g in range(group):
        span = slice(g * dim, (g + 1) * dim)
        queries, keys, grad = q_ref[:, span], k_ref[:, span], do_ref[:, span]
        both = grad.astype(F32) * o_ref[:, span].astype(F32)
        row_dot = lax.dot_general(
            jnp.ones((8, dim), F32), both, NT,
            preferred_element_type=F32, precision=lax.Precision.HIGHEST,
        )[0:1]
        scores = product(
            jnp.concatenate([keys, out_ref[...]], 1),
            jnp.concatenate([queries, in_ref[...]], 1),
            NT,
        )
        probs = jnp.exp2(scores * power - lse_ref[g])
        grad_probs = product(v_ref[:, span], grad, NT)
        grad_scores = (probs * (grad_probs - row_dot)).astype(LOW)
        grad_ref[2, :, span] = product(probs.astype(LOW), grad).astype(LOW)
        grad_ref[1, :, span] = (product(grad_scores, queries) * scale).astype(LOW)
        grad_ref[0, :, span] = (product(keys.T, grad_scores).T * scale).astype(LOW)
    parts = outs[0].shape[0]
    total = held_ref.shape[0] // 2
    size = total // parts
    step = pl.program_id(0)
    slot = lax.rem(step, 2) * total

    @pl.when(step > 1)
    def _():
        wait_rows(held_ref, 0, size, outs, sem)

    for s in range(2):

        @pl.when(slot == s * total)
        def _(s=s):
            weight_grad(
                hidden_ref, [grad_ref[j] for j in range(3)],
                place_ref, held_ref, s * total, outs, (base + step) * size, sem, pair,
            )

    @pl.when(step == pl.num_programs(0) - 1)
    def _():
        wait_rows(held_ref, 0, size, outs, sem)

        @pl.when(step > 0)
        def _():
            wait_rows(held_ref, 0, size, outs, sem)

        if extra:
            empty = held_ref.at[0:1, 0 : outs[0].shape[3]]
            held_ref[0] = jnp.zeros(held_ref.shape[1:], LOW)
            copies = [
                pltpu.make_async_copy(empty, ref.at[h, n, pl.ds(ref.shape[2] - 1, 1)], sem)
                for ref in outs
                for h in range(parts)
                for n in range(ref.shape[1])
            ]
            for copy in copies:
                copy.start()
            for copy in copies:
                copy.wait()


def middle_kernel(
    layout, rows, blocks, atts, sides, pair, table_ref, place_ref, x_ref, dz_ref, live_ref, norm_ref, *refs
):
    att_refs, chunks = refs[:atts], refs[atts : -9 - sides]
    dnorm_ref, result_ref, dmid_ref, datt_ref = refs[-9 - sides : -5 - sides]
    outs, (weight_ref, left_ref, right_ref, held_ref, sem) = refs[-5 - sides : -5], refs[-5:]
    block = x_ref.shape[0]
    here = pl.ds(pl.multiple_of(pl.program_id(0) * block, block), block)

    @pl.when(pl.program_id(0) == 0)
    def _():
        place_start(table_ref, layout, rows, chunks, weight_ref, sem)
        dnorm_ref[...] = jnp.zeros_like(dnorm_ref)

    gain, shift = norm_ref[2:3, :], norm_ref[3:4, :]
    live = live_ref[...]
    grad = dz_ref[...].astype(F32)
    dmlp = (live * grad).astype(LOW)
    right_ref[2, here, :] = dmlp

    @pl.when(pl.program_id(0) == 0)
    def _():
        place_wait(layout, rows, chunks, weight_ref, sem)

    branch, first = None, 0
    for ref in att_refs:
        left_ref[0, here, first : first + ref.shape[1]] = ref[...]
        part = product(ref[...], matrix(weight_ref, blocks[0], first, ref.shape[1]))
        branch = part if branch is None else branch + part
        first += ref.shape[1]
    middle = x_ref[...].astype(F32) + live * branch
    normed, inv_std = normalize(middle)
    hidden = (normed * gain + shift).astype(LOW)
    left_ref[1, here, :] = hidden
    upward = product(hidden, matrix(weight_ref, blocks[1]))
    square = upward * upward
    bend = jnp.tanh(gelu_coef * (upward + cubic_coef * square * upward))
    half = 0.5 * (1.0 + bend)
    active = (upward * half).astype(LOW)
    left_ref[2, here, :] = active
    slope = half + (0.5 * gelu_coef) * upward * (1.0 - bend * bend) * (
        1.0 + (3.0 * cubic_coef) * square
    )
    result_ref[...] = (middle + live * product(active, matrix(weight_ref, blocks[2]))).astype(LOW)
    dup = (product(dmlp, matrix(weight_ref, blocks[2]), NT) * slope).astype(LOW)
    right_ref[1, here, :] = dup
    dhidden = product(dup, matrix(weight_ref, blocks[1]), NT)
    dnorm_ref[0:1, :] += jnp.sum(dhidden * normed, 0, keepdims=True)
    dnorm_ref[1:2, :] += jnp.sum(dhidden, 0, keepdims=True)
    dmid = grad + norm_back(dhidden, normed, inv_std, gain)
    dmid_ref[...] = dmid
    dbranch = (live * dmid).astype(LOW)
    right_ref[0, here, :] = dbranch
    datt_ref[...] = product(dbranch, matrix(weight_ref, blocks[0]), NT).astype(LOW)

    @pl.when(pl.program_id(0) == pl.num_programs(0) - 1)
    def _():
        mats = left_ref.shape[0]
        total = held_ref.shape[0] // mats
        size = total // outs[0].shape[0]
        for j in range(mats):
            weight_grad(
                left_ref.at[j], [right_ref[j]], place_ref, held_ref, j * total, outs, j * size, sem,
                pair,
            )
        for j in range(mats):
            wait_rows(held_ref, j * total, size, outs, sem)


def last_kernel(layout, rows, blocks, parts, sides, table_ref, x_ref, dmid_ref, norm_ref, other_ref, *refs):
    chunks, grads = refs[:parts], refs[parts : -5 - sides]
    out_ref, dnorm_ref = refs[-5 - sides : -3 - sides]
    packs, (weight_ref, held_ref, sem) = refs[-3 - sides : -3], refs[-3:]

    @pl.when(pl.program_id(0) == 0)
    def _():
        place_start(table_ref, layout, rows, chunks, weight_ref, sem)
        dnorm_ref[...] = jnp.zeros_like(dnorm_ref)

    normed, inv_std = normalize(x_ref[...].astype(F32))

    @pl.when(pl.program_id(0) == 0)
    def _():
        place_wait(layout, rows, chunks, weight_ref, sem)

    total = None
    for j, ids in enumerate(blocks):
        value = jnp.concatenate([ref[j] for ref in grads], 1)
        part = product(value, matrix(weight_ref, ids), NT)
        total = part if total is None else total + part
    dnorm_ref[0:1, :] += jnp.sum(total * normed, 0, keepdims=True)
    dnorm_ref[1:2, :] += jnp.sum(total, 0, keepdims=True)
    out_ref[...] = (
        dmid_ref[...] + norm_back(total, normed, inv_std, norm_ref[0:1, :])
    ).astype(LOW)

    if packs:

        @pl.when(pl.program_id(0) == pl.num_programs(0) - 1)
        def _():
            pack_norms([ref[i : i + 1, :] for ref in (dnorm_ref, other_ref) for i in range(2)], held_ref)
            for side, ref in enumerate(packs):

                @pl.loop(0, ref.shape[0], unroll=8)
                def _(n, ref=ref, side=side):
                    row = held_ref[pl.ds(table_ref[0, side * ref.shape[0] + n], 1), :]
                    ref[n, 0] = jnp.broadcast_to(row, ref.shape[2:]).astype(LOW)


def send_rows(place_ref, held_ref, first, size, outs, block, sem, low, high, pair):
    parts, number, _, rows, _ = outs[0].shape
    chunks = [c for c in range(held_ref.shape[1] // rows) if low < (c + 1) * rows <= high]

    def start(flip):
        for chunk in chunks:
            side = int(bool((chunk ^ chunks[0]) & pair)) ^ flip if len(outs) > 1 else 0
            for h in range(parts):
                at = first + h * size
                source = held_ref.at[at : at + size, chunk * rows : (chunk + 1) * rows]
                place = place_ref[h, chunk] - side * number
                target = outs[side].at[h, place, pl.ds(block, size)]
                pltpu.make_async_copy(source, target, sem).start()

    if not chunks:
        return
    for flip in range(len(outs)):

        @pl.when((place_ref[0, chunks[0]] >= number) == (flip == 1))
        def _(flip=flip):
            start(flip)


def wait_rows(held_ref, first, size, outs, sem):
    wait_for(held_ref.at[first : first + size * outs[0].shape[0]], sem)


def weight_grad(left_ref, rights, place_ref, held_ref, first, outs, block, sem, pair):
    parts = outs[0].shape[0]
    width = left_ref.shape[1]
    step = min(256, width)
    blocks = [r.shape[1] // LANES // parts for r in rights]
    size = sum(blocks)
    for c in range(0, width, step):
        left = left_ref[:, c : c + step]
        at = first
        for right, number in zip(rights, blocks):
            grad = product(left, right, TN).astype(LOW)
            for h in range(parts):
                for b in range(number):
                    lane = (h * number + b) * LANES
                    held_ref[at + h * size + b, c : c + step, :] = grad[:, lane : lane + LANES]
            at += number
        send_rows(place_ref, held_ref, first, size, outs, block, sem, c, c + step, pair)


def slots_of(jobs, parts):
    slots = [[] for _ in range(parts)]
    for which, column, wide in jobs:
        blocks = wide // LANES // parts
        for h in range(parts):
            slots[h] += [(which, column + (h * blocks + b) * LANES) for b in range(blocks)]
    return slots


def sum_kernel(plans, *refs):
    ins, outs = refs[: -len(plans)], refs[-len(plans) :]
    for plan, out in zip(plans, outs):
        for at, terms, ends in plan:
            total = sum(ins[number][entry].astype(F32) for number, entry in terms)
            out[at] = total.astype(out.dtype)
            if ends:
                end = total.shape[0] - 1
                last = total[end:] + sum(ins[n][entry].astype(F32) for n, entry in ends)
                out[at, end:] = last.astype(out.dtype)


def stage_sums(inputs, plans, outs):
    return pl.pallas_call(
        functools.partial(sum_kernel, plans),
        out_shape=outs,
        in_specs=[VMEM] * len(inputs),
        out_specs=[VMEM] * len(outs),
        compiler_params=params(12),
        cost_estimate=cost(0, 2**22),
    )(*inputs)


def terms_of(parts, earlier, h, entry):
    return [(0, (h, entry)), (1, (h, entry))] + [
        (2 + parts * e + h, entry) for e in range(earlier)
    ]


def far_sums(keep, taken, earlier, ends=()):
    parts, chunks, *block = keep.shape
    half = chunks // 2 ** (len(earlier) + 1)
    base = 2 + parts * len(earlier)
    plans = [
        [
            (
                n,
                terms_of(parts, len(earlier), h, half + n),
                [(base + e, half + n) for e in range(len(ends))] if h == 0 else [],
            )
            for n in range(half)
        ]
        for h in range(parts)
    ]
    outs = [shape((half, *block), LOW)] * parts
    return stage_sums([keep, taken, *[t for e in earlier for t in e], *ends], plans, outs)


def near_sums(keep, taken, earlier, inner, ends=()):
    parts, _, *block = keep.shape
    base = 2 + parts * len(earlier)
    plans = [
        [
            (
                h,
                terms_of(parts, len(earlier), h, k),
                [(base + e, k) for e in range(len(ends))] if h == 0 else [],
            )
            for h in range(parts)
        ]
        for k in range(inner)
    ]
    outs = [shape((parts, *block), F32 if k == 0 else LOW) for k in range(inner)]
    return stage_sums([keep, taken, *[t for e in earlier for t in e], *ends], plans, outs)


def lamb_values(weight, grad, first, second):
    m_one = beta_one * first + (1.0 - beta_one) * grad
    m_two = beta_two * second + (1.0 - beta_two) * grad * grad
    step_dir = (
        m_one
        / (1.0 - beta_one**adam_step)
        / (jnp.sqrt(m_two / (1.0 - beta_two**adam_step)) + adam_eps)
        + decay_rate * weight
    )
    return m_one, m_two, step_dir


def whole_sum(value):
    return jnp.sum(jnp.sum(value, 0, keepdims=True), 1, keepdims=True)


def lamb_kernel(spans, groups, terms, norm_ends, prior, *refs):
    weight_ref, one_ref, two_ref = refs[:3]
    norm_refs = refs[3:6] if norm_ends else ()
    first = 3 + len(norm_refs)
    term_refs = refs[first : first + terms]
    prior_refs = refs[first + terms : first + terms + prior]
    outs = refs[first + terms + prior :]
    mats, rows, _ = weight_ref.shape
    base, start = spans
    lane = lax.broadcasted_iota(jnp.int32, (8, LANES), 1)
    line = lax.broadcasted_iota(jnp.int32, (8, LANES), 0)
    squares = prior_refs[0][...] if prior else jnp.zeros((8, LANES), F32)
    weight_sq = [jnp.zeros((1, LANES), F32)] * mats
    update_sq = [jnp.zeros((1, LANES), F32)] * mats
    for used, entry, slots in groups:
        for at, (which, column) in enumerate(slots):
            grad = sum(term_refs[t][entry, at].astype(F32) for t in used)
            j, column = which - base, column - start
            span = slice(column, column + LANES)
            weight = weight_ref[j, :, span]
            m_one, m_two, step = lamb_values(weight, grad, one_ref[j, :, span], two_ref[j, :, span])
            for ref, value in zip(outs, (grad, m_one, m_two, step)):
                ref[j, :, span] = value
            weight_sq[j] += jnp.sum(weight * weight, 0, keepdims=True)
            update_sq[j] += jnp.sum(step * step, 0, keepdims=True)
    for j in range(mats):
        spot = lane == base + j
        squares += jnp.where(spot & (line == 0), jnp.sum(weight_sq[j], 1, keepdims=True), 0.0)
        squares += jnp.where(spot & (line == 1), jnp.sum(update_sq[j], 1, keepdims=True), 0.0)
    if norm_ends:
        used, entry = norm_ends
        last = term_refs[used[0]].shape[1] - 1
        row = sum(term_refs[t][entry, last].astype(F32)[0:1] for t in used)
        for i in range(4):
            weight = norm_refs[0][i : i + 1, :]
            grad = row[:, i * rows : (i + 1) * rows]
            m_one, m_two, step = lamb_values(
                weight, grad, norm_refs[1][i : i + 1, :], norm_refs[2][i : i + 1, :]
            )
            for ref, value in zip(outs[5:], (grad, m_one, m_two, step)):
                ref[i : i + 1, :] = value
            spot = lane == 6 + i
            squares += jnp.where(spot & (line == 0), whole_sum(weight * weight), 0.0)
            squares += jnp.where(spot & (line == 1), whole_sum(step * step), 0.0)
    outs[4][...] = squares


def lamb_call(groups, terms, state, norm_state=(), norm_ends=None, prior=(), at=None):
    total, rows, width = state[0].shape
    mats, wide = at or (total, width)
    spans = (0, width - wide)
    part = pl.BlockSpec((mats, rows, wide), lambda i: (0, 0, width // wide - 1))
    outs = [shape((total, rows, width), F32)] * 4 + [shape((8, LANES), F32)]
    if norm_ends:
        outs += [shape(norm_state[0].shape, F32)] * 4
    others, kept = [*norm_state, *terms, *prior[4:]], prior[:4]
    return pl.pallas_call(
        lambda *refs: lamb_kernel(
            spans, groups, len(terms), norm_ends, len(prior[4:]),
            *refs[: 3 + len(others)], *refs[3 + len(others) + len(kept) :],
        ),
        out_shape=outs,
        grid=(1,),
        in_specs=[part] * 3
        + [whole(a) for a in others]
        + [pl.BlockSpec(memory_space=pl.ANY)] * len(kept),
        out_specs=[part] * 4 + [whole(a) for a in outs[4:]],
        input_output_aliases={3 + len(others) + n: n for n in range(len(kept))},
        compiler_params=params(12),
        cost_estimate=cost(0, 2**22),
    )(*state, *others, *kept)


def on_device(
    latents,
    lengths,
    cotangent,
    matrices,
    norm_params,
    moment1_mat,
    moment2_mat,
    moment1_norm,
    moment2_norm,
):
    _, length, width = latents.shape
    dim = width // HEADS
    scale = 1.0 / math.sqrt(dim)
    power = scale * math.log2(math.e)
    dp, fsdp = lax.axis_size("dp"), lax.axis_size("fsdp")
    count = dp * fsdp
    rows = matrices.shape[1]
    index = lax.axis_index("dp") * fsdp + lax.axis_index("fsdp")
    ring = dp == 8 and fsdp == 4 and rows == 32
    inner, pair = fsdp, fsdp
    block = 256 if length % 256 == 0 else length
    low_mats = matrices.astype(LOW)
    low_norms = norm_params.astype(LOW)

    if ring:
        firsts, seconds = (2 * fsdp, 4 * fsdp), (4 * fsdp, 2 * fsdp)
        half_blocks = width // 2 // LANES
        order_end = (2 * fsdp, 4 * fsdp)
        masks = [
            [m ^ side for side in (0, pair) for m in mask_order(o, inner)]
            for o in zip(firsts, seconds)
        ] + [
            [m ^ side ^ k for side in (0, pair) for k in range(inner) for m in mask_order(order_end, 1)]
        ]
        table = jnp.bitwise_xor(jnp.array(masks, jnp.int32), index.astype(jnp.int32))
        away = jnp.bitwise_xor(jnp.arange(count, dtype=jnp.int32), index.astype(jnp.int32))[None]

        def bit(mask, weight):
            return jnp.where(away & jnp.array(mask, jnp.int32)[:, None] != 0, weight, 0)

        places = (
            (away & (inner - 1))
            + bit(firsts, inner)
            + bit(seconds, 2 * inner)
            + bit([pair] * 2, count // 2)
        ).astype(jnp.int32)
        lower = rows // 2
        shard = by_columns(low_mats[:3], 2).reshape(2, 3 * half_blocks, 2, lower, LANES)
        shard = shard.transpose(0, 2, 1, 3, 4).reshape(2, 6 * half_blocks, lower, LANES)
        norm_rows = jnp.pad(
            low_norms.reshape(1, 1, 1, 4 * rows), ((0, 1), (0, 0), (0, lower - 1), (0, 0))
        )
        shard = jnp.concatenate([shard, norm_rows], 1)
        in_size, mid_size = 3 * half_blocks + 1, 2 * half_blocks
        eighth = count // 4
        halves = [
            (h, side * count // 2 + part * eighth)
            for h in range(2)
            for side in range(2)
            for part in range(2)
        ]
        layout_in = tuple((h, start, h * in_size) for h, start in halves)
        layout_out = tuple((h, start, h * mid_size) for h, start in halves)
        layout_out += tuple((2, n * eighth, 2 * mid_size) for n in range(4))

        def ids(size, j):
            return [h * size + j * half_blocks + b for h in range(2) for b in range(half_blocks)]

        blocks_in = [ids(in_size, j) for j in range(3)]
        blocks_out = [ids(mid_size, j) for j in range(2)]
        blocks_out.append([2 * mid_size + b for b in range(2 * half_blocks)])
        norm_block = in_size - 1
        scratch_blocks = (2 * in_size, 2 * mid_size + 2 * half_blocks)

        def near_of(value):
            return [value] + [swap(value, k, count) for k in range(1, inner)]

        def halves_of(near):
            return [jnp.stack([n[h] for n in near]) for h in range(2)]

        def grow(held, taken):
            return [jnp.concatenate(both) for both in zip(held, taken)]

        def with_pairs(held, taken, early):
            late = swap_all(taken, [pair, pair], count)
            return [a for h in range(2) for a in (held[h], taken[h], early[h], late[h])]

        near = near_of(shard)
        end = by_columns(low_mats[5:], 1)
        flat = (order_end[0], order_end[1], order_end[0] ^ order_end[1])
        end = jnp.concatenate([end] + [swap(end, mask, count) for mask in flat])
        held = halves_of(after(near, end))
        taken = swap_all(held, firsts, count)
        held = grow(held, taken)
        taken = swap_all(held, seconds, count)
        early = swap_all(held, [pair, pair], count)
        mid = near_of(after(by_columns(low_mats[3:5], 2), *held))
        end = jnp.concatenate([end, swap(after(end, *held), 1, count)])
        late = swap_all(after(taken, end, *mid), [pair, pair], count)
        parts_in = [a for h in range(2) for a in (held[h], taken[h], early[h], late[h])]
        mid = halves_of(mid)
        end = [end, swap(after(end, *mid), 2, count)]
        norm_vals = []
    else:
        weights_in = lax.all_gather(low_mats[:3], AXES, axis=1, tiled=True)
        weights_out = lax.all_gather(low_mats[3:], AXES, axis=1, tiled=True)
        norm_vals = [lax.all_gather(low_norms, AXES, axis=1, tiled=True).astype(F32)]
        table = places = jnp.zeros((1, 1), jnp.int32)
        rows = width
        parts_in, parts_out = [by_columns(weights_in, 1)], [by_columns(weights_out, 1)]
        layout_in = layout_out = ((0, 0, 0),)
        per = width // LANES
        blocks_in = blocks_out = [list(range(j * per, (j + 1) * per)) for j in range(3)]
        scratch_blocks = (3 * per, 3 * per)
        norm_block = None

    ends = jnp.cumsum(lengths[0, :-1])
    sets = ends.shape[0]
    segment = jnp.sum(
        (jnp.arange(length, dtype=jnp.int32)[:, None] >= ends[None, :]).astype(jnp.int32), axis=1
    )
    live = (segment < sets).astype(F32)[:, None]
    lanes = jnp.arange(LANES, dtype=jnp.int32)[None, :]
    same = segment[:, None] == lanes
    mark_in = same.astype(LOW)
    mark_out = jnp.where(same | (lanes > sets), 0.0, mask_depth).astype(LOW)

    x, dz = latents[0], cotangent[0]
    steps = (length // block,)
    if ring:
        taken = swap_all(mid, firsts, count)
        x = after(x, *mid)
    held_rows = pl.BlockSpec((4, width), lambda i: (0, 0))
    two_rows = pl.BlockSpec((2, width), lambda i: (0, 0))
    anywhere = pl.BlockSpec(memory_space=pl.ANY)
    scratch_in, scratch_out = (pltpu.VMEM((n, width, LANES), LOW) for n in scratch_blocks)
    norm_scratch, sem_scratch = pltpu.VMEM((count, LANES), F32), pltpu.SemaphoreType.DMA
    hidden_one, qkv, norm_vals = pl.pallas_call(
        functools.partial(
            project_kernel, layout_in, rows, blocks_in, norm_block, len(parts_in)
        ),
        grid=steps,
        out_shape=[
            shape((length, width), LOW),
            shape((length, 3 * width), LOW),
            shape((4, width), F32),
        ],
        in_specs=[SMEM, rows_of(x, block)]
        + [anywhere] * len(parts_in)
        + [held_rows] * len(norm_vals),
        out_specs=[
            pl.BlockSpec((block, width), lambda i: (i, 0)),
            pl.BlockSpec((block, 3 * width), lambda i: (i, 0)),
            held_rows,
        ],
        scratch_shapes=[scratch_in, norm_scratch, sem_scratch],
        compiler_params=params(18),
        cost_estimate=cost(6 * length * width * width, 12 * width * width),
    )(table, x, *parts_in, *norm_vals)
    x = latents[0]

    group = 2
    marks = [pl.BlockSpec((length, LANES), lambda h: (0, 0))] * 2

    def heads_at(first):
        return pl.BlockSpec((length, dim * group), lambda h: (0, first // group + h))

    def sums_at(first):
        return pl.BlockSpec((group, 1, length), lambda h: (first // group + h, 0, 0))

    def attend(first, number, qkv):
        return pl.pallas_call(
            functools.partial(attend_kernel, group, dim, power),
            grid=(number // group,),
            in_specs=[heads_at(first + i * HEADS) for i in range(3)] + marks,
            out_specs=[heads_at(0), sums_at(0)],
            out_shape=[shape((length, number * dim), LOW), shape((number, 1, length), F32)],
            compiler_params=params(14),
            cost_estimate=cost(8 * length * length * number * dim, 8 * length * number * dim),
        )(qkv, qkv, qkv, mark_in, mark_out)

    ahead = HEADS // 2
    if ring:
        mid = grow(mid, after(taken, hidden_one))
        taken = swap_all(mid, seconds, count)
        early = swap_all(mid, [pair, pair], count)
        attended, log_sums = zip(*[attend(f, ahead, after(qkv, *mid)) for f in (0, ahead)])
        end_late = [swap(e, pair, count) for e in after(end, *attended)]
        parts_out = with_pairs(mid, after(taken, *attended), early) + end + end_late
    else:
        attended, log_sums = zip(*[attend(f, ahead, qkv) for f in (0, ahead)])

    row_block = pl.BlockSpec((block, width), lambda i: (i, 0))
    low_rows = shape((length, width), LOW)
    sides, parts = (2, 2) if ring else (1, 1)
    chunk_shape = (parts, count // sides if ring else 1)
    mat_blocks = width // LANES

    def chunks_of(blocks, extra=0):
        size = blocks // parts + extra
        return [shape((*chunk_shape, size, rows, LANES), LOW)] * sides

    dnorm_two, result, dmid, dattended, *out_grads = pl.pallas_call(
        functools.partial(
            middle_kernel, layout_out, rows, blocks_out, len(attended), sides, pair
        ),
        grid=steps,
        out_shape=[
            shape((2, width), F32),
            low_rows,
            shape((length, width), F32),
            low_rows,
            *chunks_of(3 * mat_blocks),
        ],
        in_specs=[SMEM, SMEM, row_block, row_block, rows_of(live, block), held_rows]
        + [rows_of(a, block) for a in attended]
        + [anywhere] * len(parts_out),
        out_specs=[two_rows] + [row_block] * 3 + [anywhere] * sides,
        scratch_shapes=[
            scratch_out,
            *[pltpu.VMEM((3, length, width), LOW)] * 2,
            pltpu.VMEM((3 * mat_blocks, width, LANES), LOW),
            sem_scratch,
        ],
        compiler_params=params(42),
        cost_estimate=cost(18 * length * width * width, 24 * width * width),
    )(table, places, x, dz, live, norm_vals, *attended, *parts_out)

    def attend_back(first, number, dattended, base, total, extra=0, prior=()):
        side = first // ahead
        inside = first - side * ahead
        blocks = 3 * group * dim // LANES
        outs = chunks_of(blocks * total, extra)
        return pl.pallas_call(
            functools.partial(
                attend_back_kernel, group, dim, power, scale, base, extra, len(prior), pair
            ),
            grid=(number // group,),
            in_specs=[SMEM]
            + [heads_at(first + i * HEADS) for i in range(3)]
            + [heads_at(first), heads_at(inside), *marks, sums_at(inside), whole(hidden_one)]
            + [anywhere] * len(prior),
            out_specs=[pl.BlockSpec((3, length, dim * group), lambda h: (0, 0, h))]
            + [anywhere] * sides,
            out_shape=[shape((3, length, number * dim), LOW), *outs],
            input_output_aliases={10 + n: 1 + n for n in range(len(prior))},
            scratch_shapes=[pltpu.VMEM((2 * blocks, width, LANES), LOW), sem_scratch],
            compiler_params=params(20),
            cost_estimate=cost(
                20 * length * length * number * dim + 6 * length * width * number * dim,
                16 * length * number * dim,
            ),
        )(
            places, qkv, qkv, qkv, dattended, attended[side], mark_in, mark_out,
            log_sums[side], hidden_one, *prior,
        )

    def last(dmid, grads, sides):
        packs = [shape((count // max(sides, 1), 1, rows, LANES), LOW)] * sides
        return pl.pallas_call(
            functools.partial(last_kernel, layout_in, rows, blocks_in, len(parts_in), sides),
            grid=steps,
            out_shape=[low_rows, shape((2, width), F32), *packs],
            in_specs=[SMEM, row_block, row_block, held_rows, two_rows]
            + [anywhere] * len(parts_in)
            + [rows_of(g, block) for g in grads],
            out_specs=[row_block, two_rows]
            + [pl.BlockSpec(p.shape, lambda i: (0, 0, 0, 0)) for p in packs],
            scratch_shapes=[scratch_in, norm_scratch, sem_scratch],
            compiler_params=params(18),
            cost_estimate=cost(6 * length * width * width, 6 * width * width),
        )(table, x, dmid, norm_vals, dnorm_two, *parts_in, *grads)

    state, norm_state = (matrices, moment1_mat, moment2_mat), (norm_params, moment1_norm, moment2_norm)
    if ring:
        pairs = range(1, inner)
        heads_w = group * dim

        def slots(firsts, number):
            return slots_of(
                [(j, n * heads_w, heads_w) for n in range(firsts, firsts + number) for j in range(3)], 2
            )

        def from_near(near):
            return [near[0]] + swap_all(near[1:], pairs, count)

        per = ahead // group
        keep, send = out_grads
        taken = swap(send, pair, count)
        found, *one = attend_back(0, group, after(dattended, keep), 0, per)
        grads = [found]

        sent = far_sums(keep, after(taken, found), [])
        far = [swap_all(sent, seconds, count)]
        found, keep_one, send_one = attend_back(
            group, group, after(dattended, *sent, found), 1, per, 0, one
        )
        grads.append(found)
        found, *two = attend_back(ahead, group, after(dattended, found, keep_one), 0, per, 1)
        grads.append(found)

        sent = far_sums(keep, taken, after(far, found))
        far.append(swap_all(sent, firsts, count))
        taken_one = swap(after(send_one, *sent), pair, count)
        found, keep_two, send_two = attend_back(
            ahead + group, group, after(dattended, *sent, found), 1, per, 1, two
        )
        grads.append(found)

        near = from_near(near_sums(keep, taken, [far[0], after(far[1], grads[-1])], inner))
        sent_one = far_sums(keep_one, after(taken_one, grads[-1]), [])
        far_one = [swap_all(sent_one, seconds, count)]
        grad_latents, dnorm_one, *packs = last(after(dmid, near[0], *sent_one), grads, 2)

        sent_one = far_sums(keep_one, taken_one, after(far_one, grad_latents, *near))
        far_one.append(swap_all(sent_one, firsts, count))
        taken_two, ends = swap_all(after((send_two, packs[1]), *sent_one), [pair, pair], count)
        ends = [packs[0], ends]

        far_one, taken_two, ends = after((far_one, taken_two, ends), far_one, taken_two, ends)
        near_one = near_sums(keep_one, taken_one, far_one, inner)
        sent_two = far_sums(keep_two, taken_two, [], ends)
        near_one, sent_two = after((near_one, sent_two), near_one, sent_two)
        near_one = from_near(near_one)
        far_two = [swap_all(sent_two, seconds, count)]
        sent_two = far_sums(keep_two, taken_two, after(far_two, *near_one), ends)
        far_two.append(swap_all(sent_two, firsts, count))
        near_two = near_sums(keep_two, taken_two, far_two, inner, ends)
        groups = [(range(inner), h, s) for h, s in enumerate(slots_of([(j, 0, width) for j in (3, 4, 5)], 2))]
        groups += [(range(inner, 2 * inner), h, s) for h, s in enumerate(slots(0, per))]
        prior = lamb_call(groups, after([*near, *near_one], near_two[0]), state)
        near_two = from_near(near_two)
        near_two = after(near_two, prior[4])
        groups = [(range(inner), h, s) for h, s in enumerate(slots(per, per))]
        norm_ends = (range(inner), 0)
        found = lamb_call(
            groups, near_two, state, norm_state, norm_ends, prior, (3, per * heads_w)
        )
        grad_mats, m1_mat, m2_mat, dir_mat, squares, grad_norms, m1_norm, m2_norm, dir_norm = found
        x_bit, y_bit = order_end
        rounds = ((pair,), (x_bit, y_bit, x_bit ^ y_bit), tuple(pairs))
        squares = rounds_sum(squares, rounds, count)[:2, :10]
    else:
        first, *one = attend_back(0, ahead, dattended, 0, HEADS // group)
        second, in_grads = attend_back(
            ahead, ahead, dattended, ahead // group, HEADS // group, 0, one
        )
        grads = [first, second]
        grad_latents, dnorm_one = last(dmid, grads, 0)
        norms_local = jnp.concatenate([dnorm_one, dnorm_two], 0)
        per = group * dim // LANES
        local = in_grads[0, 0].reshape(HEADS // group, 3, per, width, LANES)
        local = local.transpose(1, 0, 2, 3, 4).reshape(3 * mat_blocks, width, LANES)
        local = jnp.concatenate([local, out_grads[0][0, 0]], 0).astype(F32)
        local = local.reshape(6, mat_blocks, width, LANES)
        local = local.transpose(0, 2, 1, 3).reshape(6, width, width)
        grad_mats = lax.psum_scatter(local, AXES, scatter_dimension=1, tiled=True)
        grad_norms = lax.psum_scatter(norms_local, AXES, scatter_dimension=1, tiled=True)
        m1_mat, m2_mat, dir_mat = lamb_values(matrices, grad_mats, moment1_mat, moment2_mat)
        m1_norm, m2_norm, dir_norm = lamb_values(norm_params, grad_norms, moment1_norm, moment2_norm)
        squares = jnp.stack(
            [
                jnp.concatenate([jnp.sum(m * m, (1, 2)), jnp.sum(n * n, 1)])
                for m, n in ((matrices, norm_params), (dir_mat, dir_norm))
            ]
        )
        squares = lax.psum(squares, AXES)
    ratios = jnp.sqrt(squares[0]) / jnp.sqrt(squares[1])
    scaled_mats = ratios[:6][:, None, None] * dir_mat
    scaled_norms = ratios[6:][:, None] * dir_norm
    return (
        result[None],
        grad_latents[None],
        grad_mats,
        grad_norms,
        scaled_mats,
        scaled_norms,
        m1_mat,
        m2_mat,
        m1_norm,
        m2_norm,
        ratios,
    )


def solution(mesh):
    return jax.shard_map(
        on_device,
        mesh=mesh,
        in_specs=(
            P(("dp", "fsdp"), None, None),
            P(("dp", "fsdp"), None),
            P(("dp", "fsdp"), None, None),
            P(None, ("dp", "fsdp"), None),
            P(None, ("dp", "fsdp")),
            P(None, ("dp", "fsdp"), None),
            P(None, ("dp", "fsdp"), None),
            P(None, ("dp", "fsdp")),
            P(None, ("dp", "fsdp")),
        ),
        out_specs=(
            P(("dp", "fsdp"), None, None),
            P(("dp", "fsdp"), None, None),
            P(None, ("dp", "fsdp"), None),
            P(None, ("dp", "fsdp")),
            P(None, ("dp", "fsdp"), None),
            P(None, ("dp", "fsdp")),
            P(None, ("dp", "fsdp"), None),
            P(None, ("dp", "fsdp"), None),
            P(None, ("dp", "fsdp")),
            P(None, ("dp", "fsdp")),
            P(),
        ),
        check_vma=False,
    )
```

```python
import functools
import math

import jax
import jax.numpy as jnp
from jax import lax
from jax.experimental import pallas as pl
from jax.experimental.pallas import tpu as pltpu
from jax.sharding import PartitionSpec as P

HEADS = 8
AXES = ("dp", "fsdp")
LANES = 128

ln_eps = 1e-05
beta_one = 0.9
beta_two = 0.999
adam_eps = 1e-06
decay_rate = 0.01
adam_step = 100.0
gelu_coef = 0.7978845608
cubic_coef = 0.044715
mask_depth = -1e30

F32 = jnp.float32
LOW = jnp.bfloat16
NT = (((1,), (1,)), ((), ()))
TN = (((0,), (0,)), ((), ()))
SMEM = pl.BlockSpec(memory_space=pltpu.SMEM)
VMEM = pl.BlockSpec(memory_space=pltpu.VMEM)


def params(mib):
    return pltpu.CompilerParams(vmem_limit_bytes=mib * 2**20)


def shape(dims, kind):
    return jax.ShapeDtypeStruct(dims, kind)


def product(left, right, dims=(((1,), (0,)), ((), ()))):
    return lax.dot_general(left, right, dims, preferred_element_type=F32)


def cost(flops, moved):
    return pl.CostEstimate(flops=int(flops), bytes_accessed=int(moved), transcendentals=0)


def whole(array):
    return pl.BlockSpec(
        array.shape, lambda i: (0,) * len(array.shape), pipeline_mode=pl.Buffered(1)
    )


def rows_of(array, block):
    lead = array.shape[:-2]
    return pl.BlockSpec((*lead, block, array.shape[-1]), lambda i: (*(0,) * len(lead), i, 0))


def swap(value, mask, count):
    return lax.ppermute(value, AXES, [(i, i ^ mask) for i in range(count)])


def swap_all(values, bits, count):
    return [swap(v, b, count) for v, b in zip(values, bits)]


def add_up(values):
    while len(values) > 1:
        values = [a + b for a, b in zip(values[::2], values[1::2])]
    return values[0]


def rounds_sum(value, rounds, count):
    for masks in rounds:
        value = add_up([value] + [swap(value, mask, count) for mask in masks])
    return value


def after(value, *others):
    return lax.optimization_barrier((value, others))[0]


def mask_order(order, inner):
    masks = list(range(inner))
    for bit in order:
        masks = masks + [m ^ bit for m in masks]
    return masks


def by_columns(shards, parts):
    mats, rows, columns = shards.shape
    blocks = columns // parts // LANES
    split = shards.reshape(mats, rows, parts, blocks, LANES)
    return split.transpose(2, 0, 3, 1, 4).reshape(parts, mats * blocks, rows, LANES)


def normalize(value):
    centered = value - jnp.mean(value, -1, keepdims=True)
    inv_std = lax.rsqrt(jnp.mean(centered * centered, -1, keepdims=True) + ln_eps)
    return centered * inv_std, inv_std


def norm_back(grad_out, normed, inv_std, gain):
    grad_normed = grad_out * gain
    return inv_std * (
        grad_normed
        - jnp.mean(grad_normed, -1, keepdims=True)
        - normed * jnp.mean(grad_normed * normed, -1, keepdims=True)
    )


def pieces_of(ref, rows):
    number, height = ref.shape[1:3]
    if height == rows:
        return [(0, number, 0, 0)]
    blocks = number // 2
    return [(0, blocks, 0, 0), (blocks, blocks, 0, height), (number - 1, 1, blocks, 0)]


def place_start(table_ref, layout, rows, refs, weight_ref, sem):
    for (line, start, first), ref in zip(layout, refs):

        @pl.loop(0, ref.shape[0], unroll=4)
        def _(n, line=line, start=start, first=first, ref=ref):
            row = pl.multiple_of(table_ref[line, start + n] * rows, rows)
            for at, number, block, lower in pieces_of(ref, rows):
                block += first
                target = weight_ref.at[block : block + number, pl.ds(row + lower, ref.shape[2])]
                pltpu.make_async_copy(ref.at[n, at : at + number], target, sem).start()


def place_wait(layout, rows, refs, weight_ref, sem):
    for (_, _, first), ref in zip(layout, refs):
        for _, number, block, _ in pieces_of(ref, rows):
            block += first
            wait_for(weight_ref.at[block : block + number, 0 : ref.shape[0] * ref.shape[2]], sem)


def wait_for(ref, sem):
    pltpu.make_async_copy(ref, ref, sem).wait()


def matrix(weight_ref, blocks, first=0, size=None):
    size = weight_ref.shape[1] if size is None else size
    return jnp.concatenate([weight_ref[b, first : first + size, :] for b in blocks], 1)


def lane_rows(low, first, number):
    lane = lax.broadcasted_iota(jnp.int32, low, 1)
    return (lane >= first) & (lane < first + number)


def spread_norms(rows, weight_ref, block, held_ref, norm_ref):
    for n in range(held_ref.shape[0]):
        held_ref[n : n + 1, :] = weight_ref[block, n * rows : n * rows + 16, :].astype(F32)[0:1]
    near = LANES // 32
    blocks = held_ref.shape[0] // near
    for i in range(4):
        total = jnp.zeros((blocks, LANES), F32)
        for z in range(near):
            value = held_ref[pl.ds(z, blocks, stride=near), :]
            value = pltpu.roll(value, (32 * (z - i)) % LANES, 1)
            total = total + jnp.where(lane_rows(total.shape, 32 * z, 32), value, 0.0)
        for b in range(blocks):
            norm_ref[i : i + 1, b * LANES : (b + 1) * LANES] = total[b : b + 1]


def pack_norms(norms, held_ref):
    near = LANES // 32
    blocks = held_ref.shape[0] // near
    held = [jnp.zeros((blocks, LANES), F32) for _ in range(near)]
    for i, norm in enumerate(norms):
        stacked = jnp.concatenate(
            [norm[:, b * LANES : (b + 1) * LANES] for b in range(blocks)], 0
        )
        for z in range(near):
            value = pltpu.roll(stacked, (32 * (i - z)) % LANES, 1)
            held[z] = held[z] + jnp.where(lane_rows(value.shape, 32 * i, 32), value, 0.0)
    for z in range(near):
        held_ref[pl.ds(z, blocks, stride=near), :] = held[z]


def project_kernel(layout, rows, blocks, norm_block, parts, table_ref, x_ref, *refs):
    chunks = refs[:parts]
    hidden_ref, out_ref, norm_ref, weight_ref, held_ref, sem = refs[-6:]
    width = x_ref.shape[1]

    @pl.when(pl.program_id(0) == 0)
    def _():
        place_start(table_ref, layout, rows, chunks, weight_ref, sem)

    normed, _ = normalize(x_ref[...].astype(F32))

    @pl.when(pl.program_id(0) == 0)
    def _():
        place_wait(layout, rows, chunks, weight_ref, sem)
        if norm_block is None:
            norm_ref[...] = refs[parts][...]
        else:
            spread_norms(rows, weight_ref, norm_block, held_ref, norm_ref)

    hidden = (normed * norm_ref[0:1, :] + norm_ref[1:2, :]).astype(LOW)
    hidden_ref[...] = hidden
    for j, ids in enumerate(blocks):
        out_ref[:, j * width : (j + 1) * width] = product(
            hidden, matrix(weight_ref, ids)
        ).astype(LOW)


def attend_kernel(group, dim, power, q_ref, k_ref, v_ref, in_ref, out_ref, o_ref, lse_ref):
    for g in range(group):
        span = slice(g * dim, (g + 1) * dim)
        keys = jnp.concatenate([k_ref[:, span], out_ref[...]], 1)
        queries = jnp.concatenate([q_ref[:, span], in_ref[...]], 1)
        scores = product(keys, queries, NT)
        top = jnp.max(scores, 0, keepdims=True)
        weight = jnp.exp2((scores - top) * power)
        total = jnp.sum(weight, 0, keepdims=True)
        probs = (weight * (1.0 / total)).astype(LOW)
        o_ref[:, span] = product(v_ref[:, span].T, probs).T.astype(LOW)
        lse_ref[g] = top * power + jnp.log2(total)


def attend_back_kernel(
    group, dim, power, scale, base, extra, prior, pair, place_ref,
    q_ref, k_ref, v_ref, do_ref, o_ref, in_ref, out_ref, lse_ref, hidden_ref, *refs,
):
    grad_ref, *outs = refs[prior:-2]
    held_ref, sem = refs[-2:]
    for g in range(group):
        span = slice(g * dim, (g + 1) * dim)
        queries, keys, grad = q_ref[:, span], k_ref[:, span], do_ref[:, span]
        both = grad.astype(F32) * o_ref[:, span].astype(F32)
        row_dot = lax.dot_general(
            jnp.ones((8, dim), F32), both, NT,
            preferred_element_type=F32, precision=lax.Precision.HIGHEST,
        )[0:1]
        scores = product(
            jnp.concatenate([keys, out_ref[...]], 1),
            jnp.concatenate([queries, in_ref[...]], 1),
            NT,
        )
        probs = jnp.exp2(scores * power - lse_ref[g])
        grad_probs = product(v_ref[:, span], grad, NT)
        grad_scores = (probs * (grad_probs - row_dot)).astype(LOW)
        grad_ref[2, :, span] = product(probs.astype(LOW), grad).astype(LOW)
        grad_ref[1, :, span] = (product(grad_scores, queries) * scale).astype(LOW)
        grad_ref[0, :, span] = (product(keys.T, grad_scores).T * scale).astype(LOW)
    parts = outs[0].shape[0]
    total = held_ref.shape[0] // 2
    size = total // parts
    step = pl.program_id(0)
    slot = lax.rem(step, 2) * total

    @pl.when(step > 1)
    def _():
        wait_rows(held_ref, 0, size, outs, sem)

    for s in range(2):

        @pl.when(slot == s * total)
        def _(s=s):
            weight_grad(
                hidden_ref, [grad_ref[j] for j in range(3)],
                place_ref, held_ref, s * total, outs, (base + step) * size, sem, pair,
            )

    @pl.when(step == pl.num_programs(0) - 1)
    def _():
        wait_rows(held_ref, 0, size, outs, sem)

        @pl.when(step > 0)
        def _():
            wait_rows(held_ref, 0, size, outs, sem)

        if extra:
            empty = held_ref.at[0:1, 0 : outs[0].shape[3]]
            held_ref[0] = jnp.zeros(held_ref.shape[1:], LOW)
            copies = [
                pltpu.make_async_copy(empty, ref.at[h, n, pl.ds(ref.shape[2] - 1, 1)], sem)
                for ref in outs
                for h in range(parts)
                for n in range(ref.shape[1])
            ]
            for copy in copies:
                copy.start()
            for copy in copies:
                copy.wait()


def middle_kernel(
    layout, rows, blocks, atts, sides, pair, table_ref, place_ref, x_ref, dz_ref, live_ref, norm_ref, *refs
):
    att_refs, chunks = refs[:atts], refs[atts : -9 - sides]
    dnorm_ref, result_ref, dmid_ref, datt_ref = refs[-9 - sides : -5 - sides]
    outs, (weight_ref, left_ref, right_ref, held_ref, sem) = refs[-5 - sides : -5], refs[-5:]
    block = x_ref.shape[0]
    here = pl.ds(pl.multiple_of(pl.program_id(0) * block, block), block)

    @pl.when(pl.program_id(0) == 0)
    def _():
        place_start(table_ref, layout, rows, chunks, weight_ref, sem)
        dnorm_ref[...] = jnp.zeros_like(dnorm_ref)

    gain, shift = norm_ref[2:3, :], norm_ref[3:4, :]
    live = live_ref[...]
    grad = dz_ref[...].astype(F32)
    dmlp = (live * grad).astype(LOW)
    right_ref[2, here, :] = dmlp

    @pl.when(pl.program_id(0) == 0)
    def _():
        place_wait(layout, rows, chunks, weight_ref, sem)

    branch, first = None, 0
    for ref in att_refs:
        left_ref[0, here, first : first + ref.shape[1]] = ref[...]
        part = product(ref[...], matrix(weight_ref, blocks[0], first, ref.shape[1]))
        branch = part if branch is None else branch + part
        first += ref.shape[1]
    middle = x_ref[...].astype(F32) + live * branch
    normed, inv_std = normalize(middle)
    hidden = (normed * gain + shift).astype(LOW)
    left_ref[1, here, :] = hidden
    upward = product(hidden, matrix(weight_ref, blocks[1]))
    square = upward * upward
    bend = jnp.tanh(gelu_coef * (upward + cubic_coef * square * upward))
    half = 0.5 * (1.0 + bend)
    active = (upward * half).astype(LOW)
    left_ref[2, here, :] = active
    slope = half + (0.5 * gelu_coef) * upward * (1.0 - bend * bend) * (
        1.0 + (3.0 * cubic_coef) * square
    )
    result_ref[...] = (middle + live * product(active, matrix(weight_ref, blocks[2]))).astype(LOW)
    dup = (product(dmlp, matrix(weight_ref, blocks[2]), NT) * slope).astype(LOW)
    right_ref[1, here, :] = dup
    dhidden = product(dup, matrix(weight_ref, blocks[1]), NT)
    dnorm_ref[0:1, :] += jnp.sum(dhidden * normed, 0, keepdims=True)
    dnorm_ref[1:2, :] += jnp.sum(dhidden, 0, keepdims=True)
    dmid = grad + norm_back(dhidden, normed, inv_std, gain)
    dmid_ref[...] = dmid
    dbranch = (live * dmid).astype(LOW)
    right_ref[0, here, :] = dbranch
    datt_ref[...] = product(dbranch, matrix(weight_ref, blocks[0]), NT).astype(LOW)

    @pl.when(pl.program_id(0) == pl.num_programs(0) - 1)
    def _():
        mats = left_ref.shape[0]
        total = held_ref.shape[0] // mats
        size = total // outs[0].shape[0]
        for j in range(mats):
            weight_grad(
                left_ref.at[j], [right_ref[j]], place_ref, held_ref, j * total, outs, j * size, sem,
                pair,
            )
        for j in range(mats):
            wait_rows(held_ref, j * total, size, outs, sem)


def last_kernel(layout, rows, blocks, parts, sides, table_ref, x_ref, dmid_ref, norm_ref, other_ref, *refs):
    chunks, grads = refs[:parts], refs[parts : -5 - sides]
    out_ref, dnorm_ref = refs[-5 - sides : -3 - sides]
    packs, (weight_ref, held_ref, sem) = refs[-3 - sides : -3], refs[-3:]

    @pl.when(pl.program_id(0) == 0)
    def _():
        place_start(table_ref, layout, rows, chunks, weight_ref, sem)
        dnorm_ref[...] = jnp.zeros_like(dnorm_ref)

    normed, inv_std = normalize(x_ref[...].astype(F32))

    @pl.when(pl.program_id(0) == 0)
    def _():
        place_wait(layout, rows, chunks, weight_ref, sem)

    total = None
    for j, ids in enumerate(blocks):
        value = jnp.concatenate([ref[j] for ref in grads], 1)
        part = product(value, matrix(weight_ref, ids), NT)
        total = part if total is None else total + part
    dnorm_ref[0:1, :] += jnp.sum(total * normed, 0, keepdims=True)
    dnorm_ref[1:2, :] += jnp.sum(total, 0, keepdims=True)
    out_ref[...] = (
        dmid_ref[...] + norm_back(total, normed, inv_std, norm_ref[0:1, :])
    ).astype(LOW)

    if packs:

        @pl.when(pl.program_id(0) == pl.num_programs(0) - 1)
        def _():
            pack_norms([ref[i : i + 1, :] for ref in (dnorm_ref, other_ref) for i in range(2)], held_ref)
            for side, ref in enumerate(packs):

                @pl.loop(0, ref.shape[0], unroll=8)
                def _(n, ref=ref, side=side):
                    row = held_ref[pl.ds(table_ref[0, side * ref.shape[0] + n], 1), :]
                    ref[n, 0] = jnp.broadcast_to(row, ref.shape[2:]).astype(LOW)


def send_rows(place_ref, held_ref, first, size, outs, block, sem, low, high, pair):
    parts, number, _, rows, _ = outs[0].shape
    chunks = [c for c in range(held_ref.shape[1] // rows) if low < (c + 1) * rows <= high]

    def start(flip):
        for chunk in chunks:
            side = int(bool((chunk ^ chunks[0]) & pair)) ^ flip if len(outs) > 1 else 0
            for h in range(parts):
                at = first + h * size
                source = held_ref.at[at : at + size, chunk * rows : (chunk + 1) * rows]
                place = place_ref[h, chunk] - side * number
                target = outs[side].at[h, place, pl.ds(block, size)]
                pltpu.make_async_copy(source, target, sem).start()

    if not chunks:
        return
    for flip in range(len(outs)):

        @pl.when((place_ref[0, chunks[0]] >= number) == (flip == 1))
        def _(flip=flip):
            start(flip)


def wait_rows(held_ref, first, size, outs, sem):
    wait_for(held_ref.at[first : first + size * outs[0].shape[0]], sem)


def weight_grad(left_ref, rights, place_ref, held_ref, first, outs, block, sem, pair):
    parts = outs[0].shape[0]
    width = left_ref.shape[1]
    step = min(256, width)
    blocks = [r.shape[1] // LANES // parts for r in rights]
    size = sum(blocks)
    for c in range(0, width, step):
        left = left_ref[:, c : c + step]
        at = first
        for right, number in zip(rights, blocks):
            grad = product(left, right, TN).astype(LOW)
            for h in range(parts):
                for b in range(number):
                    lane = (h * number + b) * LANES
                    held_ref[at + h * size + b, c : c + step, :] = grad[:, lane : lane + LANES]
            at += number
        send_rows(place_ref, held_ref, first, size, outs, block, sem, c, c + step, pair)


def slots_of(jobs, parts):
    slots = [[] for _ in range(parts)]
    for which, column, wide in jobs:
        blocks = wide // LANES // parts
        for h in range(parts):
            slots[h] += [(which, column + (h * blocks + b) * LANES) for b in range(blocks)]
    return slots


def sum_kernel(plans, *refs):
    ins, outs = refs[: -len(plans)], refs[-len(plans) :]
    for plan, out in zip(plans, outs):
        for at, terms, ends in plan:
            total = sum(ins[number][entry].astype(F32) for number, entry in terms)
            out[at] = total.astype(out.dtype)
            if ends:
                end = total.shape[0] - 1
                last = total[end:] + sum(ins[n][entry].astype(F32) for n, entry in ends)
                out[at, end:] = last.astype(out.dtype)


def stage_sums(inputs, plans, outs):
    return pl.pallas_call(
        functools.partial(sum_kernel, plans),
        out_shape=outs,
        in_specs=[VMEM] * len(inputs),
        out_specs=[VMEM] * len(outs),
        compiler_params=params(12),
        cost_estimate=cost(0, 2**22),
    )(*inputs)


def terms_of(parts, earlier, h, entry):
    return [(0, (h, entry)), (1, (h, entry))] + [
        (2 + parts * e + h, entry) for e in range(earlier)
    ]


def far_sums(keep, taken, earlier, ends=()):
    parts, chunks, *block = keep.shape
    half = chunks // 2 ** (len(earlier) + 1)
    base = 2 + parts * len(earlier)
    plans = [
        [
            (
                n,
                terms_of(parts, len(earlier), h, half + n),
                [(base + e, half + n) for e in range(len(ends))] if h == 0 else [],
            )
            for n in range(half)
        ]
        for h in range(parts)
    ]
    outs = [shape((half, *block), LOW)] * parts
    return stage_sums([keep, taken, *[t for e in earlier for t in e], *ends], plans, outs)


def near_sums(keep, taken, earlier, inner, ends=()):
    parts, _, *block = keep.shape
    base = 2 + parts * len(earlier)
    plans = [
        [
            (
                h,
                terms_of(parts, len(earlier), h, k),
                [(base + e, k) for e in range(len(ends))] if h == 0 else [],
            )
            for h in range(parts)
        ]
        for k in range(inner)
    ]
    outs = [shape((parts, *block), F32 if k == 0 else LOW) for k in range(inner)]
    return stage_sums([keep, taken, *[t for e in earlier for t in e], *ends], plans, outs)


def lamb_values(weight, grad, first, second):
    m_one = beta_one * first + (1.0 - beta_one) * grad
    m_two = beta_two * second + (1.0 - beta_two) * grad * grad
    step_dir = (
        m_one
        / (1.0 - beta_one**adam_step)
        / (jnp.sqrt(m_two / (1.0 - beta_two**adam_step)) + adam_eps)
        + decay_rate * weight
    )
    return m_one, m_two, step_dir


def whole_sum(value):
    return jnp.sum(jnp.sum(value, 0, keepdims=True), 1, keepdims=True)


def lamb_kernel(spans, groups, terms, norm_ends, prior, *refs):
    weight_ref, one_ref, two_ref = refs[:3]
    norm_refs = refs[3:6] if norm_ends else ()
    first = 3 + len(norm_refs)
    term_refs = refs[first : first + terms]
    prior_refs = refs[first + terms : first + terms + prior]
    outs = refs[first + terms + prior :]
    mats, rows, _ = weight_ref.shape
    base, start = spans
    lane = lax.broadcasted_iota(jnp.int32, (8, LANES), 1)
    line = lax.broadcasted_iota(jnp.int32, (8, LANES), 0)
    squares = prior_refs[0][...] if prior else jnp.zeros((8, LANES), F32)
    weight_sq = [jnp.zeros((1, LANES), F32)] * mats
    update_sq = [jnp.zeros((1, LANES), F32)] * mats
    for used, entry, slots in groups:
        for at, (which, column) in enumerate(slots):
            grad = sum(term_refs[t][entry, at].astype(F32) for t in used)
            j, column = which - base, column - start
            span = slice(column, column + LANES)
            weight = weight_ref[j, :, span]
            m_one, m_two, step = lamb_values(weight, grad, one_ref[j, :, span], two_ref[j, :, span])
            for ref, value in zip(outs, (grad, m_one, m_two, step)):
                ref[j, :, span] = value
            weight_sq[j] += jnp.sum(weight * weight, 0, keepdims=True)
            update_sq[j] += jnp.sum(step * step, 0, keepdims=True)
    for j in range(mats):
        spot = lane == base + j
        squares += jnp.where(spot & (line == 0), jnp.sum(weight_sq[j], 1, keepdims=True), 0.0)
        squares += jnp.where(spot & (line == 1), jnp.sum(update_sq[j], 1, keepdims=True), 0.0)
    if norm_ends:
        used, entry = norm_ends
        last = term_refs[used[0]].shape[1] - 1
        row = sum(term_refs[t][entry, last].astype(F32)[0:1] for t in used)
        for i in range(4):
            weight = norm_refs[0][i : i + 1, :]
            grad = row[:, i * rows : (i + 1) * rows]
            m_one, m_two, step = lamb_values(
                weight, grad, norm_refs[1][i : i + 1, :], norm_refs[2][i : i + 1, :]
            )
            for ref, value in zip(outs[5:], (grad, m_one, m_two, step)):
                ref[i : i + 1, :] = value
            spot = lane == 6 + i
            squares += jnp.where(spot & (line == 0), whole_sum(weight * weight), 0.0)
            squares += jnp.where(spot & (line == 1), whole_sum(step * step), 0.0)
    outs[4][...] = squares


def lamb_call(groups, terms, state, norm_state=(), norm_ends=None, prior=(), at=None):
    total, rows, width = state[0].shape
    mats, wide = at or (total, width)
    spans = (0, width - wide)
    part = pl.BlockSpec((mats, rows, wide), lambda i: (0, 0, width // wide - 1))
    outs = [shape((total, rows, width), F32)] * 4 + [shape((8, LANES), F32)]
    if norm_ends:
        outs += [shape(norm_state[0].shape, F32)] * 4
    others, kept = [*norm_state, *terms, *prior[4:]], prior[:4]
    return pl.pallas_call(
        lambda *refs: lamb_kernel(
            spans, groups, len(terms), norm_ends, len(prior[4:]),
            *refs[: 3 + len(others)], *refs[3 + len(others) + len(kept) :],
        ),
        out_shape=outs,
        grid=(1,),
        in_specs=[part] * 3
        + [whole(a) for a in others]
        + [pl.BlockSpec(memory_space=pl.ANY)] * len(kept),
        out_specs=[part] * 4 + [whole(a) for a in outs[4:]],
        input_output_aliases={3 + len(others) + n: n for n in range(len(kept))},
        compiler_params=params(12),
        cost_estimate=cost(0, 2**22),
    )(*state, *others, *kept)


def on_device(
    latents,
    lengths,
    cotangent,
    matrices,
    norm_params,
    moment1_mat,
    moment2_mat,
    moment1_norm,
    moment2_norm,
):
    _, length, width = latents.shape
    dim = width // HEADS
    scale = 1.0 / math.sqrt(dim)
    power = scale * math.log2(math.e)
    dp, fsdp = lax.axis_size("dp"), lax.axis_size("fsdp")
    count = dp * fsdp
    rows = matrices.shape[1]
    index = lax.axis_index("dp") * fsdp + lax.axis_index("fsdp")
    ring = dp == 8 and fsdp == 4 and rows == 32
    inner, pair = fsdp, fsdp
    block = 256 if length % 256 == 0 else length
    low_mats = matrices.astype(LOW)
    low_norms = norm_params.astype(LOW)

    if ring:
        firsts, seconds = (2 * fsdp, 4 * fsdp), (4 * fsdp, 2 * fsdp)
        half_blocks = width // 2 // LANES
        order_end = (2 * fsdp, 4 * fsdp)
        masks = [
            [m ^ side for side in (0, pair) for m in mask_order(o, inner)]
            for o in zip(firsts, seconds)
        ] + [
            [m ^ side ^ k for side in (0, pair) for k in range(inner) for m in mask_order(order_end, 1)]
        ]
        table = jnp.bitwise_xor(jnp.array(masks, jnp.int32), index.astype(jnp.int32))
        away = jnp.bitwise_xor(jnp.arange(count, dtype=jnp.int32), index.astype(jnp.int32))[None]

        def bit(mask, weight):
            return jnp.where(away & jnp.array(mask, jnp.int32)[:, None] != 0, weight, 0)

        places = (
            (away & (inner - 1))
            + bit(firsts, inner)
            + bit(seconds, 2 * inner)
            + bit([pair] * 2, count // 2)
        ).astype(jnp.int32)
        lower = rows // 2
        shard = by_columns(low_mats[:3], 2).reshape(2, 3 * half_blocks, 2, lower, LANES)
        shard = shard.transpose(0, 2, 1, 3, 4).reshape(2, 6 * half_blocks, lower, LANES)
        norm_rows = jnp.pad(
            low_norms.reshape(1, 1, 1, 4 * rows), ((0, 1), (0, 0), (0, lower - 1), (0, 0))
        )
        shard = jnp.concatenate([shard, norm_rows], 1)
        in_size, mid_size = 3 * half_blocks + 1, 2 * half_blocks
        eighth = count // 4
        halves = [
            (h, side * count // 2 + part * eighth)
            for h in range(2)
            for side in range(2)
            for part in range(2)
        ]
        layout_in = tuple((h, start, h * in_size) for h, start in halves)
        layout_out = tuple((h, start, h * mid_size) for h, start in halves)
        layout_out += tuple((2, n * eighth, 2 * mid_size) for n in range(4))

        def ids(size, j):
            return [h * size + j * half_blocks + b for h in range(2) for b in range(half_blocks)]

        blocks_in = [ids(in_size, j) for j in range(3)]
        blocks_out = [ids(mid_size, j) for j in range(2)]
        blocks_out.append([2 * mid_size + b for b in range(2 * half_blocks)])
        norm_block = in_size - 1
        scratch_blocks = (2 * in_size, 2 * mid_size + 2 * half_blocks)

        def near_of(value):
            return [value] + [swap(value, k, count) for k in range(1, inner)]

        def halves_of(near):
            return [jnp.stack([n[h] for n in near]) for h in range(2)]

        def grow(held, taken):
            return [jnp.concatenate(both) for both in zip(held, taken)]

        def with_pairs(held, taken, early):
            late = swap_all(taken, [pair, pair], count)
            return [a for h in range(2) for a in (held[h], taken[h], early[h], late[h])]

        near = near_of(shard)
        end = by_columns(low_mats[5:], 1)
        flat = (order_end[0], order_end[1], order_end[0] ^ order_end[1])
        end = jnp.concatenate([end] + [swap(end, mask, count) for mask in flat])
        held = halves_of(after(near, end))
        taken = swap_all(held, firsts, count)
        end = jnp.concatenate([end, swap(after(end, *held), 1, count)])
        held = grow(held, after(taken, end))
        taken = swap_all(held, seconds, count)
        early = swap_all(held, [pair, pair], count)
        mid = near_of(after(by_columns(low_mats[3:5], 2), *held))
        late = swap_all(after(taken, end, *mid), [pair, pair], count)
        parts_in = [a for h in range(2) for a in (held[h], taken[h], early[h], late[h])]
        mid = halves_of(mid)
        end = [end, swap(after(end, *mid), 2, count)]
        norm_vals = []
    else:
        weights_in = lax.all_gather(low_mats[:3], AXES, axis=1, tiled=True)
        weights_out = lax.all_gather(low_mats[3:], AXES, axis=1, tiled=True)
        norm_vals = [lax.all_gather(low_norms, AXES, axis=1, tiled=True).astype(F32)]
        table = places = jnp.zeros((1, 1), jnp.int32)
        rows = width
        parts_in, parts_out = [by_columns(weights_in, 1)], [by_columns(weights_out, 1)]
        layout_in = layout_out = ((0, 0, 0),)
        per = width // LANES
        blocks_in = blocks_out = [list(range(j * per, (j + 1) * per)) for j in range(3)]
        scratch_blocks = (3 * per, 3 * per)
        norm_block = None

    ends = jnp.cumsum(lengths[0, :-1])
    sets = ends.shape[0]
    segment = jnp.sum(
        (jnp.arange(length, dtype=jnp.int32)[:, None] >= ends[None, :]).astype(jnp.int32), axis=1
    )
    live = (segment < sets).astype(F32)[:, None]
    lanes = jnp.arange(LANES, dtype=jnp.int32)[None, :]
    same = segment[:, None] == lanes
    mark_in = same.astype(LOW)
    mark_out = jnp.where(same | (lanes > sets), 0.0, mask_depth).astype(LOW)

    x, dz = latents[0], cotangent[0]
    steps = (length // block,)
    if ring:
        taken = swap_all(mid, firsts, count)
        x = after(x, *mid)
    held_rows = pl.BlockSpec((4, width), lambda i: (0, 0))
    two_rows = pl.BlockSpec((2, width), lambda i: (0, 0))
    anywhere = pl.BlockSpec(memory_space=pl.ANY)
    scratch_in, scratch_out = (pltpu.VMEM((n, width, LANES), LOW) for n in scratch_blocks)
    norm_scratch, sem_scratch = pltpu.VMEM((count, LANES), F32), pltpu.SemaphoreType.DMA
    hidden_one, qkv, norm_vals = pl.pallas_call(
        functools.partial(
            project_kernel, layout_in, rows, blocks_in, norm_block, len(parts_in)
        ),
        grid=steps,
        out_shape=[
            shape((length, width), LOW),
            shape((length, 3 * width), LOW),
            shape((4, width), F32),
        ],
        in_specs=[SMEM, rows_of(x, block)]
        + [anywhere] * len(parts_in)
        + [held_rows] * len(norm_vals),
        out_specs=[
            pl.BlockSpec((block, width), lambda i: (i, 0)),
            pl.BlockSpec((block, 3 * width), lambda i: (i, 0)),
            held_rows,
        ],
        scratch_shapes=[scratch_in, norm_scratch, sem_scratch],
        compiler_params=params(18),
        cost_estimate=cost(6 * length * width * width, 12 * width * width),
    )(table, x, *parts_in, *norm_vals)
    x = latents[0]

    group = 2
    marks = [pl.BlockSpec((length, LANES), lambda h: (0, 0))] * 2

    def heads_at(first):
        return pl.BlockSpec((length, dim * group), lambda h: (0, first // group + h))

    def sums_at(first):
        return pl.BlockSpec((group, 1, length), lambda h: (first // group + h, 0, 0))

    def attend(first, number, qkv):
        return pl.pallas_call(
            functools.partial(attend_kernel, group, dim, power),
            grid=(number // group,),
            in_specs=[heads_at(first + i * HEADS) for i in range(3)] + marks,
            out_specs=[heads_at(0), sums_at(0)],
            out_shape=[shape((length, number * dim), LOW), shape((number, 1, length), F32)],
            compiler_params=params(14),
            cost_estimate=cost(8 * length * length * number * dim, 8 * length * number * dim),
        )(qkv, qkv, qkv, mark_in, mark_out)

    ahead = HEADS // 2
    if ring:
        mid = grow(mid, after(taken, hidden_one))
        taken = swap_all(mid, seconds, count)
        early = swap_all(mid, [pair, pair], count)
        attended, log_sums = zip(*[attend(f, ahead, after(qkv, *mid)) for f in (0, ahead)])
        end_late = [swap(e, pair, count) for e in after(end, *attended)]
        parts_out = with_pairs(mid, after(taken, *attended), early) + end + end_late
    else:
        attended, log_sums = zip(*[attend(f, ahead, qkv) for f in (0, ahead)])

    row_block = pl.BlockSpec((block, width), lambda i: (i, 0))
    low_rows = shape((length, width), LOW)
    sides, parts = (2, 2) if ring else (1, 1)
    chunk_shape = (parts, count // sides if ring else 1)
    mat_blocks = width // LANES

    def chunks_of(blocks, extra=0):
        size = blocks // parts + extra
        return [shape((*chunk_shape, size, rows, LANES), LOW)] * sides

    dnorm_two, result, dmid, dattended, *out_grads = pl.pallas_call(
        functools.partial(
            middle_kernel, layout_out, rows, blocks_out, len(attended), sides, pair
        ),
        grid=steps,
        out_shape=[
            shape((2, width), F32),
            low_rows,
            shape((length, width), F32),
            low_rows,
            *chunks_of(3 * mat_blocks),
        ],
        in_specs=[SMEM, SMEM, row_block, row_block, rows_of(live, block), held_rows]
        + [rows_of(a, block) for a in attended]
        + [anywhere] * len(parts_out),
        out_specs=[two_rows] + [row_block] * 3 + [anywhere] * sides,
        scratch_shapes=[
            scratch_out,
            *[pltpu.VMEM((3, length, width), LOW)] * 2,
            pltpu.VMEM((3 * mat_blocks, width, LANES), LOW),
            sem_scratch,
        ],
        compiler_params=params(42),
        cost_estimate=cost(18 * length * width * width, 24 * width * width),
    )(table, places, x, dz, live, norm_vals, *attended, *parts_out)

    def attend_back(first, number, dattended, base, total, extra=0, prior=()):
        side = first // ahead
        inside = first - side * ahead
        blocks = 3 * group * dim // LANES
        outs = chunks_of(blocks * total, extra)
        return pl.pallas_call(
            functools.partial(
                attend_back_kernel, group, dim, power, scale, base, extra, len(prior), pair
            ),
            grid=(number // group,),
            in_specs=[SMEM]
            + [heads_at(first + i * HEADS) for i in range(3)]
            + [heads_at(first), heads_at(inside), *marks, sums_at(inside), whole(hidden_one)]
            + [anywhere] * len(prior),
            out_specs=[pl.BlockSpec((3, length, dim * group), lambda h: (0, 0, h))]
            + [anywhere] * sides,
            out_shape=[shape((3, length, number * dim), LOW), *outs],
            input_output_aliases={10 + n: 1 + n for n in range(len(prior))},
            scratch_shapes=[pltpu.VMEM((2 * blocks, width, LANES), LOW), sem_scratch],
            compiler_params=params(20),
            cost_estimate=cost(
                20 * length * length * number * dim + 6 * length * width * number * dim,
                16 * length * number * dim,
            ),
        )(
            places, qkv, qkv, qkv, dattended, attended[side], mark_in, mark_out,
            log_sums[side], hidden_one, *prior,
        )

    def last(dmid, grads, sides):
        packs = [shape((count // max(sides, 1), 1, rows, LANES), LOW)] * sides
        return pl.pallas_call(
            functools.partial(last_kernel, layout_in, rows, blocks_in, len(parts_in), sides),
            grid=steps,
            out_shape=[low_rows, shape((2, width), F32), *packs],
            in_specs=[SMEM, row_block, row_block, held_rows, two_rows]
            + [anywhere] * len(parts_in)
            + [rows_of(g, block) for g in grads],
            out_specs=[row_block, two_rows]
            + [pl.BlockSpec(p.shape, lambda i: (0, 0, 0, 0)) for p in packs],
            scratch_shapes=[scratch_in, norm_scratch, sem_scratch],
            compiler_params=params(18),
            cost_estimate=cost(6 * length * width * width, 6 * width * width),
        )(table, x, dmid, norm_vals, dnorm_two, *parts_in, *grads)

    state, norm_state = (matrices, moment1_mat, moment2_mat), (norm_params, moment1_norm, moment2_norm)
    if ring:
        pairs = range(1, inner)
        heads_w = group * dim

        def slots(firsts, number):
            return slots_of(
                [(j, n * heads_w, heads_w) for n in range(firsts, firsts + number) for j in range(3)], 2
            )

        def from_near(near):
            return [near[0]] + swap_all(near[1:], pairs, count)

        per = ahead // group
        keep, send = out_grads
        taken = swap(send, pair, count)
        found, *one = attend_back(0, group, after(dattended, keep), 0, per)
        grads = [found]

        sent = far_sums(keep, after(taken, found), [])
        far = [swap_all(sent, seconds, count)]
        found, keep_one, send_one = attend_back(
            group, group, after(dattended, *sent, found), 1, per, 0, one
        )
        grads.append(found)
        found, *two = attend_back(ahead, group, after(dattended, found, keep_one), 0, per, 1)
        grads.append(found)

        sent = far_sums(keep, taken, after(far, found))
        far.append(swap_all(sent, firsts, count))
        taken_one = swap(after(send_one, *sent), pair, count)
        found, keep_two, send_two = attend_back(
            ahead + group, group, after(dattended, *sent, found), 1, per, 1, two
        )
        grads.append(found)

        near = from_near(near_sums(keep, taken, [far[0], after(far[1], grads[-1])], inner))
        sent_one = far_sums(keep_one, after(taken_one, grads[-1]), [])
        far_one = [swap_all(sent_one, seconds, count)]
        grad_latents, dnorm_one, *packs = last(after(dmid, near[0], *sent_one), grads, 2)

        sent_one = far_sums(keep_one, taken_one, after(far_one, grad_latents, *near))
        far_one.append(swap_all(sent_one, firsts, count))
        taken_two, ends = swap_all(after((send_two, packs[1]), *sent_one), [pair, pair], count)
        ends = [packs[0], ends]

        far_one, taken_two, ends = after((far_one, taken_two, ends), far_one, taken_two, ends)
        near_one = near_sums(keep_one, taken_one, far_one, inner)
        sent_two = far_sums(keep_two, taken_two, [], ends)
        near_one, sent_two = after((near_one, sent_two), near_one, sent_two)
        near_one = from_near(near_one)
        far_two = [swap_all(sent_two, seconds, count)]
        sent_two = far_sums(keep_two, taken_two, after(far_two, *near_one), ends)
        far_two.append(swap_all(sent_two, firsts, count))
        near_two = near_sums(keep_two, taken_two, far_two, inner, ends)
        groups = [(range(inner), h, s) for h, s in enumerate(slots_of([(j, 0, width) for j in (3, 4, 5)], 2))]
        groups += [(range(inner, 2 * inner), h, s) for h, s in enumerate(slots(0, per))]
        prior = lamb_call(groups, after([*near, *near_one], near_two[0]), state)
        near_two = from_near(near_two)
        near_two = after(near_two, prior[4])
        groups = [(range(inner), h, s) for h, s in enumerate(slots(per, per))]
        norm_ends = (range(inner), 0)
        found = lamb_call(
            groups, near_two, state, norm_state, norm_ends, prior, (3, per * heads_w)
        )
        grad_mats, m1_mat, m2_mat, dir_mat, squares, grad_norms, m1_norm, m2_norm, dir_norm = found
        x_bit, y_bit = order_end
        rounds = ((pair,), (x_bit, y_bit, x_bit ^ y_bit), tuple(pairs))
        squares = rounds_sum(squares, rounds, count)[:2, :10]
    else:
        first, *one = attend_back(0, ahead, dattended, 0, HEADS // group)
        second, in_grads = attend_back(
            ahead, ahead, dattended, ahead // group, HEADS // group, 0, one
        )
        grads = [first, second]
        grad_latents, dnorm_one = last(dmid, grads, 0)
        norms_local = jnp.concatenate([dnorm_one, dnorm_two], 0)
        per = group * dim // LANES
        local = in_grads[0, 0].reshape(HEADS // group, 3, per, width, LANES)
        local = local.transpose(1, 0, 2, 3, 4).reshape(3 * mat_blocks, width, LANES)
        local = jnp.concatenate([local, out_grads[0][0, 0]], 0).astype(F32)
        local = local.reshape(6, mat_blocks, width, LANES)
        local = local.transpose(0, 2, 1, 3).reshape(6, width, width)
        grad_mats = lax.psum_scatter(local, AXES, scatter_dimension=1, tiled=True)
        grad_norms = lax.psum_scatter(norms_local, AXES, scatter_dimension=1, tiled=True)
        m1_mat, m2_mat, dir_mat = lamb_values(matrices, grad_mats, moment1_mat, moment2_mat)
        m1_norm, m2_norm, dir_norm = lamb_values(norm_params, grad_norms, moment1_norm, moment2_norm)
        squares = jnp.stack(
            [
                jnp.concatenate([jnp.sum(m * m, (1, 2)), jnp.sum(n * n, 1)])
                for m, n in ((matrices, norm_params), (dir_mat, dir_norm))
            ]
        )
        squares = lax.psum(squares, AXES)
    ratios = jnp.sqrt(squares[0]) / jnp.sqrt(squares[1])
    scaled_mats = ratios[:6][:, None, None] * dir_mat
    scaled_norms = ratios[6:][:, None] * dir_norm
    return (
        result[None],
        grad_latents[None],
        grad_mats,
        grad_norms,
        scaled_mats,
        scaled_norms,
        m1_mat,
        m2_mat,
        m1_norm,
        m2_norm,
        ratios,
    )


def solution(mesh):
    return jax.shard_map(
        on_device,
        mesh=mesh,
        in_specs=(
            P(("dp", "fsdp"), None, None),
            P(("dp", "fsdp"), None),
            P(("dp", "fsdp"), None, None),
            P(None, ("dp", "fsdp"), None),
            P(None, ("dp", "fsdp")),
            P(None, ("dp", "fsdp"), None),
            P(None, ("dp", "fsdp"), None),
            P(None, ("dp", "fsdp")),
            P(None, ("dp", "fsdp")),
        ),
        out_specs=(
            P(("dp", "fsdp"), None, None),
            P(("dp", "fsdp"), None, None),
            P(None, ("dp", "fsdp"), None),
            P(None, ("dp", "fsdp")),
            P(None, ("dp", "fsdp"), None),
            P(None, ("dp", "fsdp")),
            P(None, ("dp", "fsdp"), None),
            P(None, ("dp", "fsdp"), None),
            P(None, ("dp", "fsdp")),
            P(None, ("dp", "fsdp")),
            P(),
        ),
        check_vma=False,
    )
```
